32 devices in a mesh: dp: 8 (over z, y), seq: 4 (over x, core).
Axes of the slice: x: 2, y: 2, z: 4, core: 2. Of those that a mesh axis runs over, the one named last changes fastest.
Arguments:
- embeds: bfloat16 [8, 1024, 768], P('dp', 'seq'), may hold values from -6 to 6
- lengths: int32 [8], P('dp'), may hold values from 896 to 1024, as said below
- drop_in: int32 [2, 8, 1024, 768], P(None, 'dp', 'seq'), may hold values 0 or 1
- drop_ff: int32 [2, 8, 1024, 768], P(None, 'dp', 'seq'), may hold values 0 or 1
- positive: int32 [8], replicated, may hold values from 0 to 7, each once
- w_qkv: bfloat16 [768, 2304], replicated, may hold values from -0.21875 to 0.21875
- w_out: bfloat16 [768, 768], replicated, may hold values from -6 to 6
- w_up: bfloat16 [768, 3072], replicated, may hold values from -0.21875 to 0.21875
- w_down: bfloat16 [3072, 768], replicated, may hold values from -0.109375 to 0.109375
- pool_w: bfloat16 [768, 768], replicated, may hold values from -0.21875 to 0.21875
- gains: float32 [2, 768], replicated, may hold values from 0.1 to 1.9
- biases: float32 [6, 768], replicated, may hold values from -3 to 3
- up_bias: float32 [3072], replicated, may hold values from -3 to 3
- out_grad: bfloat16 [2, 8, 1024, 768], P(None, 'dp', 'seq'), may hold values from -6 to 6
Outputs:
- mixed: bfloat16 [2, 8, 1024, 768], P(None, 'dp', 'seq')
- embeds_grad: float32 [8, 1024, 768], P('dp', 'seq')
- grad_qkv: float32 [768, 2304], P('dp', 'seq')
- grad_out: float32 [768, 768], P('dp', 'seq')
- grad_up: float32 [768, 3072], P('dp', 'seq')
- grad_down: float32 [3072, 768], P('dp', 'seq')
- grad_pool: float32 [768, 768], P('dp', 'seq')
- grad_gains: float32 [2, 768], replicated
- grad_biases: float32 [5, 768], replicated
- grad_out_bias: float32 [768], replicated
- grad_up_bias: float32 [3072], replicated
- loss: float32 [], replicated
- alignment: float32 [], replicated
- uniformity: float32 [], replicated
The draws below stay inside these ranges and needn't reach their ends.
Inputs may be any that keep to these rules, and one draw needn't show every extreme that they name: `lengths`: in every draw some sentence has 1024 live tokens and some has 896. Each sentence is the positive of exactly one anchor.
All inputs are finite; a program needn't handle non-finite values. No bound on the sum of `drop_in` or of `drop_ff` on one device may be relied on, other than what follows from the above.
Results may differ from the reference program's by a relative error of at most 0.038.
Values may be sent and summed in bfloat16 or wider, within the bound.
No kernel may reach another device: no remote copies, remote signals or barrier semaphores. Data moves between devices by JAX's collectives and lax.ppermute only.
A program may use at most 192 MiB of HBM per device.

```python
import math
import jax
import jax.numpy as jnp
from jax import lax

D = 768
HEADS = 12
HEAD = 64
FF = 3072
L = 1024
NSENT = 8


def draw_embeds(key, part):
    common = jnp.clip(jax.random.normal(jax.random.fold_in(key, 11), (1, L, D), jnp.float32), -4.0, 4.0)
    own = jnp.clip(jax.random.normal(jax.random.fold_in(key, 12), (NSENT, L, D), jnp.float32), -4.0, 4.0)
    return (common + 0.5 * own).astype(jnp.bfloat16)


def draw_lengths(key, part):
    shortest = L - L // 8
    values = jax.random.randint(jax.random.fold_in(key, 21), (NSENT,), shortest, L + 1)
    picks = jax.random.permutation(jax.random.fold_in(key, 22), NSENT)
    values = values.at[picks[0]].set(L)
    values = values.at[picks[1]].set(shortest)
    return values.astype(jnp.int32)


def place_ends(entries, rng, smallest, largest):
    place = [jax.random.randint(jax.random.fold_in(rng, axis), (), 0, length) for axis, length in enumerate(entries.shape)]
    main_axis = entries.shape.index(max(entries.shape))
    beside = place[:main_axis] + [(place[main_axis] + 1) % entries.shape[main_axis]] + place[main_axis + 1:]
    return entries.at[tuple(place)].set(smallest).at[tuple(beside)].set(largest)


def steps_of(stream_key, dims, shards, smallest, high):
    def one(dim, parts):
        heights = jax.random.uniform(jax.random.fold_in(jax.random.fold_in(stream_key, 6), dim), (parts,), jnp.float32, smallest / len(shards), high / len(shards))
        return jnp.repeat(jnp.exp(heights), dims[dim] // parts).reshape((-1,) + (1,) * (len(dims) - dim - 1))

    factor_of = one(*shards[0])
    for cut in shards[1:]:
        factor_of = factor_of * one(*cut)
    return factor_of


def gaussian(own_key, shape, width, bound, split=(), held_as=jnp.bfloat16):
    level = steps_of(own_key, shape, split, -0.22, 0.18) if split else 1.0
    drawn = jax.random.normal(own_key, shape, jnp.float32) * width * level
    return jnp.minimum(jnp.maximum(drawn, -bound), bound).astype(held_as)


def setup_inputs(seed: int = 0) -> dict:
    seeds = jax.random.split(jax.random.key(seed), 15)
    return {
        "embeds": draw_embeds(jax.random.fold_in(seeds[14], 71), 0),
        "lengths": draw_lengths(jax.random.fold_in(seeds[14], 71), 0),
        "drop_in": place_ends((jax.random.randint(seeds[2], (2, NSENT, L, D), 0, 10) < 9).astype(jnp.int32), jax.random.fold_in(seeds[2], 1), 0, 1),
        "drop_ff": place_ends((jax.random.randint(seeds[3], (2, NSENT, L, D), 0, 10) < 9).astype(jnp.int32), jax.random.fold_in(seeds[3], 1), 0, 1),
        "positive": jax.random.permutation(seeds[4], NSENT).astype(jnp.int32),
        "w_qkv": gaussian(seeds[5], (D, 3 * D), D ** -0.5, 0.21875),
        "w_out": gaussian(seeds[6], (D, D), (max(1, D // L)) ** -0.5, 6.0),
        "w_up": gaussian(seeds[7], (D, FF), D ** -0.5, 0.21875),
        "w_down": gaussian(seeds[8], (FF, D), FF ** -0.5, 0.109375),
        "pool_w": gaussian(seeds[9], (D, D), D ** -0.5, 0.21875),
        "gains": jnp.clip(1.0 + 0.18 * jax.random.normal(seeds[10], (2, D), jnp.float32), 0.1, 1.9),
        "biases": gaussian(seeds[11], (6, D), 0.5, 3.0, (), jnp.float32),
        "up_bias": gaussian(seeds[12], (FF,), 0.5, 3.0, (), jnp.float32),
        "out_grad": gaussian(seeds[13], (2, NSENT, L, D), 1.0, 6.0, ((1, 8), (2, 4))),
    }


keep_rate = 0.9
highest = lax.Precision.HIGHEST

@jax.custom_vjp
def low(v):
    return lax.optimization_barrier(v.astype(jnp.bfloat16)).astype(jnp.float32)

@jax.custom_vjp
def low_back(v):
    return v

def low_keep(v):
    return (low(v), None)

def low_pass(kept, grad):
    return (grad,)

def back_keep(v):
    return (v, None)

def back_low(kept, grad):
    return (low(grad),)
low.defvjp(low_keep, low_pass)
low_back.defvjp(back_keep, back_low)

def layer_norm(values, gain, shift):
    mean = lax.optimization_barrier(jnp.mean(values, axis=-1, keepdims=True))
    centred = values - mean
    spread = lax.optimization_barrier(jnp.mean(centred * centred, axis=-1, keepdims=True))
    return centred * lax.rsqrt(spread + 1e-06) * gain + shift

def gelu_exact(values):
    return jax.nn.gelu(values, approximate=False)

def contrast(pooled_all, positive):
    squares = lax.optimization_barrier(jnp.sum(pooled_all * pooled_all, axis=-1, keepdims=True))
    unit = pooled_all * lax.rsqrt(squares + 1e-06)
    anchors = unit[0]
    candidates = unit[1]
    count = anchors.shape[0]
    logits = jnp.dot(anchors, candidates.T, precision=highest) / 0.05
    picked = (lax.broadcasted_iota(jnp.int32, (count, count), 1) == positive[:, None]).astype(jnp.float32)
    top = lax.optimization_barrier(jnp.max(logits, axis=1, keepdims=True))
    log_total = jnp.log(lax.optimization_barrier(jnp.sum(jnp.exp(logits - top), axis=1))) + top[:, 0]
    target = lax.optimization_barrier(jnp.sum(logits * picked, axis=1))
    loss = jnp.mean(log_total - target)
    matched = jnp.dot(picked, candidates, precision=highest)
    offset = anchors - matched
    alignment = jnp.mean(lax.optimization_barrier(jnp.sum(offset * offset, axis=-1)))
    norms = lax.optimization_barrier(jnp.sum(anchors * anchors, axis=-1))
    inner = jnp.dot(anchors, anchors.T, precision=highest)
    dist = norms[:, None] + norms[None, :] - 2.0 * inner
    apart = (lax.broadcasted_iota(jnp.int32, (count, count), 0) != lax.broadcasted_iota(jnp.int32, (count, count), 1)).astype(jnp.float32)
    uniformity = jnp.log(jnp.sum(jnp.exp(-2.0 * dist) * apart) / (count * (count - 1)))
    return (loss, (alignment, uniformity))

def sentence_layer(params, sentence, mask_in, mask_ff, length):
    w_qkv, w_out, w_up, w_down, gains, biases, up_bias = params
    inv_keep = 1.0 / keep_rate
    xin = sentence[None] * mask_in * inv_keep
    xin_low = low(xin)
    qkv = jnp.einsum('vtd,de->vte', xin_low, w_qkv, precision=highest)
    query = low_back(low(qkv[..., :D] + biases[0]))
    key = low_back(low(qkv[..., D:2 * D]))
    value = low_back(low(qkv[..., 2 * D:] + biases[1]))
    q_heads = query.reshape(2, L, HEADS, HEAD)
    k_heads = key.reshape(2, L, HEADS, HEAD)
    v_heads = value.reshape(2, L, HEADS, HEAD)
    raw = jnp.einsum('vthe,vshe->vhts', q_heads, k_heads, precision=highest) / math.sqrt(HEAD)
    live = jnp.arange(L, dtype=jnp.int32) < length
    scores = low_back(jnp.where(live[None, None, None, :], raw, -1e+30))
    top = lax.optimization_barrier(jnp.max(scores, axis=-1, keepdims=True))
    expo = jnp.exp(scores - top)
    probs = expo / lax.optimization_barrier(jnp.sum(expo, axis=-1, keepdims=True))
    context = jnp.einsum('vhts,vshe->vthe', low(probs), v_heads, precision=highest).reshape(2, L, D)
    context = low_back(low(context))
    attn = low_back(jnp.einsum('vtd,de->vte', context, w_out, precision=highest) + biases[2])
    h1 = layer_norm(xin + attn, gains[0], biases[3])
    up = low_back(jnp.einsum('vtd,df->vtf', low(h1), w_up, precision=highest) + up_bias)
    hidden = low(gelu_exact(up))
    ff = low_back(jnp.einsum('vtf,fd->vtd', hidden, w_down, precision=highest) + biases[4])
    return layer_norm(h1 + ff * mask_ff * inv_keep, gains[1], biases[5])

def reference(embeds, lengths, drop_in, drop_ff, positive, w_qkv, w_out, w_up, w_down, pool_w, gains, biases, up_bias, out_grad):
    keep_in = jnp.swapaxes(drop_in.astype(jnp.float32), 0, 1)
    keep_ff = jnp.swapaxes(drop_ff.astype(jnp.float32), 0, 1)

    def forward(embeds32, w_qkv32, w_out32, w_up32, w_down32, pool_w32, gains32, biases32, up_bias32):
        params = (w_qkv32, w_out32, w_up32, w_down32, gains32, biases32, up_bias32)

        def one_sentence(item):
            sentence, mask_in, mask_ff, length = item
            return sentence_layer(params, sentence, mask_in, mask_ff, length)
        outputs = lax.map(jax.checkpoint(one_sentence), (embeds32, keep_in, keep_ff, lengths))
        cls = low(outputs[:, :, 0, :])
        pre = low_back(jnp.einsum('svd,de->sve', cls, pool_w32, precision=highest))
        pooled = jnp.swapaxes(jnp.tanh(pre), 0, 1)
        loss, extras = contrast(pooled, positive)
        return ((jnp.swapaxes(outputs, 0, 1), loss), extras)
    floats = (embeds.astype(jnp.float32), w_qkv.astype(jnp.float32), w_out.astype(jnp.float32), w_up.astype(jnp.float32), w_down.astype(jnp.float32), pool_w.astype(jnp.float32), gains.astype(jnp.float32), biases.astype(jnp.float32), up_bias.astype(jnp.float32))
    primal, backward, extras = jax.vjp(forward, *floats, has_aux=True)
    layer_out, loss = primal
    grads = backward((out_grad.astype(jnp.float32), jnp.ones((), jnp.float32)))
    alignment, uniformity = extras
    bias_grads = grads[7]
    grad_biases = jnp.concatenate([bias_grads[0:2], bias_grads[3:6]], axis=0)
    grad_out_bias = bias_grads[2]
    return (layer_out.astype(jnp.bfloat16), grads[0], grads[1], grads[2], grads[3], grads[4], grads[5], grads[6], grad_biases, grad_out_bias, grads[8], loss, alignment, uniformity)
```

```python
import functools
import math

import jax
import jax.numpy as jnp
from jax import lax
from jax.experimental import pallas as pl
from jax.experimental.pallas import tpu as pltpu
from jax.sharding import PartitionSpec as P

HEAD = 64
keep_rate = 0.9
highest = lax.Precision.HIGHEST
f32 = jnp.float32
bf16 = jnp.bfloat16

CROSS = [(i, i ^ 2) for i in range(4)]
PAIR = [(i, i ^ 1) for i in range(4)]


def dot(a, b):
    return jnp.dot(a, b, preferred_element_type=f32)


def dot_t(a, b):
    return lax.dot_general(a, b, (((1,), (1,)), ((), ())), preferred_element_type=f32)


def t_dot(a, b):
    return lax.dot_general(a, b, (((0,), (0,)), ((), ())), preferred_element_type=f32)


def one_head(block, head, extra):
    lane = lax.broadcasted_iota(jnp.int32, block.shape, 1)
    mine = (lane >= HEAD) if head else (lane < HEAD)
    out = jnp.where(mine, block, jnp.zeros_like(block))
    if extra is not None:
        out = jnp.where(lane == (0 if head else HEAD), extra, out)
    return out


def forward_kernel(chunk, q_ref, k_ref, v_ref, mask_ref, o_ref, lse_ref):
    n = q_ref.shape[0]
    keys = [one_head(k_ref[...], h, mask_ref[...]) for h in (0, 1)]
    value_t = v_ref[...].T
    one = jnp.ones((), bf16)
    for c in range(n // chunk):
        at = slice(c * chunk, (c + 1) * chunk)
        q = q_ref[at, :] * jnp.asarray(1.0 / math.sqrt(HEAD), bf16)
        outs = []
        for h in (0, 1):
            s = dot_t(keys[h], one_head(q, h, one))
            top = jnp.max(s, axis=0, keepdims=True)
            p = jnp.exp(s - top)
            total = jnp.sum(p, axis=0, keepdims=True)
            out = dot(value_t[HEAD * h : HEAD * (h + 1), :], p.astype(bf16))
            outs.append(out * (1.0 / total))
            lse_ref[0, h : h + 1, at] = top + jnp.log(total)
        o_ref[at, :] = jnp.concatenate(outs, axis=0).T.astype(bf16)


def backward_kernel(
    chunk, q_ref, k_ref, v_ref, o_ref, do_ref, lse_ref, mask_ref, dq_ref, dk_ref, dv_ref, dk_acc, dv_acc
):
    n = q_ref.shape[0]
    scale = 1.0 / math.sqrt(HEAD)
    keys = [one_head(k_ref[...], h, mask_ref[...]) for h in (0, 1)]
    key_t = k_ref[...].T
    value = v_ref[...]
    one = jnp.ones((), bf16)
    for c in range(n // chunk):
        at = slice(c * chunk, (c + 1) * chunk)
        q = q_ref[at, :] * jnp.asarray(scale, bf16)
        do = do_ref[at, :]
        prod_t = (do.astype(f32) * o_ref[at, :].astype(f32)).T
        ps, dss, dos, qs, dq_t = [], [], [], [], []
        for h in (0, 1):
            rows = slice(HEAD * h, HEAD * (h + 1))
            s = dot_t(keys[h], one_head(q, h, one))
            p = jnp.exp(s - lse_ref[0, h : h + 1, at])
            do_h = one_head(do, h, None)
            dp = dot_t(value, do_h)
            delta = jnp.sum(prod_t[rows, :], axis=0, keepdims=True)
            ds = (p * (dp - delta)).astype(bf16)
            ps.append(p.astype(bf16))
            dss.append(ds)
            dos.append(do_h)
            qs.append(one_head(q, h, None))
            dq_t.append(dot(key_t[rows, :], ds))
        dv_c = dot(jnp.concatenate(ps, 1), jnp.concatenate(dos, 0))
        dk_c = dot(jnp.concatenate(dss, 1), jnp.concatenate(qs, 0))
        if c == 0:
            dv_acc[...] = dv_c
            dk_acc[...] = dk_c
        else:
            dv_acc[...] += dv_c
            dk_acc[...] += dk_c
        dq_ref[at, :] = (jnp.concatenate(dq_t, 0).T * scale).astype(bf16)
    dk_ref[...] = dk_acc[...].astype(bf16)
    dv_ref[...] = dv_acc[...].astype(bf16)


def attend_forward(qkv, mask, chunk=512):
    n, pairs = qkv.shape[0], qkv.shape[1] // 384

    def block(offset):
        return pl.BlockSpec((n, 128), lambda i: (0, i + offset))

    return pl.pallas_call(
        functools.partial(forward_kernel, chunk),
        grid=(pairs,),
        in_specs=[block(0), block(pairs), block(2 * pairs), pl.BlockSpec((n, 128), lambda i: (0, 0))],
        out_specs=[block(0), pl.BlockSpec((1, 2, n), lambda i: (i, 0, 0))],
        out_shape=[
            jax.ShapeDtypeStruct((n, pairs * 128), bf16),
            jax.ShapeDtypeStruct((pairs, 2, n), f32),
        ],
        compiler_params=pltpu.CompilerParams(vmem_limit_bytes=48 << 20),
        cost_estimate=pl.CostEstimate(flops=4 * n * n * pairs * 128, bytes_accessed=8 * n * 384, transcendentals=2 * pairs * n * n),
        name="attend_forward",
    )(qkv, qkv, qkv, mask)


def attend_backward(qkv, context, g_context, lse, mask, chunk=512):
    n, pairs = qkv.shape[0], qkv.shape[1] // 384

    def block(offset):
        return pl.BlockSpec((n, 128), lambda i: (0, i + offset))

    return pl.pallas_call(
        functools.partial(backward_kernel, chunk),
        grid=(pairs,),
        in_specs=[
            block(0),
            block(pairs),
            block(2 * pairs),
            block(0),
            block(0),
            pl.BlockSpec((1, 2, n), lambda i: (i, 0, 0)),
            pl.BlockSpec((n, 128), lambda i: (0, 0)),
        ],
        out_specs=[block(0)] * 3,
        out_shape=[jax.ShapeDtypeStruct((n, pairs * 128), bf16)] * 3,
        scratch_shapes=[pltpu.VMEM((n, 128), f32)] * 2,
        compiler_params=pltpu.CompilerParams(vmem_limit_bytes=48 << 20),
        cost_estimate=pl.CostEstimate(flops=10 * n * n * pairs * 128, bytes_accessed=16 * n * 384, transcendentals=2 * pairs * n * n),
        name="attend_backward",
    )(qkv, qkv, qkv, context, g_context, lse, mask)


def contrast(pooled_all, positive):
    squares = jnp.sum(pooled_all * pooled_all, axis=-1, keepdims=True)
    unit = pooled_all * lax.rsqrt(squares + 1e-06)
    anchors = unit[0]
    candidates = unit[1]
    count = anchors.shape[0]
    logits = jnp.dot(anchors, candidates.T, precision=highest) / 0.05
    picked = (lax.broadcasted_iota(jnp.int32, (count, count), 1) == positive[:, None]).astype(f32)
    top = jnp.max(logits, axis=1, keepdims=True)
    log_total = jnp.log(jnp.sum(jnp.exp(logits - top), axis=1)) + top[:, 0]
    target = jnp.sum(logits * picked, axis=1)
    loss = jnp.mean(log_total - target)
    matched = jnp.dot(picked, candidates, precision=highest)
    offset = anchors - matched
    alignment = jnp.mean(jnp.sum(offset * offset, axis=-1))
    norms = jnp.sum(anchors * anchors, axis=-1)
    inner = jnp.dot(anchors, anchors.T, precision=highest)
    dist = norms[:, None] + norms[None, :] - 2.0 * inner
    apart = (
        lax.broadcasted_iota(jnp.int32, (count, count), 0)
        != lax.broadcasted_iota(jnp.int32, (count, count), 1)
    ).astype(f32)
    uniformity = jnp.log(jnp.sum(jnp.exp(-2.0 * dist) * apart) / (count * (count - 1)))
    return (loss, (alignment, uniformity))


def norm_parts(values):
    mean = jnp.mean(values, axis=-1, keepdims=True)
    centred = values - mean
    inv = lax.rsqrt(jnp.mean(centred * centred, axis=-1, keepdims=True) + 1e-06)
    return centred * inv, inv


def norm_back(g, normal, inv, gain):
    a = g * gain
    return (a - jnp.mean(a, axis=-1, keepdims=True) - normal * jnp.mean(a * normal, axis=-1, keepdims=True)) * inv


def pick(values, index, axis):
    return lax.dynamic_index_in_dim(values, index, axis, keepdims=False)


def halve(values, axis, bit, name, perm):
    arrived = lax.ppermute(pick(values, 1 - bit, axis), name, perm)
    return (pick(values, bit, axis).astype(f32) + arrived.astype(f32)).astype(bf16)


def reduce_blocks(values, side, dp, bits, order):
    shape = values.shape[2:]
    values = values.reshape((2,) * (bits + 1) + shape)
    names = ["side"] + list(range(bits - 1, -1, -1))
    for step in order:
        axis = names.index(step)
        if step == "side":
            values = halve(values, axis, side, "seq", CROSS)
        else:
            perm = [(d, d ^ (1 << step)) for d in range(1 << bits)]
            values = halve(values, axis, (dp >> step) & 1, "dp", perm)
        names.pop(axis)
    return values


def gather_dp(values, dp, bits):
    values = values[None]
    for step in range(bits):
        perm = [(d, d ^ (1 << step)) for d in range(1 << bits)]
        arrived = lax.ppermute(values, "dp", perm)
        high = ((dp >> step) & 1) == 1
        low_part = jnp.where(high, arrived, values)
        high_part = jnp.where(high, values, arrived)
        values = jnp.concatenate([low_part, high_part], axis=0)
    return values


def sum_all(values, bits):
    for perm in (PAIR, CROSS):
        values = values + lax.ppermute(values, "seq", perm)
    for step in range(bits):
        values = values + lax.ppermute(values, "dp", [(d, d ^ (1 << step)) for d in range(1 << bits)])
    return values


def own_heads(values, half, axis):
    size = values.shape[axis] // 4
    shape = values.shape[:axis] + (2, 2, size) + values.shape[axis + 1 :]
    out = pick(values.reshape(shape), half, axis + 1)
    return out.reshape(values.shape[:axis] + (2 * size,) + values.shape[axis + 1 :])


def after(value, *others):
    return lax.optimization_barrier((value,) + others)[0]


def body(
    embeds,
    lengths,
    drop_in,
    drop_ff,
    positive,
    w_qkv,
    w_out,
    w_up,
    w_down,
    pool_w,
    gains,
    biases,
    up_bias,
    out_grad,
):
    views, _, length, width = drop_in.shape
    n_dp = lax.axis_size("dp")
    bits = n_dp.bit_length() - 1
    seq = lax.axis_index("seq")
    dp = lax.axis_index("dp")
    side, half = seq // 2, seq % 2
    inv_keep = 1.0 / keep_rate
    rows = 2 * length

    token = embeds[0]
    kept_own = token * pick(drop_in, side, 0)[0].astype(bf16)
    kept_cross = lax.ppermute(token * pick(drop_in, 1 - side, 0)[0].astype(bf16), "seq", CROSS)
    kept_mine = jnp.concatenate([kept_own, kept_cross], axis=0)
    kept_pair = jnp.concatenate(
        [lax.ppermute(kept_own, "seq", PAIR), lax.ppermute(kept_cross, "seq", PAIR)], axis=0
    )
    mask_ff_own = pick(drop_ff, side, 0)[0].astype(bf16)
    mask_ff_send = after(pick(drop_ff, 1 - side, 0)[0].astype(bf16), kept_cross)
    mask_ff_cross = lax.ppermute(mask_ff_send, "seq", CROSS)
    g_out_send = after(pick(out_grad, 1 - side, 0)[0], mask_ff_cross)
    g_out_cross = lax.ppermute(g_out_send, "seq", CROSS)
    keep_ff = jnp.concatenate([mask_ff_own, mask_ff_cross], axis=0).astype(f32) * inv_keep
    g_out_rows = jnp.concatenate([pick(out_grad, side, 0)[0], g_out_cross], axis=0)

    xin = kept_mine.astype(f32) * inv_keep
    x_low = (jnp.concatenate([kept_mine, kept_pair], axis=0).astype(f32) * inv_keep).astype(bf16)
    blocks = jnp.stack([seq, seq ^ 2, seq ^ 1, seq ^ 3])
    position = (blocks[:, None] * length + jnp.arange(length, dtype=jnp.int32)[None]).reshape(-1)
    mask = jnp.where(position < lengths[0], 0.0, -1e30).astype(bf16)
    mask = jnp.broadcast_to(mask[:, None], (2 * rows, 128))

    w_own = own_heads(w_qkv.reshape(width, 3, width), half, 2).reshape(width, -1)
    bias3 = jnp.stack([biases[0], jnp.zeros_like(biases[0]), biases[1]])
    b_own = own_heads(bias3, half, 1).reshape(-1)
    qkv = (dot(x_low, w_own) + b_own).astype(bf16)
    context, lse = attend_forward(qkv, mask)
    ctx_cross = lax.ppermute(context[rows:], "seq", PAIR)
    w_out_own = own_heads(w_out, half, 0)
    w_out_pair = own_heads(w_out, 1 - half, 0)
    attn = dot(context[:rows], w_out_own) + dot(ctx_cross, w_out_pair) + biases[2]
    normal1, inv1 = norm_parts(xin + attn)
    h1 = normal1 * gains[0] + biases[3]
    h1_low = h1.astype(bf16)
    up = dot(h1_low, w_up) + up_bias
    density = jnp.exp(-0.5 * up * up) * (1.0 / math.sqrt(2.0 * math.pi))
    phi = 0.5 * (1.0 + lax.erf(up * (1.0 / math.sqrt(2.0))))
    hidden = (up * phi).astype(bf16)
    slope = (phi + up * density).astype(bf16)
    ff = dot(hidden, w_down) + biases[4]
    normal2, inv2 = norm_parts(h1 + ff * keep_ff)
    mixed = (normal2 * gains[1] + biases[5]).astype(bf16)
    mixed_cross = lax.ppermute(mixed[length:], "seq", CROSS)
    mixed_out = jnp.where(
        side == 0,
        jnp.stack([mixed[:length], mixed_cross]),
        jnp.stack([mixed_cross, mixed[:length]]),
    )[:, None]

    first = jnp.where(side == 0, mixed[0], mixed[length])
    first_pair = lax.ppermute(first, "seq", [(0, 1), (2, 3)])
    first = jnp.where(half == 0, first, first_pair)
    first_cross = lax.ppermute(first, "seq", CROSS)
    both = jnp.where(side == 0, jnp.stack([first, first_cross]), jnp.stack([first_cross, first]))
    cls_all = gather_dp(both, dp, bits).swapaxes(0, 1)
    pooled = jnp.tanh(
        jnp.einsum("vpd,de->vpe", cls_all, pool_w, preferred_element_type=f32)
    )
    loss, contrast_back, extras = jax.vjp(
        functools.partial(contrast, positive=positive), pooled, has_aux=True
    )
    alignment, uniformity = extras
    g_pooled = contrast_back(jnp.ones((), f32))[0]
    g_pre = (g_pooled * (1.0 - pooled * pooled)).astype(bf16)
    n_cls = views * n_dp
    pool_rows, pool_cols = width // n_dp, width // 4
    grad_pool = t_dot(
        lax.dynamic_slice_in_dim(cls_all.reshape(n_cls, width), dp * pool_rows, pool_rows, 1),
        lax.dynamic_slice_in_dim(g_pre.reshape(n_cls, width), seq * pool_cols, pool_cols, 1),
    )
    g_pre_mine = pick(pick(g_pre, side, 0), dp, 0)
    g_cls = dot_t(g_pre_mine[None], pool_w)
    place = jnp.where(side == 0, 0, length)
    is_first = (jnp.arange(rows, dtype=jnp.int32) == place) & (half == 0)
    g_out = g_out_rows.astype(f32) + jnp.where(is_first[:, None], g_cls, 0.0)

    g_shift2 = jnp.sum(g_out, axis=0)
    g_gain2 = jnp.sum(g_out * normal2, axis=0)
    g_h2 = norm_back(g_out, normal2, inv2, gains[1])
    g_ff = (g_h2 * keep_ff).astype(bf16)
    g_down_bias = jnp.sum(g_ff.astype(f32), axis=0)
    g_up = (dot_t(g_ff, w_down) * slope.astype(f32)).astype(bf16)
    g_up_bias = jnp.sum(g_up.astype(f32), axis=0)
    g_h1 = g_h2 + dot_t(g_up, w_up)
    g_shift1 = jnp.sum(g_h1, axis=0)
    g_gain1 = jnp.sum(g_h1 * normal1, axis=0)
    g_h1pre = norm_back(g_h1, normal1, inv1, gains[0])
    g_attn = g_h1pre.astype(bf16)
    g_out_bias = jnp.sum(g_attn.astype(f32), axis=0)

    g_ctx_pair = lax.ppermute(dot_t(g_attn, w_out_pair).astype(bf16), "seq", PAIR)
    g_context = jnp.concatenate([dot_t(g_attn, w_out_own).astype(bf16), g_ctx_pair], axis=0)

    def pair_sum(make):
        arrived = lax.ppermute(make(1 - half).astype(bf16), "seq", PAIR)
        return (make(half) + arrived.astype(f32)).astype(bf16)

    def up_part(who):
        part = t_dot(h1_low, own_heads(g_up, who, 1))
        return part.reshape(n_dp, width // n_dp, 2, -1).transpose(2, 0, 1, 3)

    def down_part(who):
        part = t_dot(own_heads(g_ff, who, 1), hidden)
        return part.reshape(2, width // 4, n_dp, -1).transpose(0, 2, 1, 3)

    def out_part(who):
        ctx = jnp.concatenate([context[:rows], ctx_cross], axis=1)
        part = t_dot(ctx, own_heads(g_attn, who, 1))
        part = part.reshape(2, 2, width // 4, 2, width // 4)
        part = jnp.where(half == 0, part, part[::-1])
        part = part.transpose(3, 1, 0, 2, 4)
        return part.reshape(2, n_dp, width // n_dp, width // 4)

    low = list(range(1, bits))
    side_first = ["side", 0] + low
    dp_first = [0, "side"] + low
    sum_up = reduce_blocks(pair_sum(up_part), side, dp, bits, side_first)
    sum_down = reduce_blocks(pair_sum(down_part), side, dp, bits, dp_first)
    sum_out = reduce_blocks(pair_sum(out_part), side, dp, bits, dp_first)
    grad_up = sum_up.astype(f32)
    grad_down = sum_down.astype(f32).T
    grad_out = sum_out.astype(f32)

    g_query, g_key, g_value = attend_backward(qkv, context, g_context, lse, mask)
    g_qkv = jnp.concatenate([g_query, g_key, g_value], axis=1)
    part = t_dot(x_low, g_qkv).astype(bf16)
    part = part.reshape(n_dp, width // n_dp, 2, -1).transpose(2, 0, 1, 3)
    cut = width // n_dp // 2
    sum_qkv = jnp.concatenate(
        [
            reduce_blocks(part[:, :, :cut], side, dp, bits, side_first),
            reduce_blocks(part[:, :, cut:], side, dp, bits, dp_first),
        ],
        axis=0,
    )
    three = sum_qkv.reshape(width // n_dp, 3, width // 4)
    swapped = lax.ppermute(jnp.where(half == 0, three[:, 2], three[:, 0]), "seq", PAIR)
    left = jnp.where(half == 0, three[:, 0], three[:, 1])
    right = jnp.where(half == 0, three[:, 1], three[:, 2])
    grad_qkv = jnp.concatenate([left, swapped, right], axis=1).astype(f32)

    g_x_pair = lax.ppermute(dot_t(g_qkv[rows:], w_own).astype(bf16), "seq", PAIR)
    g_x = dot_t(g_qkv[:rows], w_own) + g_h1pre + g_x_pair.astype(f32)
    g_x_cross = lax.ppermute(g_x[length:].astype(bf16), "seq", CROSS)
    embeds_grad = (
        g_x[:length] * pick(drop_in, side, 0)[0].astype(f32)
        + g_x_cross.astype(f32) * pick(drop_in, 1 - side, 0)[0].astype(f32)
    ) * inv_keep

    early = sum_all(
        jnp.concatenate([g_gain1, g_gain2, g_shift1, g_down_bias, g_shift2, g_out_bias, g_up_bias]),
        bits,
    )
    q_bias = jnp.sum(g_query.astype(f32), axis=0).reshape(2, -1)
    v_bias = jnp.sum(g_value.astype(f32), axis=0).reshape(2, -1)
    mine = jnp.stack([q_bias, v_bias])[:, :, None]
    where_half = (jnp.arange(2) == half)[None, None, :, None]
    late = sum_all(jnp.where(where_half, mine, 0.0).reshape(2, width), bits)
    part = early[: 6 * width].reshape(6, width)
    grad_gains = part[:2]
    grad_biases = jnp.concatenate([late, part[2:5]], axis=0)
    return (
        mixed_out,
        embeds_grad[None],
        grad_qkv,
        grad_out,
        grad_up,
        grad_down,
        grad_pool,
        grad_gains,
        grad_biases,
        part[5],
        early[6 * width :],
        loss,
        alignment,
        uniformity,
    )


def solution(mesh):
    tokens = P(None, "dp", "seq", None)
    placed = (P("dp", "seq", None), P("dp"), tokens, tokens) + (P(),) * 9 + (tokens,)
    weight = P("dp", "seq")
    return jax.shard_map(
        body,
        mesh=mesh,
        in_specs=placed,
        out_specs=(tokens, P("dp", "seq", None)) + (weight,) * 5 + (P(),) * 7,
        check_vma=False,
    )
```

```python
import functools
import math

import jax
import jax.numpy as jnp
from jax import lax
from jax.experimental import pallas as pl
from jax.experimental.pallas import tpu as pltpu
from jax.sharding import PartitionSpec as P

HEAD = 64
keep_rate = 0.9
inv_keep = 1.0 / keep_rate
highest = lax.Precision.HIGHEST
f32 = jnp.float32
bf16 = jnp.bfloat16

CROSS = [(i, i ^ 2) for i in range(4)]
PAIR = [(i, i ^ 1) for i in range(4)]
GROUPS = 8


def cost(time):
    return pl.CostEstimate(flops=time * 2_000_000_000, bytes_accessed=1 << 20, transcendentals=0)

CHUNK = 768


def dot(a, b):
    return jnp.dot(a, b, preferred_element_type=f32)


def dot_t(a, b):
    return lax.dot_general(a, b, (((1,), (1,)), ((), ())), preferred_element_type=f32)


def t_dot(a, b):
    return lax.dot_general(a, b, (((0,), (0,)), ((), ())), preferred_element_type=f32)


def whole(shape):
    return pl.BlockSpec(shape, lambda *_: (0,) * len(shape))


def struct(shape, dtype):
    return jax.ShapeDtypeStruct(shape, dtype)


def hbm(x):
    return pltpu.with_memory_space_constraint(x, pltpu.HBM)


def params(limit):
    return pltpu.CompilerParams(vmem_limit_bytes=limit << 20)


ALL = (slice(None),)


class Stream:
    def __init__(self, refs, buffers, sems, out):
        self.refs, self.buffers, self.sems, self.out = refs, buffers, sems, out
        self.count, self.copies = 0, {}

    def start(self, which, key=0, at=ALL):
        ref, buffer = self.refs[which].at[at], self.buffers[which].at[at]
        source, target = (buffer, ref) if self.out else (ref, buffer)
        copy = pltpu.make_async_copy(source, target, self.sems.at[self.count])
        copy.start()
        self.count += 1
        self.copies[which, key] = copy

    def wait(self, which, key=0):
        copy = self.copies.pop((which, key), None)
        if copy is not None:
            copy.wait()
        return self.buffers[which]

    def drain(self):
        for which, key in list(self.copies):
            self.wait(which, key)


def streamed(body, scalars, ins, outs, scratch, copies, name, time, limit=56):
    n_s, n_i, n_o = len(scalars), len(ins), len(outs)

    def kernel(*refs):
        cuts = [n_s, n_i, n_o, n_i, n_o, len(scratch), 1, 1]
        parts, at = [], 0
        for cut in cuts:
            parts.append(refs[at : at + cut])
            at += cut
        reads = Stream(parts[1], parts[3], parts[6][0], False)
        writes = Stream(parts[2], parts[4], parts[7][0], True)
        body([r[0] if r.shape[0] == 1 else r for r in parts[0]], reads, writes, *parts[5])
        reads.drain()
        writes.drain()

    smem, far = pl.BlockSpec(memory_space=pltpu.SMEM), pl.BlockSpec(memory_space=pltpu.HBM)
    return pl.pallas_call(
        kernel,
        in_specs=[smem] * n_s + [far] * n_i,
        out_specs=[far] * n_o,
        out_shape=[pltpu.HBM(o.shape, o.dtype) for o in outs],
        scratch_shapes=[pltpu.VMEM(x.shape, x.dtype) for x in list(ins) + list(outs)]
        + list(scratch)
        + [pltpu.SemaphoreType.DMA((copies[0],)), pltpu.SemaphoreType.DMA((copies[1],))],
        compiler_params=params(limit),
        cost_estimate=cost(time),
        name=name,
    )(*scalars, *[hbm(x) for x in ins])


def one_head(block, head, extra):
    lane = lax.broadcasted_iota(jnp.int32, block.shape, 1)
    mine = (lane >= HEAD) if head else (lane < HEAD)
    out = jnp.where(mine, block, jnp.zeros_like(block))
    if extra is not None:
        out = jnp.where(lane == (0 if head else HEAD), extra, out)
    return out


def key_mask(place_ref, rows):
    quarter = rows // 4
    parts = []
    for b in range(4):
        at = lax.broadcasted_iota(jnp.int32, (quarter, 128), 0) + (place_ref[0] ^ b) * quarter
        parts.append(jnp.where(at < place_ref[1], 0.0, -1e30).astype(bf16))
    return jnp.concatenate(parts, axis=0)


def forward_kernel(place_ref, ql_ref, qc_ref, kl_ref, kc_ref, vl_ref, vc_ref, own_ref, send_ref, lse_ref):
    key = jnp.concatenate([kl_ref[...], kc_ref[...]], axis=0)
    mask = key_mask(place_ref, key.shape[0])
    keys = [one_head(key, h, mask) for h in (0, 1)]
    value_t = jnp.concatenate([vl_ref[...], vc_ref[...]], axis=0).T
    one = jnp.ones((), bf16)
    rows = ql_ref.shape[0]
    for part, q_ref in enumerate((ql_ref, qc_ref)):
        q = q_ref[...] * jnp.asarray(1.0 / math.sqrt(HEAD), bf16)
        outs = []
        for h in (0, 1):
            s = dot_t(keys[h], one_head(q, h, one))
            top = jnp.max(s, axis=0, keepdims=True)
            p = jnp.exp(s - top)
            total = jnp.sum(p, axis=0, keepdims=True)
            out = dot(value_t[HEAD * h : HEAD * (h + 1), :], p.astype(bf16))
            outs.append(out * (1.0 / total))
            lse_ref[0, h : h + 1, part * rows : (part + 1) * rows] = top + jnp.log(total)
        out = jnp.concatenate(outs, axis=0).T.astype(bf16)
        at = slice(part * rows // 2, (part + 1) * rows // 2)
        own_ref[at, :] = out[: rows // 2]
        send_ref[at, :] = out[rows // 2 :]


def attend_forward(place, qkv_local, qkv_cross):
    rows, pairs = qkv_local.shape[0], qkv_local.shape[1] // 384

    def block(offset):
        return [pl.BlockSpec((rows, 128), lambda i: (0, i + offset))] * 2

    return pl.pallas_call(
        forward_kernel,
        grid=(pairs,),
        in_specs=[pl.BlockSpec(memory_space=pltpu.SMEM)] + block(0) + block(pairs) + block(2 * pairs),
        out_specs=block(0) + [pl.BlockSpec((1, 2, 2 * rows), lambda i: (i, 0, 0))],
        out_shape=[
            pltpu.HBM((rows, pairs * 128), bf16),
            pltpu.HBM((rows, pairs * 128), bf16),
            pltpu.HBM((pairs, 2, 2 * rows), f32),
        ],
        compiler_params=params(56),
        cost_estimate=cost(13),
        name="attend_forward",
    )(place, *(hbm(qkv_local), hbm(qkv_cross)) * 3)


def backward_kernel(
    blocks,
    place_ref,
    ql_ref,
    qc_ref,
    kl_ref,
    kc_ref,
    vl_ref,
    vc_ref,
    o0,
    o1,
    g0,
    g1,
    lse_ref,
    x0,
    x1,
    x2,
    x3,
    out0,
    out1,
    dq_ref,
    dk_ref,
    dv_ref,
    *rest,
):
    *weight_refs, dk_acc, dv_acc, turned_ref = rest
    step = pl.program_id(0)

    @pl.when(step == 0)
    def _():
        x = jnp.concatenate([x0[...], x1[...], x2[...], x3[...]], axis=0)
        turned_ref[...] = (x.astype(f32) * inv_keep).astype(bf16).T

    chunk = ql_ref.shape[0]
    scale = 1.0 / math.sqrt(HEAD)
    key = jnp.concatenate([kl_ref[...], kc_ref[...]], axis=0)
    mask = key_mask(place_ref, key.shape[0])
    keys = [one_head(key, h, mask) for h in (0, 1)]
    key_t = key.T
    value = jnp.concatenate([vl_ref[...], vc_ref[...]], axis=0)
    one = jnp.ones((), bf16)
    for c, q_ref in enumerate((ql_ref, qc_ref)):
        at = slice(c * chunk, (c + 1) * chunk)
        half = slice(c * chunk // 2, (c + 1) * chunk // 2)
        out = jnp.concatenate([o0[half, :], o1[half, :]], axis=0)
        do = jnp.concatenate([g0[half, :], g1[half, :]], axis=0)
        q = q_ref[...] * jnp.asarray(scale, bf16)
        prod_t = (do.astype(f32) * out.astype(f32)).T
        ps, dss, dos, qs, dq_t = [], [], [], [], []
        for h in (0, 1):
            rows = slice(HEAD * h, HEAD * (h + 1))
            s = dot_t(keys[h], one_head(q, h, one))
            p = jnp.exp(s - lse_ref[0, h : h + 1, at])
            do_h = one_head(do, h, None)
            dp = dot_t(value, do_h)
            delta = jnp.sum(prod_t[rows, :], axis=0, keepdims=True)
            ds = (p * (dp - delta)).astype(bf16)
            ps.append(p.astype(bf16))
            dss.append(ds)
            dos.append(do_h)
            qs.append(one_head(q, h, None))
            dq_t.append(dot(key_t[rows, :], ds))
        dv_c = dot(jnp.concatenate(ps, 1), jnp.concatenate(dos, 0))
        dk_c = dot(jnp.concatenate(dss, 1), jnp.concatenate(qs, 0))
        if c == 0:
            dv_acc[...] = dv_c
            dk_acc[...] = dk_c
        else:
            dv_ref[...] = (dv_acc[...] + dv_c).astype(bf16)
            dk_ref[...] = (dk_acc[...] + dk_c).astype(bf16)
        dq_ref[at, :] = (jnp.concatenate(dq_t, 0).T * scale).astype(bf16)

    grads = jnp.concatenate([dq_ref[...], dk_ref[...], dv_ref[...]], axis=1)
    part = dot(turned_ref[...], grads).astype(bf16)
    size = part.shape[1] // 3
    width = part.shape[0]
    cut = width // 4
    deep = width // blocks

    def store(side, at, values):
        count = values.shape[1]
        values = values.reshape(blocks, deep, count)
        done = 0
        for ref in weight_refs:
            lines = ref.shape[1] // blocks
            ref[side, :, at : at + count] = values[:, done : done + lines].reshape(blocks * lines, count)
            done += lines

    for i in range(2 * cut // size):

        @pl.when(step == i)
        def _(i=i):
            for kind in range(3):
                done = 0
                while done < size:
                    column = kind * 2 * cut + i * size + done
                    side, at = column // (3 * cut), column % (3 * cut)
                    count = min(size - done, 3 * cut - at)
                    source = kind * size + done
                    store(side, at, part[:, source : source + count])
                    done += count
            if i == 0:
                for side in (0, 1):
                    store(side, 3 * cut, add_low(out0[side, :, :cut], out1[side, :, :cut]))


def attend_backward(place, qkv_local, qkv_cross, own, send, g_own, g_pair, lse, kept, outs, blocks, splits):
    rows, pairs = qkv_local.shape[0], qkv_local.shape[1] // 384
    width = kept[0].shape[1]

    def block(offset):
        return [pl.BlockSpec((rows, 128), lambda i: (0, i + offset))] * 2

    return pl.pallas_call(
        functools.partial(backward_kernel, blocks),
        grid=(pairs,),
        in_specs=[pl.BlockSpec(memory_space=pltpu.SMEM)]
        + block(0)
        + block(pairs)
        + block(2 * pairs)
        + block(0) * 2
        + [pl.BlockSpec((1, 2, 2 * rows), lambda i: (i, 0, 0))]
        + [whole(kept[0].shape)] * 4
        + [whole(outs[0].shape)] * 2,
        out_specs=[pl.BlockSpec((2 * rows, 128), lambda i: (0, i))] * 3
        + [whole((2, blocks * lines, width)) for lines in splits],
        out_shape=[pltpu.HBM((2 * rows, pairs * 128), bf16)] * 3
        + [pltpu.HBM((2, blocks * lines, width), bf16) for lines in splits],
        scratch_shapes=[pltpu.VMEM((2 * rows, 128), f32)] * 2 + [pltpu.VMEM((width, 2 * rows), bf16)],
        compiler_params=params(56),
        cost_estimate=cost(24),
        name="attend_backward",
    )(place, *[hbm(x) for x in (qkv_local, qkv_cross) * 3 + (own, send, g_own, g_pair, lse) + kept + outs])


def project_local(half, own, pair, w_qkv, biases):
    rows, width = own.shape
    cut = width // 4

    def body(scalars, reads, writes, bias):
        (half,) = scalars
        for which in (2, 3, 0, 1):
            reads.start(which)
        w, b = reads.wait(2), reads.wait(3)
        w_own, b_own = writes.buffers[0], writes.buffers[1]
        for who in (0, 1):

            @pl.when(half == who)
            def _(who=who):
                for kind in range(3):
                    base = kind * width
                    lines = [slice(base + (who + 2 * i) * cut, base + (who + 2 * i + 1) * cut) for i in (0, 1)]
                    target = slice(kind * 2 * cut, (kind + 1) * 2 * cut)
                    w_own[:, target] = jnp.concatenate([w[:, line] for line in lines], axis=1)
                    if kind == 1:
                        b_own[:, target] = jnp.zeros((8, 2 * cut), f32)
                    else:
                        row = b[kind // 2 : kind // 2 + 1, :]
                        row = jnp.concatenate([row[:, line.start - base : line.stop - base] for line in lines], axis=1)
                        b_own[:, target] = jnp.broadcast_to(row, (8, 2 * cut))

        writes.start(0)
        writes.start(1)
        x = jnp.concatenate([reads.wait(0)[...], reads.wait(1)[...]], axis=0)
        x = (x.astype(f32) * inv_keep).astype(bf16)
        writes.buffers[2][...] = (dot(x, w_own[...]) + b_own[0:1, :]).astype(bf16)
        writes.start(2)

    return streamed(
        body,
        [half],
        [own, pair, w_qkv, biases],
        [struct((width, 6 * cut), bf16), struct((8, 6 * cut), f32), struct((2 * rows, 6 * cut), bf16)],
        [pltpu.VMEM((8, 128), f32)],
        (4, 3),
        "project_local",
        5,
    )


def project_cross(own, pair, w_own, b_own):
    rows = own.shape[0]

    def body(scalars, reads, writes):
        for which in range(4):
            reads.start(which)
        x = jnp.concatenate([reads.wait(0)[...], reads.wait(1)[...]], axis=0)
        x = (x.astype(f32) * inv_keep).astype(bf16)
        w, b = reads.wait(2), reads.wait(3)
        writes.buffers[0][...] = (dot(x, w[...]) + b[0:1, :]).astype(bf16)
        writes.start(0)

    return streamed(
        body,
        [],
        [own, pair, w_own, b_own],
        [struct((2 * rows, w_own.shape[1]), bf16)],
        [],
        (4, 1),
        "project_cross",
        4,
    )[0]


def norm_parts(values):
    mean = jnp.mean(values, axis=-1, keepdims=True)
    centred = values - mean
    inv = lax.rsqrt(jnp.mean(centred * centred, axis=-1, keepdims=True) + 1e-06)
    return centred * inv, inv


def norm_back(g, normal, inv, gain):
    a = g * gain
    return (
        a - jnp.mean(a, axis=-1, keepdims=True) - normal * jnp.mean(a * normal, axis=-1, keepdims=True)
    ) * inv


def gelu_parts(u):
    e = jnp.exp(-0.5 * u * u)
    t = 1.0 / (1.0 + (0.3275911 / math.sqrt(2.0)) * jnp.abs(u))
    poly = 0.5 * 1.061405429
    for a in (-1.453152027, 1.421413741, -0.284496736, 0.254829592):
        poly = poly * t + 0.5 * a
    tail = poly * t * e
    phi = jnp.where(u < 0, tail, 1.0 - tail)
    return u * phi, phi + u * e * (1.0 / math.sqrt(2.0 * math.pi))


def layer_forward(half, own, pair, kept, keep, w_out, w_up, w_down, gains, biases, up_bias):
    rows, width = kept[0].shape
    hid = w_up.shape[1]
    parts = hid // width
    tile = (rows, width)
    full = (2 * rows, width)
    cuts = [slice(c * width, (c + 1) * width) for c in range(parts)]
    OWN, PAIR_, KEPT, KEEP, W_OUT, W_UP, W_DOWN, GAINS, BIASES, UP_BIAS = 0, 1, 2, 4, 6, 7, 8, 9, 10, 11
    HIDDEN, SLOPE, H1_LOW, NORMAL1, INV1, NORMAL2, INV2, MIXED = range(8)

    def body(scalars, reads, writes, h1):
        (half,) = scalars
        for which in (OWN, PAIR_, W_OUT, BIASES, KEPT, KEPT + 1, GAINS, UP_BIAS):
            reads.start(which)
        for c, at in enumerate(cuts):
            reads.start(W_UP, c, (slice(None), at))
            reads.start(W_DOWN, c, (at,))
        reads.start(KEEP)
        reads.start(KEEP + 1)
        own, pair, w_out = (reads.wait(w)[...] for w in (OWN, PAIR_, W_OUT))
        biases = reads.wait(BIASES)
        half = jnp.int32(half)

        def mine(who):
            w = reads.buffers[W_OUT]
            return jnp.concatenate([w[who], w[who + 2]], axis=0)

        attn = dot(own, mine(half)) + dot(pair, mine(1 - half)) + biases[2:3, :]
        xin = jnp.concatenate([reads.wait(KEPT)[...], reads.wait(KEPT + 1)[...]], axis=0)
        normal, inv = norm_parts(xin.astype(f32) * inv_keep + attn)
        gains = reads.wait(GAINS)
        buf = writes.buffers
        buf[NORMAL1][...] = normal.astype(bf16)
        buf[INV1][...] = jnp.broadcast_to(inv, buf[INV1].shape)
        h1[...] = normal * gains[0:1, :] + biases[3:4, :]
        h1_low = h1[...].astype(bf16)
        buf[H1_LOW][...] = h1_low
        for which in (NORMAL1, INV1, H1_LOW):
            writes.start(which)
        up_bias = reads.wait(UP_BIAS)
        for c in range(parts):
            reads.wait(W_UP, c)
            reads.wait(W_DOWN, c)
        ff = biases[4:5, :]
        for c, at in enumerate(cuts):
            up = dot(h1_low, reads.wait(W_UP, c)[:, at]) + up_bias[:, at]
            hidden, slope = gelu_parts(up)
            hidden = hidden.astype(bf16)
            buf[HIDDEN][:, at] = hidden
            buf[SLOPE][:, at] = slope.astype(bf16)
            writes.start(HIDDEN, c, (slice(None), at))
            writes.start(SLOPE, c, (slice(None), at))
            ff = ff + dot(hidden, reads.wait(W_DOWN, c)[at, :])
        keep = jnp.concatenate([reads.wait(KEEP)[...], reads.wait(KEEP + 1)[...]], axis=0)
        normal, inv = norm_parts(h1[...] + ff * (keep.astype(f32) * inv_keep))
        mixed = (normal * gains[1:2, :] + biases[5:6, :]).astype(bf16)
        buf[MIXED][...] = mixed[:rows]
        buf[MIXED + 1][...] = mixed[rows:]
        writes.start(MIXED)
        writes.start(MIXED + 1)
        buf[NORMAL2][...] = normal.astype(bf16)
        buf[INV2][...] = jnp.broadcast_to(inv, buf[INV2].shape)
        writes.start(NORMAL2)
        writes.start(INV2)

    return streamed(
        body,
        [half],
        [own, pair, *kept, *keep, w_out, w_up, w_down, gains, biases, up_bias],
        [
            struct((2 * rows, hid), bf16),
            struct((2 * rows, hid), bf16),
            struct(full, bf16),
            struct(full, bf16),
            struct((2 * rows, 128), f32),
            struct(full, bf16),
            struct((2 * rows, 128), f32),
            struct(tile, bf16),
            struct(tile, bf16),
        ],
        [pltpu.VMEM(full, f32)],
        (10 + 2 * parts, 7 + 2 * parts),
        "layer_forward",
        16,
    )


def loss_kernel(shift_ref, cls_ref, pool_ref, positive_ref, values_ref, order_ref, g_pre_ref, g_cls_ref):
    rows = cls_ref.shape[0]
    n = rows // 2
    row = lax.broadcasted_iota(jnp.int32, (rows, rows), 0)
    column = lax.broadcasted_iota(jnp.int32, (rows, rows), 1)
    view, sentence = (column % 2) ^ shift_ref[0], (column // 2) ^ shift_ref[1]
    cls = dot((row == view * n + sentence).astype(bf16), cls_ref[...]).astype(bf16)
    order_ref[...] = cls
    pooled = jnp.tanh(dot(cls, pool_ref[...]))
    inv = lax.rsqrt(jnp.sum(pooled * pooled, axis=-1, keepdims=True) + 1e-06)
    unit = pooled * inv
    anchors, candidates = unit[:n], unit[n:]

    def exact(a, b, dims):
        return lax.dot_general(a, b, (dims, ((), ())), precision=highest, preferred_element_type=f32)

    logits = exact(anchors, candidates, ((1,), (1,))) / 0.05
    mine = lax.broadcasted_iota(jnp.int32, (n, n), 0)
    other = lax.broadcasted_iota(jnp.int32, (n, n), 1)
    picked = (other == positive_ref[:, 0:1]).astype(f32)
    top = jnp.max(logits, axis=1, keepdims=True)
    expo = jnp.exp(logits - top)
    total = jnp.sum(expo, axis=1, keepdims=True)
    target = jnp.sum(logits * picked, axis=1, keepdims=True)
    loss = jnp.mean(jnp.log(total) + top - target, axis=0, keepdims=True)
    matched = exact(picked, candidates, ((1,), (0,)))
    offset = anchors - matched
    alignment = jnp.mean(jnp.sum(offset * offset, axis=-1, keepdims=True), axis=0, keepdims=True)
    inner = exact(anchors, anchors, ((1,), (1,)))
    norms = jnp.sum(anchors * anchors, axis=-1, keepdims=True)
    norms_row = jnp.sum(jnp.where(mine == other, norms, 0.0), axis=0, keepdims=True)
    dist = norms + norms_row - 2.0 * inner
    near = jnp.where(mine != other, jnp.exp(-2.0 * dist), 0.0)
    near = jnp.sum(jnp.sum(near, axis=1, keepdims=True), axis=0, keepdims=True)
    uniformity = jnp.log(near / (n * (n - 1)))
    line = lax.broadcasted_iota(jnp.int32, values_ref.shape, 0)
    values_ref[...] = jnp.where(line == 0, loss, jnp.where(line == 1, alignment, uniformity))
    g_logits = (expo / total - picked) * (1.0 / (0.05 * n))
    g_unit = jnp.concatenate(
        [exact(g_logits, candidates, ((1,), (0,))), exact(g_logits, anchors, ((0,), (0,)))], axis=0
    )
    g_pooled = inv * (g_unit - unit * jnp.sum(g_unit * unit, axis=-1, keepdims=True))
    g_pre = (g_pooled * (1.0 - pooled * pooled)).astype(bf16)
    g_pre_ref[...] = g_pre
    line = lax.broadcasted_iota(jnp.int32, g_pre.shape, 0)
    mine = jnp.where(line == shift_ref[0] * n + shift_ref[1], g_pre.astype(f32), 0.0)
    mine = jnp.broadcast_to(jnp.sum(mine, axis=0, keepdims=True), (8, mine.shape[1])).astype(bf16)
    g_cls_ref[...] = dot_t(mine, pool_ref[...])


def loss_parts(shift, cls, pool_w, positive):
    rows, width = cls.shape
    return pl.pallas_call(
        loss_kernel,
        in_specs=[pl.BlockSpec(memory_space=pltpu.SMEM)] + [pl.BlockSpec(memory_space=pltpu.VMEM)] * 3,
        out_shape=[
            struct((8, 128), f32),
            struct((rows, width), bf16),
            struct((rows, width), bf16),
            struct((8, width), f32),
        ],
        compiler_params=params(16),
        cost_estimate=cost(2),
        name="contrast",
    )(shift, cls, pool_w, positive)


def down_backward(half, side, g_parts, g_cls, normal, inv, keeps, gains, hidden):
    rows, width = g_parts[0].shape
    hid = hidden.shape[1]
    wide = hid // GROUPS
    deep = width // 8
    part = struct((GROUPS, 2, deep, 2 * wide), bf16)
    full = (2 * rows, width)
    G, G_CLS, NORMAL, INV, KEEP, GAINS, HIDDEN = 0, 2, 3, 4, 5, 7, 8
    G_H2, G_FF, SUMS, SEND, KEPT = range(5)
    cuts = [slice(i * wide, (i + 2) * wide) for i in range(0, GROUPS, 2)]

    def body(scalars, reads, writes, turned):
        half, cls_side = scalars
        for which in (G, G + 1, G_CLS, NORMAL, INV, GAINS, KEEP, KEEP + 1):
            reads.start(which)
        for c, at in enumerate(cuts):
            reads.start(HIDDEN, c, (slice(None), at))
        buf = writes.buffers
        g = jnp.concatenate([reads.wait(G)[...], reads.wait(G + 1)[...]], axis=0).astype(f32)
        place = jnp.where(half == 0, cls_side * rows, 2 * rows)
        first = lax.broadcasted_iota(jnp.int32, g.shape, 0) == place
        g = g + jnp.where(first, reads.wait(G_CLS)[0:1, :], 0.0)
        normal = reads.wait(NORMAL)[...].astype(f32)
        g_h2 = norm_back(g, normal, reads.wait(INV)[:, 0:1], reads.wait(GAINS)[1:2, :])
        keep = jnp.concatenate([reads.wait(KEEP)[...], reads.wait(KEEP + 1)[...]], axis=0)
        g_ff = (g_h2 * (keep.astype(f32) * inv_keep)).astype(bf16)
        buf[G_H2][...] = g_h2.astype(bf16)
        buf[G_FF][...] = g_ff
        buf[SUMS][...] = jnp.concatenate(
            [jnp.sum(v, axis=0, keepdims=True) for v in (g * normal, g, g_ff.astype(f32))]
            + [jnp.zeros((5, width), f32)],
            axis=0,
        )
        for which in (G_H2, G_FF, SUMS):
            writes.start(which)
        turned[...] = g_ff.T.reshape(turned.shape)
        for who, ref in ((1 - half, SEND), (half, KEPT)):
            lhs = jnp.concatenate([turned[who], turned[who + 2]], axis=0)
            for c, at in enumerate(cuts):
                out = dot(lhs, reads.wait(HIDDEN, c)[:, at]).astype(bf16)
                for g in (0, 1):
                    for side in (0, 1):
                        lines = out[2 * side * deep : 2 * (side + 1) * deep, g * wide : (g + 1) * wide]
                        buf[ref][2 * c + g, side] = jnp.concatenate([lines[:deep], lines[deep:]], axis=1)
            writes.start(ref)

    return streamed(
        body,
        [half, side],
        [*g_parts, g_cls, normal, inv, *keeps, gains, hidden],
        [struct(full, bf16), struct(full, bf16), struct((8, width), f32), part, part],
        [pltpu.VMEM((4, width // 4, 2 * rows), bf16)],
        (8 + len(cuts), 5),
        "down_backward",
        8,
    )


def up_backward(half, g_ff, g_h2, w_down, w_up, slope, h1_low, normal, inv, gains, w_out, sums2):
    rows, width = h1_low.shape
    hid = w_up.shape[1]
    chunk = hid // 4
    block = struct((2, width, chunk), bf16)
    narrow = struct((rows, width // 2), bf16)
    full = (rows, width)
    G_FF, G_H2, W_DOWN, W_UP, SLOPE, H1, NORMAL, INV, GAINS, W_OUT, SUMS2 = range(11)
    SEND, KEPT, UP_SUM, G_ATTN, OWN, PAIR_, SUMS = range(7)

    def body(scalars, reads, writes, turned):
        (half,) = scalars
        steps = []
        for who, ref in ((1 - half, SEND), (half, KEPT)):
            for b in (0, 1):
                steps.append((ref, b, pl.ds(pl.multiple_of((2 * b + who) * chunk, chunk), chunk)))

        def fetch(c):
            at = steps[c][2]
            reads.start(W_DOWN, c, (at,))
            reads.start(SLOPE, c, (slice(None), at))
            reads.start(W_UP, c, (slice(None), at))

        for which in (G_FF, H1, G_H2):
            reads.start(which)
        fetch(0)
        fetch(1)
        for which in (G_FF, H1, G_H2):
            reads.wait(which)
        buf = writes.buffers
        g_ff = reads.wait(G_FF)[...]
        turned[...] = reads.wait(H1)[...].T
        g = reads.wait(G_H2)[...].astype(f32)
        for c, (ref, b, at) in enumerate(steps):
            for which in (W_DOWN, SLOPE, W_UP):
                reads.wait(which, c)
            if c < 2:
                fetch(c + 2)
            if c == 1:
                for which in (NORMAL, INV, GAINS, W_OUT, SUMS2):
                    reads.start(which)
            w_down = reads.buffers[W_DOWN][at, :]
            slope = reads.buffers[SLOPE][:, at]
            g_up = (dot_t(g_ff, w_down) * slope.astype(f32)).astype(bf16)
            buf[UP_SUM][:, at] = jnp.sum(g_up.astype(f32), axis=0, keepdims=True)
            buf[ref][b] = dot(turned[...], g_up).astype(bf16)
            writes.start(ref, b, (b,))
            g = g + dot_t(g_up, reads.buffers[W_UP][:, at])
        writes.start(UP_SUM)
        normal = reads.wait(NORMAL)[...].astype(f32)
        g_pre = norm_back(g, normal, reads.wait(INV)[:, 0:1], reads.wait(GAINS)[0:1, :])
        g_attn = g_pre.astype(bf16)
        w_out = reads.wait(W_OUT)
        for who, ref in ((1 - half, PAIR_), (half, OWN)):
            w = jnp.concatenate([w_out[who], w_out[who + 2]], axis=0)
            buf[ref][...] = dot_t(g_attn, w).astype(bf16)
            writes.start(ref)
        buf[G_ATTN][...] = g_attn
        writes.start(G_ATTN)
        first = [jnp.sum(v, axis=0, keepdims=True) for v in (g * normal, g, g_attn.astype(f32))]
        second = reads.wait(SUMS2)
        zero = jnp.zeros((2, width), f32)
        buf[SUMS][...] = jnp.concatenate(
            [first[0], second[0:1, :], zero, first[1], second[2:3, :], second[1:2, :], first[2]], axis=0
        )
        writes.start(SUMS)

    return streamed(
        body,
        [half],
        [g_ff, g_h2, w_down, w_up, slope, h1_low, normal, inv, gains, w_out, sums2],
        [
            block,
            block,
            struct((1, hid), f32),
            struct(full, bf16),
            narrow,
            narrow,
            struct((8, width), f32),
        ],
        [pltpu.VMEM((width, rows), bf16)],
        (20, 10),
        "up_backward",
        16,
    )


def out_backward(half, own, pair, g_attn):
    rows, width = g_attn.shape
    size = width // 4
    padded = -(-size // 128) * 128
    part = struct((2, width, padded), bf16)

    def body(scalars, reads, writes, ctx, cut):
        (half,) = scalars
        for which in range(3):
            reads.start(which)
        own_t, pair_t = reads.wait(0)[...].T, reads.wait(1)[...].T
        for b in (0, 1):
            lines = slice(b * size, (b + 1) * size)
            ctx[2 * b + half] = own_t[lines]
            ctx[2 * b + 1 - half] = pair_t[lines]
        g = reads.wait(2)
        for b in range(4):
            cut[b] = g[:, b * size : (b + 1) * size]
        lhs = ctx[...].reshape(4 * size, -1)
        for who, ref in ((1 - half, 0), (half, 1)):
            for b in (0, 1):
                writes.buffers[ref][b, :, :size] = dot(lhs, cut[2 * b + who]).astype(bf16)
                writes.buffers[ref][b, :, size:] = jnp.zeros((width, padded - size), bf16)
            writes.start(ref)

    return streamed(
        body,
        [half],
        [own, pair, g_attn],
        [part, part],
        [pltpu.VMEM((4, size, rows), bf16), pltpu.VMEM((4, rows, size), bf16)],
        (3, 2),
        "out_backward",
        4,
    )


def qkv_rows(half, w_own, g_query, g_key, g_value, g_pre, sums, up_sum):
    rows, width = g_pre.shape
    n, narrow = g_query.shape
    quarter = n // 4
    size = narrow // 2
    lines = up_sum.shape[1] // width

    def body(scalars, reads, writes, late):
        (half,) = scalars
        for which in range(7):
            reads.start(which)
        w = reads.wait(0)
        for which in (1, 0):
            total = None
            for i in range(3):
                g_ref = reads.wait(1 + i)
                g = jnp.concatenate(
                    [g_ref[(which + b) * quarter : (which + b + 1) * quarter, :] for b in (0, 2)], axis=0
                )
                part = dot_t(g, w[:, i * narrow : (i + 1) * narrow])
                total = part if total is None else total + part
            if which:
                writes.buffers[1][...] = total.astype(bf16)
            else:
                writes.buffers[0][...] = total + reads.wait(4)[...].astype(f32)
            writes.start(which)
        out = writes.buffers[2]
        out[0:8, :] = reads.wait(5)[...]
        tail = [reads.wait(6)[:, i * width : (i + 1) * width] for i in range(lines)]
        out[8:, :] = jnp.concatenate(tail + [jnp.zeros((8 - lines, width), f32)], axis=0)
        for line, which in ((2, 1), (3, 3)):
            total = jnp.sum(reads.buffers[which][...].astype(f32), axis=0, keepdims=True)
            for b in (0, 1):
                block = total[:, b * size : (b + 1) * size]
                zero = jnp.zeros_like(block)
                for who in (0, 1):
                    at = (2 * b + who) * size
                    out[line : line + 1, at : at + size] = jnp.where(half == who, block, zero)
        writes.start(2)

    return streamed(
        body,
        [half],
        [w_own, g_query, g_key, g_value, g_pre, sums, up_sum],
        [struct((rows, width), f32), struct((rows, width), bf16), struct((16, width), f32)],
        [pltpu.VMEM((8, 128), f32)],
        (7, 3),
        "qkv_rows",
        8,
    )


def pick(values, index, axis):
    return lax.dynamic_index_in_dim(values, index, axis, keepdims=False)


def add_low(a, b):
    return (a.astype(f32) + b.astype(f32)).astype(bf16)


class Halving:
    def __init__(self, values, shape, names, order, place):
        self.values = [v.reshape(shape) for v in values]
        self.names, self.order, self.place = list(names), list(order), place

    def total(self):
        return self.values[0] if len(self.values) == 1 else add_low(*self.values)

    def cut(self):
        step = self.order.pop(0)
        axis = self.names.index(step)
        self.names.pop(axis)
        side, dp, bits = self.place
        if step == "side":
            bit, self.route = side, ("seq", CROSS)
        else:
            bit = (dp >> step) & 1
            self.route = ("dp", [(d, d ^ (1 << step)) for d in range(1 << bits)])
        halves = []
        for which in (1 - bit, bit):
            parts = [pick(v, which, axis) for v in self.values]
            halves.append(parts[0] if len(parts) == 1 else add_low(*parts))
        return halves

    def join(self, arrived, kept):
        self.values = [kept, arrived]


class Summing:
    def __init__(self, values, bits):
        self.values = values
        self.order = [("seq", PAIR), ("seq", CROSS)]
        self.order += [("dp", [(d, d ^ (1 << k)) for d in range(1 << bits)]) for k in range(bits)]

    def cut(self):
        self.route = self.order.pop(0)
        return self.values, None

    def join(self, arrived, kept):
        self.values = self.values + arrived


class Rows:
    def __init__(self, own, send, length):
        self.values, self.send, self.length, self.order = own, send, length, [PAIR, CROSS]

    def cut(self):
        self.route = ("seq", self.order.pop(0))
        if self.order:
            return self.send, self.values
        return self.values[self.length :].astype(bf16), self.values[: self.length]

    def join(self, arrived, kept):
        self.values = kept + arrived.astype(f32) if self.order else (kept, arrived)


def advance(streams, *others):
    streams = [stream for stream in streams if stream.order]
    cuts = [stream.cut() for stream in streams]
    cuts, others = lax.optimization_barrier((cuts, others))
    for stream, (send, kept) in zip(streams, cuts):
        stream.join(lax.ppermute(send, *stream.route), kept)
    return others


class Tiled:
    def __init__(self, values, names, lines, order):
        self.values, self.names, self.lines, self.order = values, list(names), lines, list(order)

    def total(self):
        parts = [lax.slice_in_dim(v, at, at + self.lines, axis=0) for v, at in self.values]
        return parts[0] if len(parts) == 1 else add_low(*parts)


def combine(bits_of, streams):
    streams = [stream for stream in streams if stream.order]
    arrays, cuts, links = [], [], {}
    for stream in streams:
        step = stream.order.pop(0)
        axis = stream.names.index(step)
        stream.names.pop(axis)
        half = (stream.lines << len(stream.names) + 1) // 2
        at = links.setdefault(step, 0)
        links[step] += half
        loads = []
        for array, first in stream.values:
            known = [i for i, a in enumerate(arrays) if a is array]
            loads.append((known[0] if known else len(arrays), first))
            if not known:
                arrays.append(array)
        cuts.append((step, at, 1 << axis, half >> axis, half, loads))
    steps = list(links)
    width = arrays[0].shape[1]

    def body(scalars, reads, writes):
        (place,) = scalars
        for i, (_, _, _, _, half, loads) in enumerate(cuts):
            for which, first in loads:
                reads.start(which, i, (pl.ds(first, 2 * half),))
        for i, (step, at, pre, post, half, loads) in enumerate(cuts):
            for which, _ in loads:
                reads.wait(which, i)
            bit = place[0 if step == "side" else step + 1]
            tile = math.gcd(post, 96)
            targets = ((steps.index(step), at, 1 - bit), (len(steps) + i, 0, bit))

            def move(p, post=post, loads=loads, tile=tile, targets=targets):
                for out, base, which in targets:
                    source = (2 * p + which) * post

                    def one(t, source=source, out=out, base=base):
                        rows = [
                            reads.buffers[w][pl.ds(pl.multiple_of(first + source + t * tile, 16), tile), :]
                            for w, first in loads
                        ]
                        total = rows[0] if len(rows) == 1 else add_low(*rows)
                        spot = pl.multiple_of(base + p * post + t * tile, 16)
                        writes.buffers[out][pl.ds(spot, tile), :] = total

                    if post == tile:
                        one(0)
                    else:
                        pl.loop(0, post // tile)(one)

            for p in range(pre):
                move(p)
            writes.start(steps.index(step), i, (pl.ds(at, half),))
            writes.start(len(steps) + i)

    outs = streamed(
        body,
        [bits_of],
        arrays,
        [struct((links[step], width), bf16) for step in steps] + [struct((c[4], width), bf16) for c in cuts],
        [],
        (sum(len(c[5]) for c in cuts), 2 * len(cuts)),
        "combine",
        4,
    )
    sends = dict(zip(steps, outs))
    for stream, (step, at, _, _, _, _), kept in zip(streams, cuts, outs[len(steps) :]):
        stream.values = [(kept, 0), (step, at)]
    return sends


def exchange(streams, sends, bits):
    arrived = {}
    for step, send in sends.items():
        if step == "side":
            arrived[step] = lax.ppermute(send, "seq", CROSS)
        else:
            arrived[step] = lax.ppermute(send, "dp", [(d, d ^ (1 << step)) for d in range(1 << bits)])
    for stream in streams:
        stream.values = [(arrived.get(v, v) if isinstance(v, (str, int)) else v, at) for v, at in stream.values]


def hold(small, streams):
    arrays = list({id(v): v for stream in streams for v, _ in stream.values}.values())
    held = advance(small, *arrays)
    where = {id(v): h for v, h in zip(arrays, held)}
    for stream in streams:
        stream.values = [(where[id(v)], at) for v, at in stream.values]


def gather_step(values, at, bits):
    count = 4 << bits

    def partner(device, offset):
        for k in (0, 1):
            if offset >> k & 1 and at + k <= bits:
                device ^= 2 if at + k == 0 else 4 << (at + k - 1)
        return device

    offsets = range(1, 4 if at + 1 <= bits else 2)
    parts = [
        lax.ppermute(values, ("dp", "seq"), [(d, partner(d, offset)) for d in range(count)]) for offset in offsets
    ]
    return jnp.concatenate([values] + parts, axis=0)


def own_heads(values, half, axis):
    size = values.shape[axis] // 4
    shape = values.shape[:axis] + (2, 2, size) + values.shape[axis + 1 :]
    out = pick(values.reshape(shape), half, axis + 1)
    return out.reshape(values.shape[:axis] + (2 * size,) + values.shape[axis + 1 :])


def after(value, *others):
    return lax.optimization_barrier((value,) + others)[0]


def body(
    embeds,
    lengths,
    drop_in,
    drop_ff,
    positive,
    w_qkv,
    w_out,
    w_up,
    w_down,
    pool_w,
    gains,
    biases,
    up_bias,
    out_grad,
):
    _, _, length, width = drop_in.shape
    n_dp = lax.axis_size("dp")
    bits = n_dp.bit_length() - 1
    seq = lax.axis_index("seq")
    dp = lax.axis_index("dp")
    side, half = seq // 2, seq % 2
    half1 = half.astype(jnp.int32).reshape(1)
    side1 = side.astype(jnp.int32).reshape(1)
    first_side = side == 0
    place_keys = jnp.stack([seq.astype(jnp.int32), lengths[0]])

    token = embeds[0]
    masks_in = (pick(drop_in, side, 0)[0], pick(drop_in, 1 - side, 0)[0])
    kept_send = token * masks_in[1].astype(bf16)
    kept_cross = lax.ppermute(kept_send, "seq", CROSS)
    kept_local = token * masks_in[0].astype(bf16)
    kept_local_pair = lax.ppermute(kept_local, "seq", PAIR)

    w_own, b_own, qkv_local = project_local(half1, kept_local, kept_local_pair, w_qkv, biases)
    kept_cross, w_own = lax.optimization_barrier((kept_cross, w_own))
    kept_cross_pair = lax.ppermute(kept_cross, "seq", PAIR)
    qkv_cross = project_cross(kept_cross, kept_cross_pair, w_own, b_own)
    kept = (kept_local, kept_local_pair, kept_cross, kept_cross_pair)
    rest = jnp.stack([pick(drop_ff, 1 - side, 0)[0].astype(bf16), pick(out_grad, 1 - side, 0)[0]])
    rest = lax.ppermute(after(rest, kept_cross), "seq", CROSS)
    keeps = (pick(drop_ff, side, 0)[0].astype(bf16), rest[0])
    g_parts = (pick(out_grad, side, 0)[0], rest[1])
    w_out4 = w_out.reshape(4, width // 4, width)
    up_bias2 = up_bias[None]

    own, send, lse = attend_forward(place_keys, qkv_local, qkv_cross)
    pair = lax.ppermute(send, "seq", PAIR)
    hidden, slope, h1_low, normal1, inv1, normal2, inv2, mixed_local, mixed_cross = layer_forward(
        half1, own, pair, (kept_local, kept_cross), keeps, w_out4, w_up, w_down, gains, biases, up_bias2
    )

    first = jnp.where(first_side, mixed_local[:1], mixed_cross[:1])
    first = jnp.where(half == 0, first, lax.ppermute(first, "seq", [(0, 1), (2, 3)]))
    rel = first
    for at in range(0, bits + 1, 2):
        rel = gather_step(rel, at, bits)
    shift = jnp.stack([side, dp]).astype(jnp.int32)
    positive_col = jnp.broadcast_to(positive[:, None], (n_dp, 128))
    values, cls_all, g_pre, g_cls = loss_parts(shift, rel, pool_w, positive_col)
    pool_rows, pool_cols = width // n_dp, width // 4
    grad_pool = t_dot(
        lax.dynamic_slice_in_dim(cls_all, dp * pool_rows, pool_rows, 1),
        lax.dynamic_slice_in_dim(g_pre, seq * pool_cols, pool_cols, 1),
    )
    mixed_back = lax.ppermute(after(mixed_cross, values), "seq", CROSS)
    mixed_out = jnp.stack(
        [jnp.where(first_side, mixed_local, mixed_back), jnp.where(first_side, mixed_back, mixed_local)]
    )[:, None]

    g_h2, g_ff, sums2, down_send, down_keep = down_backward(
        half1, side1, g_parts, g_cls, normal2, inv2, keeps, gains, hidden
    )
    g_ff, mixed_out = lax.optimization_barrier((g_ff, mixed_out))
    up_send, up_keep, up_sum, g_attn, g_own, g_send, sums = up_backward(
        half1, g_ff, g_h2, w_down, w_up, slope, h1_low, normal1, inv1, gains, w_out4, sums2
    )
    g_pair = lax.ppermute(g_send, "seq", PAIR)

    dims = (2,) * bits
    place = (side, dp, bits)
    dp_names = list(range(bits - 1, -1, -1))
    names = ["side"] + dp_names
    low = list(range(1, bits))
    sub = n_dp // GROUPS
    deep = width // n_dp
    cut = width // 4

    tiled = deep % 16 == 0
    down_pair = lax.ppermute(down_send, "seq", PAIR)
    up_pair = lax.ppermute(up_send, "seq", PAIR)
    g_attn, down_pair = lax.optimization_barrier((g_attn, down_pair))
    side_first, dp_first = ["side", 0] + low, [0, "side"] + low
    low_first = low[:1] + ["side", 0] + low[1:]
    if tiled:

        def flat(values):
            return values.reshape(-1, width)

        bits_of = jnp.stack([side] + [(dp >> k) & 1 for k in range(bits)]).astype(jnp.int32)
        down_order = [0] + low + ["side"]
        down = Tiled([(flat(down_keep), 0), (flat(down_pair), 0)], dp_names + ["side"], deep, down_order)
        up = Tiled([(flat(up_keep), 0), (flat(up_pair), 0)], names, deep, side_first)
        out_send, out_keep = out_backward(half1, own, pair, g_attn)
        outs = (out_keep, lax.ppermute(out_send, "seq", PAIR))
        sends = combine(bits_of, [down, up])
        g_own, g_pair, *held = lax.optimization_barrier((g_own, g_pair, *sends.values()))
        exchange([down, up], dict(zip(sends, held)), bits)
        splits = (deep - 32, 16, 16)
        *grads, part_a, part_b, part_c = attend_backward(
            place_keys, qkv_local, qkv_cross, own, send, g_own, g_pair, lse, kept, outs, n_dp, splits
        )
        qkv = [
            Tiled([(flat(part), 0)], names, lines, order)
            for part, lines, order in zip(
                (part_a, part_b, part_c), splits, (side_first, dp_first, low_first)
            )
        ]
        streams = qkv + [up, down]
        sends = combine(bits_of, streams)
        *grads, w_own = lax.optimization_barrier((*grads, w_own, *sends.values()))[:4]
        exchange(streams, sends, bits)
    else:
        sub = n_dp // GROUPS

        def turned(values):
            values = values.reshape(GROUPS, 2, width // 8, 2, sub, -1)
            return values.transpose(0, 4, 1, 3, 2, 5)

        down = Halving(
            [turned(down_keep), turned(down_pair)], dims + (2, cut, -1), dp_names + ["side"], dp_first, place
        )
        up = Halving([up_keep, up_pair], (2,) + dims + (deep, -1), names, side_first, place)
        out_send, out_keep = out_backward(half1, own, pair, g_attn)
        outs = (out_keep, lax.ppermute(out_send, "seq", PAIR))
        g_own, g_pair = advance([up, down], g_own, g_pair)
        *grads, part = attend_backward(
            place_keys, qkv_local, qkv_cross, own, send, g_own, g_pair, lse, kept, outs, 1, (width,)
        )
        qkv = [Halving([part], (2,) + dims + (deep, width), names, side_first, place)]
        streams = qkv + [up, down]
    g_x, g_x_send, sums = qkv_rows(half1, w_own, *grads, g_attn, sums, up_sum)
    small = [Summing(sums, bits), Rows(g_x, g_x_send, length)]
    advance(small)
    while any(stream.order for stream in streams + small):
        if tiled:
            hold(small, streams)
            if any(stream.order for stream in streams):
                sends = combine(bits_of, streams)
                exchange(streams, sends, bits)
        else:
            advance(streams + small)
    streams += small
    total, (g_x, g_x_cross) = streams[-2].values, streams[-1].values
    grad_up = up.total().astype(f32)
    grad_down = down.total()
    if tiled:
        grad_down = grad_down.reshape(deep, 2, -1).swapaxes(0, 1).reshape(cut, -1)
    grad_down = grad_down.astype(f32).T
    sum_qkv = jnp.concatenate([stream.total() for stream in qkv], axis=0)
    grad_out = sum_qkv[:, 3 * cut :].astype(f32)
    three = sum_qkv[:, : 3 * cut].reshape(deep, 3, cut)
    swapped = lax.ppermute(jnp.where(half == 0, three[:, 2], three[:, 0]), "seq", PAIR)
    left = jnp.where(half == 0, three[:, 0], three[:, 1])
    right = jnp.where(half == 0, three[:, 1], three[:, 2])
    grad_qkv = jnp.concatenate([left, swapped, right], axis=1).astype(f32)
    embeds_grad = (g_x * masks_in[0].astype(f32) + g_x_cross.astype(f32) * masks_in[1].astype(f32)) * inv_keep
    return (
        mixed_out,
        embeds_grad[None],
        grad_qkv,
        grad_out,
        grad_up,
        grad_down,
        grad_pool,
        total[0:2],
        total[2:7],
        total[7],
        total[8 : 8 + up_bias.shape[0] // width].reshape(-1),
        values[0, 0],
        values[1, 0],
        values[2, 0],
    )


def solution(mesh):
    tokens = P(None, "dp", "seq", None)
    placed = (P("dp", "seq", None), P("dp"), tokens, tokens) + (P(),) * 9 + (tokens,)
    weight = P("dp", "seq")
    return jax.shard_map(
        body,
        mesh=mesh,
        in_specs=placed,
        out_specs=(tokens, P("dp", "seq", None)) + (weight,) * 5 + (P(),) * 7,
        check_vma=False,
    )
```

```python
import functools
import math

import jax
import jax.numpy as jnp
from jax import lax
from jax.experimental import pallas as pl
from jax.experimental.pallas import tpu as pltpu
from jax.sharding import PartitionSpec as P

HEAD = 64
keep_rate = 0.9
inv_keep = 1.0 / keep_rate
highest = lax.Precision.HIGHEST
f32 = jnp.float32
bf16 = jnp.bfloat16

CROSS = [(i, i ^ 2) for i in range(4)]
PAIR = [(i, i ^ 1) for i in range(4)]
GROUPS = 8


def cost(time):
    return pl.CostEstimate(flops=time * 2_000_000_000, bytes_accessed=1 << 20, transcendentals=0)

CHUNK = 768


def dot(a, b):
    return jnp.dot(a, b, preferred_element_type=f32)


def dot_t(a, b):
    return lax.dot_general(a, b, (((1,), (1,)), ((), ())), preferred_element_type=f32)


def t_dot(a, b):
    return lax.dot_general(a, b, (((0,), (0,)), ((), ())), preferred_element_type=f32)


def whole(shape):
    return pl.BlockSpec(shape, lambda *_: (0,) * len(shape))


def struct(shape, dtype):
    return jax.ShapeDtypeStruct(shape, dtype)


def hbm(x):
    return pltpu.with_memory_space_constraint(x, pltpu.HBM)


def params(limit):
    return pltpu.CompilerParams(vmem_limit_bytes=limit << 20)


ALL = (slice(None),)


class Stream:
    def __init__(self, refs, buffers, sems, out):
        self.refs, self.buffers, self.sems, self.out = refs, buffers, sems, out
        self.count, self.copies = 0, {}

    def start(self, which, key=0, at=ALL):
        ref, buffer = self.refs[which].at[at], self.buffers[which].at[at]
        source, target = (buffer, ref) if self.out else (ref, buffer)
        copy = pltpu.make_async_copy(source, target, self.sems.at[self.count])
        copy.start()
        self.count += 1
        self.copies[which, key] = copy

    def wait(self, which, key=0):
        copy = self.copies.pop((which, key), None)
        if copy is not None:
            copy.wait()
        return self.buffers[which]

    def drain(self):
        for which, key in list(self.copies):
            self.wait(which, key)


def streamed(body, scalars, ins, outs, scratch, copies, name, time, limit=56, far=True):
    n_s, n_i, n_o = len(scalars), len(ins), len(outs)

    def kernel(*refs):
        cuts = [n_s, n_i, n_o, n_i, n_o, len(scratch), 1, 1]
        parts, at = [], 0
        for cut in cuts:
            parts.append(refs[at : at + cut])
            at += cut
        reads = Stream(parts[1], parts[3], parts[6][0], False)
        writes = Stream(parts[2], parts[4], parts[7][0], True)
        body([r[0] if r.shape[0] == 1 else r for r in parts[0]], reads, writes, *parts[5])
        reads.drain()
        writes.drain()

    smem, home = pl.BlockSpec(memory_space=pltpu.SMEM), pl.BlockSpec(memory_space=pltpu.HBM)
    if far:
        ins = [hbm(x) for x in ins]
    return pl.pallas_call(
        kernel,
        in_specs=[smem] * n_s + [home if far else pl.BlockSpec(memory_space=pl.ANY)] * n_i,
        out_specs=[home] * n_o,
        out_shape=[pltpu.HBM(o.shape, o.dtype) for o in outs],
        scratch_shapes=[pltpu.VMEM(x.shape, x.dtype) for x in list(ins) + list(outs)]
        + list(scratch)
        + [pltpu.SemaphoreType.DMA((copies[0],)), pltpu.SemaphoreType.DMA((copies[1],))],
        compiler_params=params(limit),
        cost_estimate=cost(time),
        name=name,
    )(*scalars, *ins)


def one_head(block, head, extra):
    lane = lax.broadcasted_iota(jnp.int32, block.shape, 1)
    mine = (lane >= HEAD) if head else (lane < HEAD)
    out = jnp.where(mine, block, jnp.zeros_like(block))
    if extra is not None:
        out = jnp.where(lane == (0 if head else HEAD), extra, out)
    return out


def key_mask(place_ref, rows):
    quarter = rows // 4
    parts = []
    for b in range(4):
        at = lax.broadcasted_iota(jnp.int32, (quarter, 128), 0) + (place_ref[0] ^ b) * quarter
        parts.append(jnp.where(at < place_ref[1], 0.0, -1e30).astype(bf16))
    return jnp.concatenate(parts, axis=0)


def forward_kernel(place_ref, ql_ref, qc_ref, kl_ref, kc_ref, vl_ref, vc_ref, own_ref, send_ref, lse_ref):
    key = jnp.concatenate([kl_ref[...], kc_ref[...]], axis=0)
    mask = key_mask(place_ref, key.shape[0])
    keys = [one_head(key, h, mask) for h in (0, 1)]
    value_t = jnp.concatenate([vl_ref[...], vc_ref[...]], axis=0).T
    one = jnp.ones((), bf16)
    rows = ql_ref.shape[0]
    cut = rows // 2
    units = [(part, c, h) for part in (0, 1) for c in (0, 1) for h in (0, 1)]
    scores, weights = [], []
    for part, c, h in units:
        q = (ql_ref, qc_ref)[part][c * cut : (c + 1) * cut, :] * jnp.asarray(1.0 / math.sqrt(HEAD), bf16)
        scores.append(dot_t(keys[h], one_head(q, h, one)))
    for (part, c, h), s in zip(units, scores):
        top = jnp.max(s, axis=0, keepdims=True)
        p = jnp.exp(s - top)
        total = jnp.sum(p, axis=0, keepdims=True)
        start = part * rows + c * cut
        lse_ref[0, h : h + 1, start : start + cut] = top + jnp.log(total)
        weights.append((p.astype(bf16), total))
    outs = [
        dot(value_t[HEAD * h : HEAD * (h + 1), :], p) * (1.0 / total)
        for (part, c, h), (p, total) in zip(units, weights)
    ]
    for i in range(0, len(units), 2):
        part, c, _ = units[i]
        out = jnp.concatenate(outs[i : i + 2], axis=0).T.astype(bf16)
        (own_ref, send_ref)[c][part * cut : (part + 1) * cut, :] = out


def attend_forward(place, qkv_local, qkv_cross):
    rows, pairs = qkv_local.shape[0], qkv_local.shape[1] // 384

    def block(offset):
        return [pl.BlockSpec((rows, 128), lambda i: (0, i + offset))] * 2

    return pl.pallas_call(
        forward_kernel,
        grid=(pairs,),
        in_specs=[pl.BlockSpec(memory_space=pltpu.SMEM)] + block(0) + block(pairs) + block(2 * pairs),
        out_specs=block(0) + [pl.BlockSpec((1, 2, 2 * rows), lambda i: (i, 0, 0))],
        out_shape=[
            pltpu.HBM((rows, pairs * 128), bf16),
            pltpu.HBM((rows, pairs * 128), bf16),
            pltpu.HBM((pairs, 2, 2 * rows), f32),
        ],
        compiler_params=params(56),
        cost_estimate=cost(13),
        name="attend_forward",
    )(place, *(hbm(qkv_local), hbm(qkv_cross)) * 3)


def backward_kernel(
    place_ref,
    ql_ref,
    qc_ref,
    kl_ref,
    kc_ref,
    vl_ref,
    vc_ref,
    o0,
    o1,
    g0,
    g1,
    lse_ref,
    dq_ref,
    dk_ref,
    dv_ref,
    dk_acc,
    dv_acc,
):
    chunk = ql_ref.shape[0]
    scale = 1.0 / math.sqrt(HEAD)
    key = jnp.concatenate([kl_ref[...], kc_ref[...]], axis=0)
    mask = key_mask(place_ref, key.shape[0])
    keys = [one_head(key, h, mask) for h in (0, 1)]
    key_t = key.T
    value = jnp.concatenate([vl_ref[...], vc_ref[...]], axis=0)
    one = jnp.ones((), bf16)
    for c, q_ref in enumerate((ql_ref, qc_ref)):
        at = slice(c * chunk, (c + 1) * chunk)
        half = slice(c * chunk // 2, (c + 1) * chunk // 2)
        out = jnp.concatenate([o0[half, :], o1[half, :]], axis=0)
        do = jnp.concatenate([g0[half, :], g1[half, :]], axis=0)
        q = q_ref[...] * jnp.asarray(scale, bf16)
        prod_t = (do.astype(f32) * out.astype(f32)).T
        ps, dss, dos, qs, dq_t = [], [], [], [], []
        for h in (0, 1):
            rows = slice(HEAD * h, HEAD * (h + 1))
            s = dot_t(keys[h], one_head(q, h, one))
            p = jnp.exp(s - lse_ref[0, h : h + 1, at])
            do_h = one_head(do, h, None)
            dp = dot_t(value, do_h)
            delta = jnp.sum(prod_t[rows, :], axis=0, keepdims=True)
            ds = (p * (dp - delta)).astype(bf16)
            ps.append(p.astype(bf16))
            dss.append(ds)
            dos.append(do_h)
            qs.append(one_head(q, h, None))
            dq_t.append(dot(key_t[rows, :], ds))
        dv_c = dot(jnp.concatenate(ps, 1), jnp.concatenate(dos, 0))
        dk_c = dot(jnp.concatenate(dss, 1), jnp.concatenate(qs, 0))
        if c == 0:
            dv_acc[...] = dv_c
            dk_acc[...] = dk_c
        else:
            dv_ref[...] = (dv_acc[...] + dv_c).astype(bf16)
            dk_ref[...] = (dk_acc[...] + dk_c).astype(bf16)
        dq_ref[at, :] = (jnp.concatenate(dq_t, 0).T * scale).astype(bf16)


def attend_backward(place, qkv_local, qkv_cross, own, send, g_own, g_pair, lse):
    rows, pairs = qkv_local.shape[0], qkv_local.shape[1] // 384

    def block(offset):
        return [pl.BlockSpec((rows, 128), lambda i: (0, i + offset))] * 2

    return pl.pallas_call(
        backward_kernel,
        grid=(pairs,),
        in_specs=[pl.BlockSpec(memory_space=pltpu.SMEM)]
        + block(0)
        + block(pairs)
        + block(2 * pairs)
        + block(0) * 2
        + [pl.BlockSpec((1, 2, 2 * rows), lambda i: (i, 0, 0))],
        out_specs=[pl.BlockSpec((2 * rows, 128), lambda i: (0, i))] * 3,
        out_shape=[pltpu.HBM((2 * rows, pairs * 128), bf16)] * 3,
        scratch_shapes=[pltpu.VMEM((2 * rows, 128), f32)] * 2,
        compiler_params=params(56),
        cost_estimate=cost(20),
        name="attend_backward",
    )(place, *[hbm(x) for x in (qkv_local, qkv_cross) * 3 + (own, send, g_own, g_pair, lse)])


def project_backward(half, bits_of, grads, kept, outs, w_own, g_attn, sums, up_sum, splits, lines):
    rows, width = g_attn.shape
    n, narrow = grads[0].shape
    quarter = n // 4
    cut = width // 4
    many = up_sum.shape[1] // width
    GRADS, KEPT, OUTS, W_OWN, G_ATTN, SUMS_IN, UP_SUM = 0, 3, 7, 9, 10, 11, 12
    OWN, SEND, SUMS, FIRST = range(4)
    if lines:
        weights = [(width // lines * take, width) for _, take in splits]
        results = [struct(shape, bf16) for shape in weights for _ in (0, 1)]
    else:
        results = [struct((2, width, width), bf16)]

    def body(scalars, reads, writes):
        half, bits_ref = scalars
        for which in (KEPT, KEPT + 1, KEPT + 2, KEPT + 3, 0, 1, 2, OUTS, OUTS + 1, W_OWN, G_ATTN, SUMS_IN, UP_SUM):
            reads.start(which)
        buf = writes.buffers
        x = jnp.concatenate([reads.wait(KEPT + i)[...] for i in range(4)], axis=0)
        x_t = (x.astype(f32) * inv_keep).astype(bf16).T
        for which in (0, 1, 2, OUTS, OUTS + 1):
            reads.wait(which)
        q, k, v = (reads.buffers[GRADS + i] for i in range(3))
        columns = (
            jnp.concatenate([q[...], k[:, :cut]], axis=1),
            jnp.concatenate([k[:, cut:], v[...]], axis=1),
        )
        for side in (0, 1):
            out = add_low(reads.buffers[OUTS][side, :, :cut], reads.buffers[OUTS + 1][side, :, :cut])
            part = jnp.concatenate([dot(x_t, columns[side]).astype(bf16), out], axis=1)
            if not lines:
                buf[FIRST][side] = part
                continue
            blocks = width // lines
            done = 0
            for i, (bit, take) in enumerate(splits):
                block = part.reshape(blocks, lines, width)[:, done : done + take]
                done += take
                target, kept = buf[FIRST + 2 * i], buf[FIRST + 2 * i + 1]
                if bit == 0:
                    block = block.reshape(blocks * take, width)

                    @pl.when(bits_ref[0] == side)
                    def _(block=block, kept=kept):
                        kept[...] = block

                    @pl.when(bits_ref[0] != side)
                    def _(block=block, target=target):
                        target[...] = block

                    continue
                post = 1 << bit - 1
                block = block.reshape(blocks // (2 * post), 2, post * take, width)
                size = blocks * take // 2
                spot = slice(side * size, (side + 1) * size)
                for value in (0, 1):
                    piece = block[:, value].reshape(size, width)

                    @pl.when(bits_ref[bit] == value)
                    def _(piece=piece, kept=kept, spot=spot):
                        kept[spot, :] = piece

                    @pl.when(bits_ref[bit] != value)
                    def _(piece=piece, target=target, spot=spot):
                        target[spot, :] = piece

        for i in range(len(results)):
            writes.start(FIRST + i)
        for which in (W_OWN, G_ATTN, SUMS_IN, UP_SUM):
            reads.wait(which)
        w = reads.buffers[W_OWN]
        for which, ref in ((1, SEND), (0, OWN)):
            total = None
            for i in range(3):
                g = reads.buffers[GRADS + i]
                g = jnp.concatenate(
                    [g[(which + b) * quarter : (which + b + 1) * quarter, :] for b in (0, 2)], axis=0
                )
                part = dot_t(g, w[:, i * narrow : (i + 1) * narrow])
                total = part if total is None else total + part
            if which == 0:
                total = total + reads.buffers[G_ATTN][...].astype(f32)
            buf[ref][...] = total.astype(bf16)
            writes.start(ref)
        buf[SUMS][0:8, :] = reads.buffers[SUMS_IN][...]
        tail = [reads.buffers[UP_SUM][:, i * width : (i + 1) * width] for i in range(many)]
        buf[SUMS][8:, :] = jnp.concatenate(tail + [jnp.zeros((8 - many, width), f32)], axis=0)
        for line, which in ((2, 0), (3, 2)):
            total = jnp.sum(reads.buffers[which][...].astype(f32), axis=0, keepdims=True)
            for b in (0, 1):
                block = total[:, b * cut : (b + 1) * cut]
                for who in (0, 1):
                    at = (2 * b + who) * cut
                    buf[SUMS][line : line + 1, at : at + cut] = jnp.where(half == who, block, jnp.zeros_like(block))
        writes.start(SUMS)

    return streamed(
        body,
        [half, bits_of],
        [*grads, *kept, *outs, w_own, g_attn, sums, up_sum],
        [struct((rows, width), bf16), struct((rows, width), bf16), struct((16, width), f32)] + results,
        [],
        (13, 3 + len(results)),
        "project_backward",
        10,
    )


def project_local(half, own, pair, w_qkv, biases):
    rows, width = own.shape
    cut = width // 4

    def body(scalars, reads, writes, bias):
        (half,) = scalars
        for which in (2, 3, 0, 1):
            reads.start(which)
        w, b = reads.wait(2), reads.wait(3)
        w_own, b_own = writes.buffers[0], writes.buffers[1]
        for who in (0, 1):

            @pl.when(half == who)
            def _(who=who):
                for kind in range(3):
                    base = kind * width
                    lines = [slice(base + (who + 2 * i) * cut, base + (who + 2 * i + 1) * cut) for i in (0, 1)]
                    target = slice(kind * 2 * cut, (kind + 1) * 2 * cut)
                    w_own[:, target] = jnp.concatenate([w[:, line] for line in lines], axis=1)
                    if kind == 1:
                        b_own[:, target] = jnp.zeros((8, 2 * cut), f32)
                    else:
                        row = b[kind // 2 : kind // 2 + 1, :]
                        row = jnp.concatenate([row[:, line.start - base : line.stop - base] for line in lines], axis=1)
                        b_own[:, target] = jnp.broadcast_to(row, (8, 2 * cut))

        writes.start(0)
        writes.start(1)
        x = jnp.concatenate([reads.wait(0)[...], reads.wait(1)[...]], axis=0)
        x = (x.astype(f32) * inv_keep).astype(bf16)
        writes.buffers[2][...] = (dot(x, w_own[...]) + b_own[0:1, :]).astype(bf16)
        writes.start(2)

    return streamed(
        body,
        [half],
        [own, pair, w_qkv, biases],
        [struct((width, 6 * cut), bf16), struct((8, 6 * cut), f32), struct((2 * rows, 6 * cut), bf16)],
        [pltpu.VMEM((8, 128), f32)],
        (4, 3),
        "project_local",
        5,
    )


def project_cross(own, pair, w_own, b_own):
    rows = own.shape[0]

    def body(scalars, reads, writes):
        for which in range(4):
            reads.start(which)
        x = jnp.concatenate([reads.wait(0)[...], reads.wait(1)[...]], axis=0)
        x = (x.astype(f32) * inv_keep).astype(bf16)
        w, b = reads.wait(2), reads.wait(3)
        writes.buffers[0][...] = (dot(x, w[...]) + b[0:1, :]).astype(bf16)
        writes.start(0)

    return streamed(
        body,
        [],
        [own, pair, w_own, b_own],
        [struct((2 * rows, w_own.shape[1]), bf16)],
        [],
        (4, 1),
        "project_cross",
        4,
    )[0]


def norm_parts(values):
    mean = jnp.mean(values, axis=-1, keepdims=True)
    centred = values - mean
    inv = lax.rsqrt(jnp.mean(centred * centred, axis=-1, keepdims=True) + 1e-06)
    return centred * inv, inv


def norm_back(g, normal, inv, gain):
    a = g * gain
    return (
        a - jnp.mean(a, axis=-1, keepdims=True) - normal * jnp.mean(a * normal, axis=-1, keepdims=True)
    ) * inv


def gelu_parts(u):
    e = jnp.exp(-0.5 * u * u)
    t = 1.0 / (1.0 + (0.3275911 / math.sqrt(2.0)) * jnp.abs(u))
    poly = 0.5 * 1.061405429
    for a in (-1.453152027, 1.421413741, -0.284496736, 0.254829592):
        poly = poly * t + 0.5 * a
    tail = poly * t * e
    phi = jnp.where(u < 0, tail, 1.0 - tail)
    return u * phi, phi + u * e * (1.0 / math.sqrt(2.0 * math.pi))


def layer_forward(half, own, pair, kept, keep, w_out, w_up, w_down, gains, biases, up_bias):
    rows, width = kept[0].shape
    hid = w_up.shape[1]
    parts = hid // width
    tile = (rows, width)
    full = (2 * rows, width)
    cuts = [slice(c * width, (c + 1) * width) for c in range(parts)]
    OWN, PAIR_, KEPT, KEEP, W_OUT, W_UP, W_DOWN, GAINS, BIASES, UP_BIAS = 0, 1, 2, 4, 6, 7, 8, 9, 10, 11
    HIDDEN, SLOPE, H1_LOW, NORMAL1, INV1, NORMAL2, INV2, MIXED = range(8)

    def body(scalars, reads, writes, h1):
        (half,) = scalars
        for which in (OWN, PAIR_, W_OUT, BIASES, KEPT, KEPT + 1, GAINS, UP_BIAS):
            reads.start(which)
        for c, at in enumerate(cuts):
            reads.start(W_UP, c, (slice(None), at))
            reads.start(W_DOWN, c, (at,))
        reads.start(KEEP)
        reads.start(KEEP + 1)
        own, pair, w_out = (reads.wait(w)[...] for w in (OWN, PAIR_, W_OUT))
        biases = reads.wait(BIASES)
        half = jnp.int32(half)

        def mine(who):
            w = reads.buffers[W_OUT]
            return jnp.concatenate([w[who], w[who + 2]], axis=0)

        attn = dot(own, mine(half)) + dot(pair, mine(1 - half)) + biases[2:3, :]
        xin = jnp.concatenate([reads.wait(KEPT)[...], reads.wait(KEPT + 1)[...]], axis=0)
        normal, inv = norm_parts(xin.astype(f32) * inv_keep + attn)
        gains = reads.wait(GAINS)
        buf = writes.buffers
        buf[NORMAL1][...] = normal.astype(bf16)
        buf[INV1][...] = jnp.broadcast_to(inv, buf[INV1].shape)
        h1[...] = normal * gains[0:1, :] + biases[3:4, :]
        h1_low = h1[...].astype(bf16)
        buf[H1_LOW][...] = h1_low
        for which in (NORMAL1, INV1, H1_LOW):
            writes.start(which)
        up_bias = reads.wait(UP_BIAS)
        for c in range(parts):
            reads.wait(W_UP, c)
            reads.wait(W_DOWN, c)
        ff = biases[4:5, :]
        for c, at in enumerate(cuts):
            up = dot(h1_low, reads.wait(W_UP, c)[:, at]) + up_bias[:, at]
            hidden, slope = gelu_parts(up)
            hidden = hidden.astype(bf16)
            buf[HIDDEN][:, at] = hidden
            buf[SLOPE][:, at] = slope.astype(bf16)
            writes.start(HIDDEN, c, (slice(None), at))
            writes.start(SLOPE, c, (slice(None), at))
            ff = ff + dot(hidden, reads.wait(W_DOWN, c)[at, :])
        keep = jnp.concatenate([reads.wait(KEEP)[...], reads.wait(KEEP + 1)[...]], axis=0)
        normal, inv = norm_parts(h1[...] + ff * (keep.astype(f32) * inv_keep))
        mixed = (normal * gains[1:2, :] + biases[5:6, :]).astype(bf16)
        buf[MIXED][...] = mixed[:rows]
        buf[MIXED + 1][...] = mixed[rows:]
        writes.start(MIXED)
        writes.start(MIXED + 1)
        buf[NORMAL2][...] = normal.astype(bf16)
        buf[INV2][...] = jnp.broadcast_to(inv, buf[INV2].shape)
        writes.start(NORMAL2)
        writes.start(INV2)

    return streamed(
        body,
        [half],
        [own, pair, *kept, *keep, w_out, w_up, w_down, gains, biases, up_bias],
        [
            struct((2 * rows, hid), bf16),
            struct((2 * rows, hid), bf16),
            struct(full, bf16),
            struct(full, bf16),
            struct((2 * rows, 128), f32),
            struct(full, bf16),
            struct((2 * rows, 128), f32),
            struct(tile, bf16),
            struct(tile, bf16),
        ],
        [pltpu.VMEM(full, f32)],
        (10 + 2 * parts, 7 + 2 * parts),
        "layer_forward",
        16,
    )


def loss_kernel(shift_ref, cls_ref, pool_ref, positive_ref, values_ref, order_ref, g_pre_ref, g_cls_ref):
    rows = cls_ref.shape[0]
    n = rows // 2
    row = lax.broadcasted_iota(jnp.int32, (rows, rows), 0)
    column = lax.broadcasted_iota(jnp.int32, (rows, rows), 1)
    view, sentence = (column % 2) ^ shift_ref[0], (column // 2) ^ shift_ref[1]
    cls = dot((row == view * n + sentence).astype(bf16), cls_ref[...]).astype(bf16)
    order_ref[...] = cls
    pooled = jnp.tanh(dot(cls, pool_ref[...]))
    inv = lax.rsqrt(jnp.sum(pooled * pooled, axis=-1, keepdims=True) + 1e-06)
    unit = pooled * inv
    anchors, candidates = unit[:n], unit[n:]

    def exact(a, b, dims):
        return lax.dot_general(a, b, (dims, ((), ())), precision=highest, preferred_element_type=f32)

    logits = exact(anchors, candidates, ((1,), (1,))) / 0.05
    mine = lax.broadcasted_iota(jnp.int32, (n, n), 0)
    other = lax.broadcasted_iota(jnp.int32, (n, n), 1)
    picked = (other == positive_ref[:, 0:1]).astype(f32)
    top = jnp.max(logits, axis=1, keepdims=True)
    expo = jnp.exp(logits - top)
    total = jnp.sum(expo, axis=1, keepdims=True)
    target = jnp.sum(logits * picked, axis=1, keepdims=True)
    loss = jnp.mean(jnp.log(total) + top - target, axis=0, keepdims=True)
    matched = exact(picked, candidates, ((1,), (0,)))
    offset = anchors - matched
    alignment = jnp.mean(jnp.sum(offset * offset, axis=-1, keepdims=True), axis=0, keepdims=True)
    inner = exact(anchors, anchors, ((1,), (1,)))
    norms = jnp.sum(anchors * anchors, axis=-1, keepdims=True)
    norms_row = jnp.sum(jnp.where(mine == other, norms, 0.0), axis=0, keepdims=True)
    dist = norms + norms_row - 2.0 * inner
    near = jnp.where(mine != other, jnp.exp(-2.0 * dist), 0.0)
    near = jnp.sum(jnp.sum(near, axis=1, keepdims=True), axis=0, keepdims=True)
    uniformity = jnp.log(near / (n * (n - 1)))
    line = lax.broadcasted_iota(jnp.int32, values_ref.shape, 0)
    values_ref[...] = jnp.where(line == 0, loss, jnp.where(line == 1, alignment, uniformity))
    g_logits = (expo / total - picked) * (1.0 / (0.05 * n))
    g_unit = jnp.concatenate(
        [exact(g_logits, candidates, ((1,), (0,))), exact(g_logits, anchors, ((0,), (0,)))], axis=0
    )
    g_pooled = inv * (g_unit - unit * jnp.sum(g_unit * unit, axis=-1, keepdims=True))
    g_pre = (g_pooled * (1.0 - pooled * pooled)).astype(bf16)
    g_pre_ref[...] = g_pre
    line = lax.broadcasted_iota(jnp.int32, g_pre.shape, 0)
    mine = jnp.where(line == shift_ref[0] * n + shift_ref[1], g_pre.astype(f32), 0.0)
    mine = jnp.broadcast_to(jnp.sum(mine, axis=0, keepdims=True), (8, mine.shape[1])).astype(bf16)
    g_cls_ref[...] = dot_t(mine, pool_ref[...])


def loss_parts(shift, cls, pool_w, positive):
    rows, width = cls.shape
    return pl.pallas_call(
        loss_kernel,
        in_specs=[pl.BlockSpec(memory_space=pltpu.SMEM)] + [pl.BlockSpec(memory_space=pltpu.VMEM)] * 3,
        out_shape=[
            struct((8, 128), f32),
            struct((rows, width), bf16),
            struct((rows, width), bf16),
            struct((8, width), f32),
        ],
        compiler_params=params(16),
        cost_estimate=cost(2),
        name="contrast",
    )(shift, cls, pool_w, positive)


def feed_backward(
    half, side, g_parts, g_cls, normal2, inv2, keeps, gains, hidden, w_down, w_up, slope, h1_low, normal1, inv1, w_out
):
    rows, width = h1_low.shape
    hid = hidden.shape[1]
    wide = hid // GROUPS
    chunk = hid // 4
    deep = width // 8
    full = (rows, width)
    down = struct((GROUPS, 2, deep, 2 * wide), bf16)
    up = struct((2, width, chunk), bf16)
    narrow = struct((rows, width // 2), bf16)
    G, G_CLS, NORMAL2, INV2, KEEP, GAINS, HIDDEN, W_DOWN, W_UP, SLOPE, H1, NORMAL1, INV1, W_OUT = (
        0, 2, 3, 4, 5, 7, 8, 9, 10, 11, 12, 13, 14, 15,
    )
    D_SEND, D_KEEP, U_SEND, U_KEEP, UP_SUM, G_ATTN, OWN, PAIR_, SUMS = range(9)
    cuts = [slice(i * wide, (i + 2) * wide) for i in range(0, GROUPS, 2)]

    def body(scalars, reads, writes, turned, turned_h1, g_h2_ref, g_ff_ref):
        half, cls_side = scalars
        steps = []
        for who, ref in ((1 - half, U_SEND), (half, U_KEEP)):
            for b in (0, 1):
                steps.append((ref, b, pl.ds(pl.multiple_of((2 * b + who) * chunk, chunk), chunk)))
        first = (G, G + 1, G_CLS, NORMAL2, INV2, GAINS, KEEP, KEEP + 1)
        for which in first:
            reads.start(which)
        reads.start(HIDDEN)
        reads.start(H1)
        for which in first:
            reads.wait(which)
        for c, (ref, b, at) in enumerate(steps):
            reads.start(W_DOWN, c, (at,))
            reads.start(SLOPE, c, (slice(None), at))
            reads.start(W_UP, c, (slice(None), at))
        for which in (NORMAL1, INV1, W_OUT):
            reads.start(which)
        got, buf = reads.buffers, writes.buffers
        g = jnp.concatenate([got[G][...], got[G + 1][...]], axis=0).astype(f32)
        place = jnp.where(half == 0, cls_side * (rows // 2), rows)
        here = lax.broadcasted_iota(jnp.int32, g.shape, 0) == place
        g = g + jnp.where(here, got[G_CLS][0:1, :], 0.0)
        normal = got[NORMAL2][...].astype(f32)
        g_h2 = norm_back(g, normal, got[INV2][:, 0:1], got[GAINS][1:2, :])
        keep = jnp.concatenate([got[KEEP][...], got[KEEP + 1][...]], axis=0)
        g_ff = (g_h2 * (keep.astype(f32) * inv_keep)).astype(bf16)
        g_h2_ref[...] = g_h2
        g_ff_ref[...] = g_ff
        second = [jnp.sum(v, axis=0, keepdims=True) for v in (g * normal, g, g_ff.astype(f32))]
        turned[...] = g_ff.T.reshape(turned.shape)
        reads.wait(HIDDEN)
        reads.wait(H1)
        for who, ref in ((1 - half, D_SEND), (half, D_KEEP)):
            lhs = jnp.concatenate([turned[who], turned[who + 2]], axis=0)
            for c, at in enumerate(cuts):
                out = dot(lhs, got[HIDDEN][:, at]).astype(bf16)
                for i in (0, 1):
                    for s in (0, 1):
                        lines = out[2 * s * deep : 2 * (s + 1) * deep, i * wide : (i + 1) * wide]
                        buf[ref][2 * c + i, s] = jnp.concatenate([lines[:deep], lines[deep:]], axis=1)
            writes.start(ref)
        turned_h1[...] = got[H1][...].T
        for c in range(4):
            for which in (W_DOWN, SLOPE, W_UP):
                reads.wait(which, c)
        g = g_h2_ref[...]
        for c, (ref, b, at) in enumerate(steps):
            g_up = (dot_t(g_ff_ref[...], got[W_DOWN][at, :]) * got[SLOPE][:, at].astype(f32)).astype(bf16)
            buf[UP_SUM][:, at] = jnp.sum(g_up.astype(f32), axis=0, keepdims=True)
            buf[ref][b] = dot(turned_h1[...], g_up).astype(bf16)
            writes.start(ref, b, (b,))
            g = g + dot_t(g_up, got[W_UP][:, at])
        writes.start(UP_SUM)
        for which in (NORMAL1, INV1, W_OUT):
            reads.wait(which)
        normal = got[NORMAL1][...].astype(f32)
        g_attn = norm_back(g, normal, got[INV1][:, 0:1], got[GAINS][0:1, :]).astype(bf16)
        for who, ref in ((1 - half, PAIR_), (half, OWN)):
            w = jnp.concatenate([got[W_OUT][who], got[W_OUT][who + 2]], axis=0)
            buf[ref][...] = dot_t(g_attn, w).astype(bf16)
            writes.start(ref)
        buf[G_ATTN][...] = g_attn
        writes.start(G_ATTN)
        first = [jnp.sum(v, axis=0, keepdims=True) for v in (g * normal, g, g_attn.astype(f32))]
        zero = jnp.zeros((2, width), f32)
        buf[SUMS][...] = jnp.concatenate(
            [first[0], second[0], zero, first[1], second[2], second[1], first[2]], axis=0
        )
        writes.start(SUMS)

    return streamed(
        body,
        [half, side],
        [
            *g_parts, g_cls, normal2, inv2, *keeps, gains, hidden, w_down, w_up, slope, h1_low, normal1, inv1, w_out,
        ],
        [
            down,
            down,
            up,
            up,
            struct((1, hid), f32),
            struct(full, bf16),
            narrow,
            narrow,
            struct((8, width), f32),
        ],
        [
            pltpu.VMEM((4, width // 4, rows), bf16),
            pltpu.VMEM((width, rows), bf16),
            pltpu.VMEM(full, f32),
            pltpu.VMEM(full, bf16),
        ],
        (25, 11),
        "feed_backward",
        20,
    )


def out_backward(half, own, pair, g_attn):
    rows, width = g_attn.shape
    size = width // 4
    padded = -(-size // 128) * 128
    part = struct((2, width, padded), bf16)

    def body(scalars, reads, writes, ctx, cut):
        (half,) = scalars
        for which in range(3):
            reads.start(which)
        own_t, pair_t = reads.wait(0)[...].T, reads.wait(1)[...].T
        for b in (0, 1):
            lines = slice(b * size, (b + 1) * size)
            ctx[2 * b + half] = own_t[lines]
            ctx[2 * b + 1 - half] = pair_t[lines]
        g = reads.wait(2)
        for b in range(4):
            cut[b] = g[:, b * size : (b + 1) * size]
        lhs = ctx[...].reshape(4 * size, -1)
        for who, ref in ((1 - half, 0), (half, 1)):
            for b in (0, 1):
                writes.buffers[ref][b, :, :size] = dot(lhs, cut[2 * b + who]).astype(bf16)
                writes.buffers[ref][b, :, size:] = jnp.zeros((width, padded - size), bf16)
            writes.start(ref)

    return streamed(
        body,
        [half],
        [own, pair, g_attn],
        [part, part],
        [pltpu.VMEM((4, size, rows), bf16), pltpu.VMEM((4, rows, size), bf16)],
        (3, 2),
        "out_backward",
        4,
    )


def pick(values, index, axis):
    return lax.dynamic_index_in_dim(values, index, axis, keepdims=False)


def add_low(a, b):
    return (a.astype(f32) + b.astype(f32)).astype(bf16)


class Halving:
    def __init__(self, values, shape, names, order, place):
        self.values = [v.reshape(shape) for v in values]
        self.names, self.order, self.place = list(names), list(order), place

    def total(self):
        return self.values[0] if len(self.values) == 1 else add_low(*self.values)

    def cut(self):
        step = self.order.pop(0)
        axis = self.names.index(step)
        self.names.pop(axis)
        side, dp, bits = self.place
        if step == "side":
            bit, self.route = side, ("seq", CROSS)
        else:
            bit = (dp >> step) & 1
            self.route = ("dp", [(d, d ^ (1 << step)) for d in range(1 << bits)])
        halves = []
        for which in (1 - bit, bit):
            parts = [pick(v, which, axis) for v in self.values]
            halves.append(parts[0] if len(parts) == 1 else add_low(*parts))
        return halves

    def join(self, arrived, kept):
        self.values = [kept, arrived]


class Summing:
    def __init__(self, values, bits):
        self.values = values
        self.order = [("seq", PAIR), ("seq", CROSS)]
        self.order += [("dp", [(d, d ^ (1 << k)) for d in range(1 << bits)]) for k in range(bits)]

    def cut(self):
        self.route = self.order.pop(0)
        return self.values, None

    def join(self, arrived, kept):
        self.values = self.values + arrived


class Rows:
    def __init__(self, own, send, length):
        self.values, self.send, self.length, self.order = own, send, length, [PAIR, CROSS]

    def cut(self):
        self.route = ("seq", self.order.pop(0))
        if self.order:
            return self.send, self.values
        return self.values[self.length :].astype(bf16), self.values[: self.length]

    def join(self, arrived, kept):
        self.values = kept.astype(f32) + arrived.astype(f32) if self.order else (kept, arrived)


def advance(streams, *others):
    streams = [stream for stream in streams if stream.order]
    cuts = [stream.cut() for stream in streams]
    cuts, others = lax.optimization_barrier((cuts, others))
    for stream, (send, kept) in zip(streams, cuts):
        stream.join(lax.ppermute(send, *stream.route), kept)
    return others


class Tiled:
    def __init__(self, values, names, lines, order):
        self.values, self.names, self.lines, self.order = values, list(names), lines, list(order)

    def total(self):
        parts = [lax.slice_in_dim(v, at, at + self.lines, axis=0) for v, at, _ in self.values]
        return parts[0] if len(parts) == 1 else add_low(*parts)


class Shared:
    def __init__(self, values, lines, order):
        self.values, self.lines, self.order = values, lines, list(order)

    total = Tiled.total


def combine(bits_of, streams):
    streams = [stream for stream in streams if stream.order]
    arrays, cuts, links = [], [], {}
    for stream in streams:
        step = stream.order.pop(0)
        if isinstance(stream, Shared):
            pre, half = 0, stream.lines
        else:
            axis = stream.names.index(step)
            stream.names.pop(axis)
            pre, half = 1 << axis, stream.lines << len(stream.names)
        at = links.setdefault(step, 0)
        links[step] += half
        loads = []
        for array, first, stride in stream.values:
            known = [i for i, a in enumerate(arrays) if a is array]
            loads.append((known[0] if known else len(arrays), first, stride))
            if not known:
                arrays.append(array)
        cuts.append((step, at, pre, stream.lines, half, loads))
    steps = list(links)
    width = arrays[0].shape[1]

    def piece(load, pre, lines, half):
        which, first, stride = load
        if pre == 0:
            return which, first, lines
        return (which, first, 2 * half) if stride == lines else (which, 0, 2 * half // lines * stride)

    fetched = list({piece(load, *c[2:5]) for c in cuts for load in c[5]})
    fetched.sort()

    def body(scalars, reads, writes):
        (place,) = scalars
        for key in fetched:
            reads.start(key[0], key, (pl.ds(key[1], key[2]),))
        for i, (step, at, pre, lines, half, loads) in enumerate(cuts):
            for load in loads:
                reads.wait(load[0], piece(load, pre, lines, half))
            bit = place[0 if step == "side" else step + 1]
            if pre == 0:
                total = add_low(*[reads.buffers[w][first : first + lines, :] for w, first, _ in loads])
                writes.buffers[steps.index(step)][at : at + lines, :] = total
                writes.buffers[len(steps) + i][...] = total
            post = half // lines // max(pre, 1)
            for p in range(pre):
                for out, base, which in ((steps.index(step), at, 1 - bit), (len(steps) + i, 0, bit)):
                    block = (2 * p + which) * post

                    def one(t, block=block, out=out, base=base + p * post * lines, loads=loads, lines=lines):
                        rows = []
                        for w, first, stride in loads:
                            start = pl.multiple_of(first + (block + t) * stride, 16)
                            rows.append(reads.buffers[w][pl.ds(start, lines), :])
                        total = rows[0] if len(rows) == 1 else add_low(*rows)
                        writes.buffers[out][pl.ds(pl.multiple_of(base + t * lines, 16), lines), :] = total

                    if post == 1:
                        one(0)
                    else:
                        pl.loop(0, post)(one)
            writes.start(steps.index(step), i, (pl.ds(at, half),))
            writes.start(len(steps) + i)

    outs = streamed(
        body,
        [bits_of],
        arrays,
        [struct((links[step], width), bf16) for step in steps] + [struct((c[4], width), bf16) for c in cuts],
        [],
        (len(fetched), 2 * len(cuts)),
        "combine",
        4,
        far=False,
    )
    sends = dict(zip(steps, outs))
    for stream, (step, at, _, _, _, _), kept in zip(streams, cuts, outs[len(steps) :]):
        stream.values = [(kept, 0, stream.lines), (step, at, stream.lines)]
    return sends


def exchange(streams, sends, bits):
    arrived = {}
    for step, send in sends.items():
        if step == "side":
            arrived[step] = lax.ppermute(send, "seq", CROSS)
        else:
            arrived[step] = lax.ppermute(send, "dp", [(d, d ^ (1 << step)) for d in range(1 << bits)])
    for stream in streams:
        stream.values = [(arrived.get(v, v) if isinstance(v, (str, int)) else v, *at) for v, *at in stream.values]


def hold(small, streams):
    arrays = arrays_of(streams)
    replace(streams, arrays, advance(small, *arrays))


def arrays_of(streams):
    return list({id(v): v for stream in streams for v, _, _ in stream.values}.values())


def replace(streams, arrays, held):
    where = {id(v): h for v, h in zip(arrays, held)}
    for stream in streams:
        stream.values = [(where[id(v)], *at) for v, *at in stream.values]


def tie(streams, *others):
    arrays = arrays_of(streams)
    replace(streams, arrays, lax.optimization_barrier((*arrays, *others)))


def gather_step(values, at, bits):
    count = 4 << bits

    def partner(device, offset):
        for k in (0, 1):
            if offset >> k & 1 and at + k <= bits:
                device ^= 2 if at + k == 0 else 4 << (at + k - 1)
        return device

    offsets = range(1, 4 if at + 1 <= bits else 2)
    parts = [
        lax.ppermute(values, ("dp", "seq"), [(d, partner(d, offset)) for d in range(count)])
        for offset in offsets
    ]
    return jnp.concatenate([values] + parts, axis=0)


def own_heads(values, half, axis):
    size = values.shape[axis] // 4
    shape = values.shape[:axis] + (2, 2, size) + values.shape[axis + 1 :]
    out = pick(values.reshape(shape), half, axis + 1)
    return out.reshape(values.shape[:axis] + (2 * size,) + values.shape[axis + 1 :])


def after(value, *others):
    return lax.optimization_barrier((value,) + others)[0]


def body(
    embeds,
    lengths,
    drop_in,
    drop_ff,
    positive,
    w_qkv,
    w_out,
    w_up,
    w_down,
    pool_w,
    gains,
    biases,
    up_bias,
    out_grad,
):
    _, _, length, width = drop_in.shape
    n_dp = lax.axis_size("dp")
    bits = n_dp.bit_length() - 1
    seq = lax.axis_index("seq")
    dp = lax.axis_index("dp")
    side, half = seq // 2, seq % 2
    half1 = half.astype(jnp.int32).reshape(1)
    side1 = side.astype(jnp.int32).reshape(1)
    first_side = side == 0
    place_keys = jnp.stack([seq.astype(jnp.int32), lengths[0]])

    token = embeds[0]
    masks_in = (pick(drop_in, side, 0)[0], pick(drop_in, 1 - side, 0)[0])
    kept_send = token * masks_in[1].astype(bf16)
    kept_cross = lax.ppermute(kept_send, "seq", CROSS)
    kept_local = token * masks_in[0].astype(bf16)
    kept_local_pair = lax.ppermute(kept_local, "seq", PAIR)

    w_own, b_own, qkv_local = project_local(half1, kept_local, kept_local_pair, w_qkv, biases)
    kept_cross, w_own = lax.optimization_barrier((kept_cross, w_own))
    kept_cross_pair = lax.ppermute(kept_cross, "seq", PAIR)
    qkv_cross = project_cross(kept_cross, kept_cross_pair, w_own, b_own)
    kept = (kept_local, kept_local_pair, kept_cross, kept_cross_pair)
    rest = jnp.stack([pick(drop_ff, 1 - side, 0)[0].astype(bf16), pick(out_grad, 1 - side, 0)[0]])
    rest = lax.ppermute(after(rest, kept_cross), "seq", CROSS)
    keeps = (pick(drop_ff, side, 0)[0].astype(bf16), rest[0])
    g_parts = (pick(out_grad, side, 0)[0], rest[1])
    w_out4 = w_out.reshape(4, width // 4, width)
    up_bias2 = up_bias[None]

    own, send, lse = attend_forward(place_keys, qkv_local, qkv_cross)
    pair = lax.ppermute(send, "seq", PAIR)
    hidden, slope, h1_low, normal1, inv1, normal2, inv2, mixed_local, mixed_cross = layer_forward(
        half1, own, pair, (kept_local, kept_cross), keeps, w_out4, w_up, w_down, gains, biases, up_bias2
    )

    first = jnp.where(first_side, mixed_local[:1], mixed_cross[:1])
    rel = first
    for at in range(0, bits + 1, 2):
        rel = gather_step(rel, at, bits)
    shift = jnp.stack([side, dp]).astype(jnp.int32)
    positive_col = jnp.broadcast_to(positive[:, None], (n_dp, 128))
    _, _, _, g_cls = loss_parts(shift, rel, pool_w, positive_col)
    mixed_back = lax.ppermute(after(mixed_cross, g_cls), "seq", CROSS)
    mixed_out = jnp.stack(
        [jnp.where(first_side, mixed_local, mixed_back), jnp.where(first_side, mixed_back, mixed_local)]
    )[:, None]

    down_send, down_keep, up_send, up_keep, up_sum, g_attn, g_own, g_send, sums = feed_backward(
        half1,
        side1,
        g_parts,
        g_cls,
        normal2,
        inv2,
        keeps,
        gains,
        hidden,
        w_down,
        w_up,
        slope,
        h1_low,
        normal1,
        inv1,
        w_out4,
    )
    g_attn, g_send, down_send, up_send, mixed_out = lax.optimization_barrier(
        (g_attn, g_send, down_send, up_send, mixed_out)
    )
    g_pair = lax.ppermute(g_send, "seq", PAIR)

    dims = (2,) * bits
    place = (side, dp, bits)
    dp_names = list(range(bits - 1, -1, -1))
    names = ["side"] + dp_names
    low = list(range(1, bits))
    sub = n_dp // GROUPS
    deep = width // n_dp
    cut = width // 4

    rel = jnp.where(half == 0, rel, lax.ppermute(rel, "seq", [(0, 1), (2, 3)]))
    g_pair, rel = lax.optimization_barrier((g_pair, rel))
    tiled = deep % 16 == 0
    down_pair = lax.ppermute(down_send, "seq", PAIR)
    up_pair = lax.ppermute(up_send, "seq", PAIR)
    side_first, dp_first = ["side", 0] + low, [0, "side"] + low
    low_first = low[:1] + ["side", 0] + low[1:]
    if tiled:

        def flat(values):
            return values.reshape(-1, width)

        bits_of = jnp.stack([side] + [(dp >> k) & 1 for k in range(bits)]).astype(jnp.int32)
        most = deep * 2 // 3

        def split(keep, pair, axes, order, rest):
            values = [(flat(keep), 0, deep), (flat(pair), 0, deep)]
            later = [(v, most, stride) for v, _, stride in values]
            return [Tiled(values, axes, most, order), Tiled(later, axes, deep - most, rest)]

        ups = split(up_keep, up_pair, names, side_first, low[:1] + ["side"] + low[1:] + [0])
        downs = split(down_keep, down_pair, dp_names + ["side"], dp_first, low[:1] + [0] + low[1:] + ["side"])
        early = [ups[0], downs[0], ups[1], downs[1]]
        out_send, out_keep = out_backward(half1, own, pair, g_attn)
        outs = (out_keep, lax.ppermute(out_send, "seq", PAIR))
        sends = combine(bits_of, early)
        g_own, g_pair, *held = lax.optimization_barrier((g_own, g_pair, *sends.values()))
        exchange(early, dict(zip(sends, held)), bits)
        grads = attend_backward(place_keys, qkv_local, qkv_cross, own, send, g_own, g_pair, lse)
        tie(early, *grads)
        sends = combine(bits_of, early)
        grads = lax.optimization_barrier((*grads, *sends.values()))[:3]
        exchange(early, sends, bits)
        splits = ((0, deep // 2), (1, deep // 2))
        orders = (side_first, dp_first)
        g_x, g_x_send, sums, *parts = project_backward(
            half1, bits_of, grads, kept, outs, w_own, g_attn, sums, up_sum, splits, deep
        )
        qkv = []
        for (_, take), order, send_part, keep_part in zip(splits, orders, parts[::2], parts[1::2]):
            left = [name for name in names if name != order[0]]
            stream = Tiled([(keep_part, 0, take), (order[0], 0, take)], left, take, order[1:])
            exchange([stream], {order[0]: send_part}, bits)
            qkv.append(stream)
        small = [Rows(g_x, g_x_send, length)]
        advance(small)
        sums = sums.astype(bf16)
        shared = Shared(
            [(sums, 0, 16), (lax.ppermute(sums, "seq", PAIR), 0, 16)], 16, low[:1] + ["side", 0] + low[1:]
        )
        tie(early, *parts)
        sends = combine(bits_of, early + [shared])
        exchange(early + [shared], sends, bits)
        streams = qkv + early + [shared]
    else:
        sub = n_dp // GROUPS

        def turned(values):
            values = values.reshape(GROUPS, 2, width // 8, 2, sub, -1)
            return values.transpose(0, 4, 1, 3, 2, 5)

        down = Halving(
            [turned(down_keep), turned(down_pair)], dims + (2, cut, -1), dp_names + ["side"], dp_first, place
        )
        up = Halving([up_keep, up_pair], (2,) + dims + (deep, -1), names, side_first, place)
        out_send, out_keep = out_backward(half1, own, pair, g_attn)
        outs = (out_keep, lax.ppermute(out_send, "seq", PAIR))
        g_own, g_pair = advance([up, down], g_own, g_pair)
        grads = attend_backward(place_keys, qkv_local, qkv_cross, own, send, g_own, g_pair, lse)
        g_x, g_x_send, sums, part = project_backward(
            half1, place_keys, grads, kept, outs, w_own, g_attn, sums, up_sum, (), 0
        )
        qkv = [Halving([part], (2,) + dims + (deep, width), names, side_first, place)]
        streams = qkv + [up, down]
        small = [Summing(sums, bits), Rows(g_x, g_x_send, length)]
    while any(stream.order for stream in streams + small):
        if tiled:
            hold(small, streams)
            if any(stream.order for stream in streams):
                sends = combine(bits_of, streams)
                exchange(streams, sends, bits)
        else:
            advance(streams + small)
    values, cls_all, g_pre, _ = loss_parts(shift, rel, pool_w, positive_col)
    pool_rows, pool_cols = width // n_dp, width // 4
    grad_pool = t_dot(
        lax.dynamic_slice_in_dim(cls_all, dp * pool_rows, pool_rows, 1),
        lax.dynamic_slice_in_dim(g_pre, seq * pool_cols, pool_cols, 1),
    )
    total = shared.total().astype(f32) if tiled else small[0].values
    g_x, g_x_cross = small[-1].values
    if tiled:
        grad_up = jnp.concatenate([stream.total() for stream in ups], axis=0).astype(f32)
        grad_down = jnp.concatenate([stream.total() for stream in downs], axis=0)
    else:
        grad_up = up.total().astype(f32)
        grad_down = down.total()
    if tiled:
        grad_down = grad_down.reshape(deep, 2, -1).swapaxes(0, 1).reshape(cut, -1)
    grad_down = grad_down.astype(f32).T
    sum_qkv = jnp.concatenate([stream.total() for stream in qkv], axis=0)
    grad_out = sum_qkv[:, 3 * cut :].astype(f32)
    three = sum_qkv[:, : 3 * cut].reshape(deep, 3, cut)
    swapped = lax.ppermute(jnp.where(half == 0, three[:, 2], three[:, 0]), "seq", PAIR)
    left = jnp.where(half == 0, three[:, 0], three[:, 1])
    right = jnp.where(half == 0, three[:, 1], three[:, 2])
    grad_qkv = jnp.concatenate([left, swapped, right], axis=1).astype(f32)
    embeds_grad = (g_x * masks_in[0].astype(f32) + g_x_cross.astype(f32) * masks_in[1].astype(f32)) * inv_keep
    return (
        mixed_out,
        embeds_grad[None],
        grad_qkv,
        grad_out,
        grad_up,
        grad_down,
        grad_pool,
        total[0:2],
        total[2:7],
        total[7],
        total[8 : 8 + up_bias.shape[0] // width].reshape(-1),
        values[0, 0],
        values[1, 0],
        values[2, 0],
    )


def solution(mesh):
    tokens = P(None, "dp", "seq", None)
    placed = (P("dp", "seq", None), P("dp"), tokens, tokens) + (P(),) * 9 + (tokens,)
    weight = P("dp", "seq")
    return jax.shard_map(
        body,
        mesh=mesh,
        in_specs=placed,
        out_specs=(tokens, P("dp", "seq", None)) + (weight,) * 5 + (P(),) * 7,
        check_vma=False,
    )
```

```python
import functools
import math

import jax
import jax.numpy as jnp
from jax import lax
from jax.experimental import pallas as pl
from jax.experimental.pallas import tpu as pltpu
from jax.sharding import PartitionSpec as P

HEAD = 64
keep_rate = 0.9
inv_keep = 1.0 / keep_rate
highest = lax.Precision.HIGHEST
f32 = jnp.float32
bf16 = jnp.bfloat16

CROSS = [(i, i ^ 2) for i in range(4)]
PAIR = [(i, i ^ 1) for i in range(4)]
GROUPS = 8


def cost(time):
    return pl.CostEstimate(flops=time * 2_000_000_000, bytes_accessed=1 << 20, transcendentals=0)

CHUNK = 768


def dot(a, b):
    return jnp.dot(a, b, preferred_element_type=f32)


def dot_t(a, b):
    return lax.dot_general(a, b, (((1,), (1,)), ((), ())), preferred_element_type=f32)


def t_dot(a, b):
    return lax.dot_general(a, b, (((0,), (0,)), ((), ())), preferred_element_type=f32)


def whole(shape):
    return pl.BlockSpec(shape, lambda *_: (0,) * len(shape))


def struct(shape, dtype):
    return jax.ShapeDtypeStruct(shape, dtype)


def hbm(x):
    return pltpu.with_memory_space_constraint(x, pltpu.HBM)


def params(limit):
    return pltpu.CompilerParams(vmem_limit_bytes=limit << 20)


ALL = (slice(None),)


class Stream:
    def __init__(self, refs, buffers, sems, out):
        self.refs, self.buffers, self.sems, self.out = refs, buffers, sems, out
        self.count, self.copies = 0, {}

    def start(self, which, key=0, at=ALL):
        ref, buffer = self.refs[which].at[at], self.buffers[which].at[at]
        source, target = (buffer, ref) if self.out else (ref, buffer)
        copy = pltpu.make_async_copy(source, target, self.sems.at[self.count])
        copy.start()
        self.count += 1
        self.copies[which, key] = copy

    def wait(self, which, key=0):
        copy = self.copies.pop((which, key), None)
        if copy is not None:
            copy.wait()
        return self.buffers[which]

    def drain(self):
        for which, key in list(self.copies):
            self.wait(which, key)


def streamed(body, scalars, ins, outs, scratch, copies, name, time, limit=56, far=True):
    n_s, n_i, n_o = len(scalars), len(ins), len(outs)

    def kernel(*refs):
        cuts = [n_s, n_i, n_o, n_i, n_o, len(scratch), 1, 1]
        parts, at = [], 0
        for cut in cuts:
            parts.append(refs[at : at + cut])
            at += cut
        reads = Stream(parts[1], parts[3], parts[6][0], False)
        writes = Stream(parts[2], parts[4], parts[7][0], True)
        body([r[0] if r.shape[0] == 1 else r for r in parts[0]], reads, writes, *parts[5])
        reads.drain()
        writes.drain()

    smem, home = pl.BlockSpec(memory_space=pltpu.SMEM), pl.BlockSpec(memory_space=pltpu.HBM)
    if far:
        ins = [hbm(x) for x in ins]
    return pl.pallas_call(
        kernel,
        in_specs=[smem] * n_s + [home if far else pl.BlockSpec(memory_space=pl.ANY)] * n_i,
        out_specs=[home] * n_o,
        out_shape=[pltpu.HBM(o.shape, o.dtype) for o in outs],
        scratch_shapes=[pltpu.VMEM(x.shape, x.dtype) for x in list(ins) + list(outs)]
        + list(scratch)
        + [pltpu.SemaphoreType.DMA((copies[0],)), pltpu.SemaphoreType.DMA((copies[1],))],
        compiler_params=params(limit),
        cost_estimate=cost(time),
        name=name,
    )(*scalars, *ins)


def one_head(block, head, extra):
    lane = lax.broadcasted_iota(jnp.int32, block.shape, 1)
    mine = (lane >= HEAD) if head else (lane < HEAD)
    out = jnp.where(mine, block, jnp.zeros_like(block))
    if extra is not None:
        out = jnp.where(lane == (0 if head else HEAD), extra, out)
    return out


def key_mask(place_ref, rows):
    quarter = rows // 4
    parts = []
    for b in range(4):
        at = lax.broadcasted_iota(jnp.int32, (quarter, 128), 0) + (place_ref[0] ^ b) * quarter
        parts.append(jnp.where(at < place_ref[1], 0.0, -1e30).astype(bf16))
    return jnp.concatenate(parts, axis=0)


def forward_kernel(place_ref, ql_ref, qc_ref, kl_ref, kc_ref, vl_ref, vc_ref, own_ref, send_ref, lse_ref):
    key = jnp.concatenate([kl_ref[...], kc_ref[...]], axis=0)
    mask = key_mask(place_ref, key.shape[0])
    keys = [one_head(key, h, mask) for h in (0, 1)]
    value_t = jnp.concatenate([vl_ref[...], vc_ref[...]], axis=0).T
    one = jnp.ones((), bf16)
    rows = ql_ref.shape[0]
    cut = rows // 2
    units = [(part, c, h) for part in (0, 1) for c in (0, 1) for h in (0, 1)]
    scores, weights = [], []
    for part, c, h in units:
        q = (ql_ref, qc_ref)[part][c * cut : (c + 1) * cut, :] * jnp.asarray(1.0 / math.sqrt(HEAD), bf16)
        scores.append(dot_t(keys[h], one_head(q, h, one)))
    for (part, c, h), s in zip(units, scores):
        top = jnp.max(s, axis=0, keepdims=True)
        p = jnp.exp(s - top)
        total = jnp.sum(p, axis=0, keepdims=True)
        start = part * rows + c * cut
        lse_ref[0, h : h + 1, start : start + cut] = top + jnp.log(total)
        weights.append((p.astype(bf16), total))
    outs = [
        dot(value_t[HEAD * h : HEAD * (h + 1), :], p) * (1.0 / total)
        for (part, c, h), (p, total) in zip(units, weights)
    ]
    for i in range(0, len(units), 2):
        part, c, _ = units[i]
        out = jnp.concatenate(outs[i : i + 2], axis=0).T.astype(bf16)
        (own_ref, send_ref)[c][part * cut : (part + 1) * cut, :] = out


def attend_forward(place, qkv_local, qkv_cross):
    rows, pairs = qkv_local.shape[0], qkv_local.shape[1] // 384

    def block(offset):
        return [pl.BlockSpec((rows, 128), lambda i: (0, i + offset))] * 2

    return pl.pallas_call(
        forward_kernel,
        grid=(pairs,),
        in_specs=[pl.BlockSpec(memory_space=pltpu.SMEM)] + block(0) + block(pairs) + block(2 * pairs),
        out_specs=block(0) + [pl.BlockSpec((1, 2, 2 * rows), lambda i: (i, 0, 0))],
        out_shape=[
            pltpu.HBM((rows, pairs * 128), bf16),
            pltpu.HBM((rows, pairs * 128), bf16),
            pltpu.HBM((pairs, 2, 2 * rows), f32),
        ],
        compiler_params=params(56),
        cost_estimate=cost(13),
        name="attend_forward",
    )(place, *(hbm(qkv_local), hbm(qkv_cross)) * 3)


def backward_kernel(
    place_ref,
    ql_ref,
    qc_ref,
    kl_ref,
    kc_ref,
    vl_ref,
    vc_ref,
    o0,
    o1,
    g0,
    g1,
    lse_ref,
    dq_ref,
    dk_ref,
    dv_ref,
    swap_ref,
    dk_acc,
    dv_acc,
):
    chunk = ql_ref.shape[0]
    scale = 1.0 / math.sqrt(HEAD)
    key = jnp.concatenate([kl_ref[...], kc_ref[...]], axis=0)
    mask = key_mask(place_ref, key.shape[0])
    keys = [one_head(key, h, mask) for h in (0, 1)]
    key_t = key.T
    value = jnp.concatenate([vl_ref[...], vc_ref[...]], axis=0)
    one = jnp.ones((), bf16)
    for c, q_ref in enumerate((ql_ref, qc_ref)):
        at = slice(c * chunk, (c + 1) * chunk)
        half = slice(c * chunk // 2, (c + 1) * chunk // 2)
        out = jnp.concatenate([o0[half, :], o1[half, :]], axis=0)
        do = jnp.concatenate([g0[half, :], g1[half, :]], axis=0)
        q = q_ref[...] * jnp.asarray(scale, bf16)
        prod_t = (do.astype(f32) * out.astype(f32)).T
        ps, dss, dos, qs, dq_t = [], [], [], [], []
        for h in (0, 1):
            rows = slice(HEAD * h, HEAD * (h + 1))
            s = dot_t(keys[h], one_head(q, h, one))
            p = jnp.exp(s - lse_ref[0, h : h + 1, at])
            do_h = one_head(do, h, None)
            dp = dot_t(value, do_h)
            delta = jnp.sum(prod_t[rows, :], axis=0, keepdims=True)
            ds = (p * (dp - delta)).astype(bf16)
            ps.append(p.astype(bf16))
            dss.append(ds)
            dos.append(do_h)
            qs.append(one_head(q, h, None))
            dq_t.append(dot(key_t[rows, :], ds))
        dv_c = dot(jnp.concatenate(ps, 1), jnp.concatenate(dos, 0))
        dk_c = dot(jnp.concatenate(dss, 1), jnp.concatenate(qs, 0))
        if c == 0:
            dv_acc[...] = dv_c
            dk_acc[...] = dk_c
        else:
            dv_ref[...] = (dv_acc[...] + dv_c).astype(bf16)
            dk_ref[...] = (dk_acc[...] + dk_c).astype(bf16)
        dq_ref[at, :] = (jnp.concatenate(dq_t, 0).T * scale).astype(bf16)

    step = pl.program_id(0)
    even = place_ref[0] % 2 == 0
    lane = lax.broadcasted_iota(jnp.int32, dq_ref.shape, 1) + 128 * step
    early = jnp.where(even, dk_ref[...], dq_ref[...])
    late = jnp.where(even, dv_ref[...], dk_ref[...])
    swap_ref[...] = jnp.where(lane < 64 * pl.num_programs(0), early, late)


def attend_backward(place, qkv_local, qkv_cross, own, send, g_own, g_pair, lse):
    rows, pairs = qkv_local.shape[0], qkv_local.shape[1] // 384

    def block(offset):
        return [pl.BlockSpec((rows, 128), lambda i: (0, i + offset))] * 2

    return pl.pallas_call(
        backward_kernel,
        grid=(pairs,),
        in_specs=[pl.BlockSpec(memory_space=pltpu.SMEM)]
        + block(0)
        + block(pairs)
        + block(2 * pairs)
        + block(0) * 2
        + [pl.BlockSpec((1, 2, 2 * rows), lambda i: (i, 0, 0))],
        out_specs=[pl.BlockSpec((2 * rows, 128), lambda i: (0, i))] * 4,
        out_shape=[pltpu.HBM((2 * rows, pairs * 128), bf16)] * 4,
        scratch_shapes=[pltpu.VMEM((2 * rows, 128), f32)] * 2,
        compiler_params=params(56),
        cost_estimate=cost(20),
        name="attend_backward",
    )(place, *[hbm(x) for x in (qkv_local, qkv_cross) * 3 + (own, send, g_own, g_pair, lse)])


def project_backward(half, bits_of, grads, swapped, kept, outs, w_own, g_attn, sums, up_sum, splits, lines):
    rows, width = g_attn.shape
    n, narrow = grads[0].shape
    quarter = n // 4
    cut = width // 4
    many = up_sum.shape[1] // width
    GRADS, KEPT, OUTS, W_OWN, G_ATTN, SUMS_IN, UP_SUM, SWAPPED = 0, 3, 7, 9, 10, 11, 12, 13
    OWN, SEND, SUMS, FIRST = range(4)
    if lines:
        weights = [(width // lines * take, width) for _, take in splits]
        results = [struct(shape, bf16) for shape in weights for _ in (0, 1)]
    else:
        results = [struct((2, width, width), bf16)]

    def body(scalars, reads, writes):
        half, bits_ref = scalars
        for which in (KEPT, KEPT + 1, KEPT + 2, KEPT + 3, 0, 1, 2, SWAPPED, OUTS, OUTS + 1, W_OWN, G_ATTN, SUMS_IN, UP_SUM):
            reads.start(which)
        buf = writes.buffers
        x = jnp.concatenate([reads.wait(KEPT + i)[...] for i in range(4)], axis=0)
        x_t = (x.astype(f32) * inv_keep).astype(bf16).T
        for which in (0, 1, 2, SWAPPED, OUTS, OUTS + 1):
            reads.wait(which)
        q, k, v = (reads.buffers[GRADS + i] for i in range(3))
        came = jnp.concatenate(
            [reads.buffers[SWAPPED][b * quarter : (b + 1) * quarter, :] for b in (1, 0, 3, 2)], axis=0
        )
        even = half == 0
        columns = (
            jnp.concatenate(
                [
                    jnp.where(even, q[:, :cut], q[:, cut:]),
                    came[:, :cut],
                    jnp.where(even, q[:, cut:], k[:, :cut]),
                ],
                axis=1,
            ),
            jnp.concatenate(
                [
                    jnp.where(even, k[:, cut:], v[:, :cut]),
                    came[:, cut:],
                    jnp.where(even, v[:, :cut], v[:, cut:]),
                ],
                axis=1,
            ),
        )
        for side in (0, 1):
            out = add_low(reads.buffers[OUTS][side, :, :cut], reads.buffers[OUTS + 1][side, :, :cut])
            part = jnp.concatenate([dot(x_t, columns[side]).astype(bf16), out], axis=1)
            if not lines:
                buf[FIRST][side] = part
                continue
            blocks = width // lines
            done = 0
            for i, (bit, take) in enumerate(splits):
                block = part.reshape(blocks, lines, width)[:, done : done + take]
                done += take
                target, kept = buf[FIRST + 2 * i], buf[FIRST + 2 * i + 1]
                if bit == 0:
                    block = block.reshape(blocks * take, width)

                    @pl.when(bits_ref[0] == side)
                    def _(block=block, kept=kept):
                        kept[...] = block

                    @pl.when(bits_ref[0] != side)
                    def _(block=block, target=target):
                        target[...] = block

                    continue
                post = 1 << bit - 1
                block = block.reshape(blocks // (2 * post), 2, post * take, width)
                size = blocks * take // 2
                spot = slice(side * size, (side + 1) * size)
                for value in (0, 1):
                    piece = block[:, value].reshape(size, width)

                    @pl.when(bits_ref[bit] == value)
                    def _(piece=piece, kept=kept, spot=spot):
                        kept[spot, :] = piece

                    @pl.when(bits_ref[bit] != value)
                    def _(piece=piece, target=target, spot=spot):
                        target[spot, :] = piece

        for i in range(len(results)):
            writes.start(FIRST + i)
        for which in (W_OWN, G_ATTN, SUMS_IN, UP_SUM):
            reads.wait(which)
        w = reads.buffers[W_OWN]
        for which, ref in ((1, SEND), (0, OWN)):
            total = None
            for i in range(3):
                g = reads.buffers[GRADS + i]
                g = jnp.concatenate(
                    [g[(which + b) * quarter : (which + b + 1) * quarter, :] for b in (0, 2)], axis=0
                )
                part = dot_t(g, w[:, i * narrow : (i + 1) * narrow])
                total = part if total is None else total + part
            if which == 0:
                total = total + reads.buffers[G_ATTN][...].astype(f32)
            buf[ref][...] = total.astype(bf16)
            writes.start(ref)
        buf[SUMS][0:8, :] = reads.buffers[SUMS_IN][...]
        tail = [reads.buffers[UP_SUM][:, i * width : (i + 1) * width] for i in range(many)]
        buf[SUMS][8:, :] = jnp.concatenate(tail + [jnp.zeros((8 - many, width), f32)], axis=0)
        for line, which in ((2, 0), (3, 2)):
            total = jnp.sum(reads.buffers[which][...].astype(f32), axis=0, keepdims=True)
            for b in (0, 1):
                block = total[:, b * cut : (b + 1) * cut]
                for who in (0, 1):
                    at = (2 * b + who) * cut
                    buf[SUMS][line : line + 1, at : at + cut] = jnp.where(half == who, block, jnp.zeros_like(block))
        writes.start(SUMS)

    return streamed(
        body,
        [half, bits_of],
        [*grads, *kept, *outs, w_own, g_attn, sums, up_sum, swapped],
        [struct((rows, width), bf16), struct((rows, width), bf16), struct((16, width), f32)] + results,
        [],
        (14, 3 + len(results)),
        "project_backward",
        10,
    )


def project_local(half, own, pair, w_qkv, biases):
    rows, width = own.shape
    cut = width // 4

    def body(scalars, reads, writes, bias):
        (half,) = scalars
        for which in (2, 3, 0, 1):
            reads.start(which)
        w, b = reads.wait(2), reads.wait(3)
        w_own, b_own = writes.buffers[0], writes.buffers[1]
        for who in (0, 1):

            @pl.when(half == who)
            def _(who=who):
                for kind in range(3):
                    base = kind * width
                    lines = [slice(base + (who + 2 * i) * cut, base + (who + 2 * i + 1) * cut) for i in (0, 1)]
                    target = slice(kind * 2 * cut, (kind + 1) * 2 * cut)
                    w_own[:, target] = jnp.concatenate([w[:, line] for line in lines], axis=1)
                    if kind == 1:
                        b_own[:, target] = jnp.zeros((8, 2 * cut), f32)
                    else:
                        row = b[kind // 2 : kind // 2 + 1, :]
                        row = jnp.concatenate([row[:, line.start - base : line.stop - base] for line in lines], axis=1)
                        b_own[:, target] = jnp.broadcast_to(row, (8, 2 * cut))

        writes.start(0)
        writes.start(1)
        x = jnp.concatenate([reads.wait(0)[...], reads.wait(1)[...]], axis=0)
        x = (x.astype(f32) * inv_keep).astype(bf16)
        writes.buffers[2][...] = (dot(x, w_own[...]) + b_own[0:1, :]).astype(bf16)
        writes.start(2)

    return streamed(
        body,
        [half],
        [own, pair, w_qkv, biases],
        [struct((width, 6 * cut), bf16), struct((8, 6 * cut), f32), struct((2 * rows, 6 * cut), bf16)],
        [pltpu.VMEM((8, 128), f32)],
        (4, 3),
        "project_local",
        5,
    )


def project_cross(own, pair, w_own, b_own):
    rows = own.shape[0]

    def body(scalars, reads, writes):
        for which in range(4):
            reads.start(which)
        x = jnp.concatenate([reads.wait(0)[...], reads.wait(1)[...]], axis=0)
        x = (x.astype(f32) * inv_keep).astype(bf16)
        w, b = reads.wait(2), reads.wait(3)
        writes.buffers[0][...] = (dot(x, w[...]) + b[0:1, :]).astype(bf16)
        writes.start(0)

    return streamed(
        body,
        [],
        [own, pair, w_own, b_own],
        [struct((2 * rows, w_own.shape[1]), bf16)],
        [],
        (4, 1),
        "project_cross",
        4,
    )[0]


def norm_parts(values):
    mean = jnp.mean(values, axis=-1, keepdims=True)
    centred = values - mean
    inv = lax.rsqrt(jnp.mean(centred * centred, axis=-1, keepdims=True) + 1e-06)
    return centred * inv, inv


def norm_back(g, normal, inv, gain):
    a = g * gain
    return (
        a - jnp.mean(a, axis=-1, keepdims=True) - normal * jnp.mean(a * normal, axis=-1, keepdims=True)
    ) * inv


def gelu_parts(u):
    e = jnp.exp(-0.5 * u * u)
    t = 1.0 / (1.0 + (0.3275911 / math.sqrt(2.0)) * jnp.abs(u))
    poly = 0.5 * 1.061405429
    for a in (-1.453152027, 1.421413741, -0.284496736, 0.254829592):
        poly = poly * t + 0.5 * a
    tail = poly * t * e
    phi = jnp.where(u < 0, tail, 1.0 - tail)
    return u * phi, phi + u * e * (1.0 / math.sqrt(2.0 * math.pi))


def layer_forward(half, own, pair, kept, keep, w_out, w_up, w_down, gains, biases, up_bias):
    rows, width = kept[0].shape
    hid = w_up.shape[1]
    parts = hid // width
    tile = (rows, width)
    full = (2 * rows, width)
    cuts = [slice(c * width, (c + 1) * width) for c in range(parts)]
    OWN, PAIR_, KEPT, KEEP, W_OUT, W_UP, W_DOWN, GAINS, BIASES, UP_BIAS = 0, 1, 2, 4, 6, 7, 8, 9, 10, 11
    HIDDEN, SLOPE, H1_LOW, NORMAL1, INV1, NORMAL2, INV2, MIXED = range(8)

    def body(scalars, reads, writes, h1):
        (half,) = scalars
        for which in (OWN, PAIR_, W_OUT, BIASES, KEPT, KEPT + 1, GAINS, UP_BIAS):
            reads.start(which)
        def fetch(c):
            reads.start(W_UP, c, (slice(None), cuts[c]))
            reads.start(W_DOWN, c, (cuts[c],))

        fetch(0)
        own, pair, w_out = (reads.wait(w)[...] for w in (OWN, PAIR_, W_OUT))
        for c in range(1, parts):
            fetch(c)
        reads.start(KEEP)
        reads.start(KEEP + 1)
        biases = reads.wait(BIASES)
        half = jnp.int32(half)

        def mine(who):
            w = reads.buffers[W_OUT]
            return jnp.concatenate([w[who], w[who + 2]], axis=0)

        attn = dot(own, mine(half)) + dot(pair, mine(1 - half)) + biases[2:3, :]
        xin = jnp.concatenate([reads.wait(KEPT)[...], reads.wait(KEPT + 1)[...]], axis=0)
        normal, inv = norm_parts(xin.astype(f32) * inv_keep + attn)
        gains = reads.wait(GAINS)
        buf = writes.buffers
        buf[NORMAL1][...] = normal.astype(bf16)
        buf[INV1][...] = jnp.broadcast_to(inv, buf[INV1].shape)
        h1[...] = normal * gains[0:1, :] + biases[3:4, :]
        h1_low = h1[...].astype(bf16)
        buf[H1_LOW][...] = h1_low
        for which in (NORMAL1, INV1, H1_LOW):
            writes.start(which)
        up_bias = reads.wait(UP_BIAS)
        reads.wait(W_UP, 0)
        reads.wait(W_DOWN, 0)
        ff = biases[4:5, :]
        for c, at in enumerate(cuts):
            if c == 1:
                for k in range(1, parts):
                    reads.wait(W_UP, k)
                    reads.wait(W_DOWN, k)
            up = dot(h1_low, reads.buffers[W_UP][:, at]) + up_bias[:, at]
            hidden, slope = gelu_parts(up)
            hidden = hidden.astype(bf16)
            buf[HIDDEN][:, at] = hidden
            buf[SLOPE][:, at] = slope.astype(bf16)
            writes.start(HIDDEN, c, (slice(None), at))
            writes.start(SLOPE, c, (slice(None), at))
            ff = ff + dot(hidden, reads.buffers[W_DOWN][at, :])
        keep = jnp.concatenate([reads.wait(KEEP)[...], reads.wait(KEEP + 1)[...]], axis=0)
        normal, inv = norm_parts(h1[...] + ff * (keep.astype(f32) * inv_keep))
        mixed = (normal * gains[1:2, :] + biases[5:6, :]).astype(bf16)
        buf[MIXED][...] = mixed[:rows]
        buf[MIXED + 1][...] = mixed[rows:]
        writes.start(MIXED)
        writes.start(MIXED + 1)
        buf[NORMAL2][...] = normal.astype(bf16)
        buf[INV2][...] = jnp.broadcast_to(inv, buf[INV2].shape)
        writes.start(NORMAL2)
        writes.start(INV2)

    return streamed(
        body,
        [half],
        [own, pair, *kept, *keep, w_out, w_up, w_down, gains, biases, up_bias],
        [
            struct((2 * rows, hid), bf16),
            struct((2 * rows, hid), bf16),
            struct(full, bf16),
            struct(full, bf16),
            struct((2 * rows, 128), f32),
            struct(full, bf16),
            struct((2 * rows, 128), f32),
            struct(tile, bf16),
            struct(tile, bf16),
        ],
        [pltpu.VMEM(full, f32)],
        (10 + 2 * parts, 7 + 2 * parts),
        "layer_forward",
        16,
    )


def loss_kernel(shift_ref, cls_ref, pool_ref, positive_ref, values_ref, order_ref, g_pre_ref, g_cls_ref):
    rows = cls_ref.shape[0]
    n = rows // 2
    row = lax.broadcasted_iota(jnp.int32, (rows, rows), 0)
    column = lax.broadcasted_iota(jnp.int32, (rows, rows), 1)
    view, sentence = (column % 2) ^ shift_ref[0], (column // 2) ^ shift_ref[1]
    cls = dot((row == view * n + sentence).astype(bf16), cls_ref[...]).astype(bf16)
    order_ref[...] = cls
    pooled = jnp.tanh(dot(cls, pool_ref[...]))
    inv = lax.rsqrt(jnp.sum(pooled * pooled, axis=-1, keepdims=True) + 1e-06)
    unit = pooled * inv
    anchors, candidates = unit[:n], unit[n:]

    def exact(a, b, dims):
        return lax.dot_general(a, b, (dims, ((), ())), precision=highest, preferred_element_type=f32)

    logits = exact(anchors, candidates, ((1,), (1,))) / 0.05
    mine = lax.broadcasted_iota(jnp.int32, (n, n), 0)
    other = lax.broadcasted_iota(jnp.int32, (n, n), 1)
    picked = (other == positive_ref[:, 0:1]).astype(f32)
    top = jnp.max(logits, axis=1, keepdims=True)
    expo = jnp.exp(logits - top)
    total = jnp.sum(expo, axis=1, keepdims=True)
    target = jnp.sum(logits * picked, axis=1, keepdims=True)
    loss = jnp.mean(jnp.log(total) + top - target, axis=0, keepdims=True)
    matched = exact(picked, candidates, ((1,), (0,)))
    offset = anchors - matched
    alignment = jnp.mean(jnp.sum(offset * offset, axis=-1, keepdims=True), axis=0, keepdims=True)
    inner = exact(anchors, anchors, ((1,), (1,)))
    norms = jnp.sum(anchors * anchors, axis=-1, keepdims=True)
    norms_row = jnp.sum(jnp.where(mine == other, norms, 0.0), axis=0, keepdims=True)
    dist = norms + norms_row - 2.0 * inner
    near = jnp.where(mine != other, jnp.exp(-2.0 * dist), 0.0)
    near = jnp.sum(jnp.sum(near, axis=1, keepdims=True), axis=0, keepdims=True)
    uniformity = jnp.log(near / (n * (n - 1)))
    line = lax.broadcasted_iota(jnp.int32, values_ref.shape, 0)
    values_ref[...] = jnp.where(line == 0, loss, jnp.where(line == 1, alignment, uniformity))
    g_logits = (expo / total - picked) * (1.0 / (0.05 * n))
    g_unit = jnp.concatenate(
        [exact(g_logits, candidates, ((1,), (0,))), exact(g_logits, anchors, ((0,), (0,)))], axis=0
    )
    g_pooled = inv * (g_unit - unit * jnp.sum(g_unit * unit, axis=-1, keepdims=True))
    g_pre = (g_pooled * (1.0 - pooled * pooled)).astype(bf16)
    g_pre_ref[...] = g_pre
    line = lax.broadcasted_iota(jnp.int32, g_pre.shape, 0)
    mine = jnp.where(line == shift_ref[0] * n + shift_ref[1], g_pre.astype(f32), 0.0)
    mine = jnp.broadcast_to(jnp.sum(mine, axis=0, keepdims=True), (8, mine.shape[1])).astype(bf16)
    g_cls_ref[...] = dot_t(mine, pool_ref[...])


def loss_parts(shift, cls, pool_w, positive):
    rows, width = cls.shape
    return pl.pallas_call(
        loss_kernel,
        in_specs=[pl.BlockSpec(memory_space=pltpu.SMEM)] + [pl.BlockSpec(memory_space=pltpu.VMEM)] * 3,
        out_shape=[
            struct((8, 128), f32),
            struct((rows, width), bf16),
            struct((rows, width), bf16),
            struct((8, width), f32),
        ],
        compiler_params=params(16),
        cost_estimate=cost(2),
        name="contrast",
    )(shift, cls, pool_w, positive)


def feed_backward(
    half, side, g_parts, g_cls, normal2, inv2, keeps, gains, hidden, w_down, w_up, slope, h1_low, normal1, inv1, w_out
):
    rows, width = h1_low.shape
    hid = hidden.shape[1]
    wide = hid // GROUPS
    chunk = hid // 4
    deep = width // 8
    full = (rows, width)
    down = struct((GROUPS, 2, deep, 2 * wide), bf16)
    up = struct((2, width, chunk), bf16)
    narrow = struct((rows, width // 2), bf16)
    G, G_CLS, NORMAL2, INV2, KEEP, GAINS, HIDDEN, W_DOWN, W_UP, SLOPE, H1, NORMAL1, INV1, W_OUT = (
        0, 2, 3, 4, 5, 7, 8, 9, 10, 11, 12, 13, 14, 15,
    )
    D_SEND, D_KEEP, U_SEND, U_KEEP, UP_SUM, G_ATTN, OWN, PAIR_, SUMS = range(9)
    cuts = [slice(i * wide, (i + 2) * wide) for i in range(0, GROUPS, 2)]

    def body(scalars, reads, writes, turned, turned_h1, g_h2_ref, g_ff_ref):
        half, cls_side = scalars
        steps = []
        for who, ref in ((1 - half, U_SEND), (half, U_KEEP)):
            for b in (0, 1):
                steps.append((ref, b, pl.ds(pl.multiple_of((2 * b + who) * chunk, chunk), chunk)))
        first = (G, G + 1, G_CLS, NORMAL2, INV2, GAINS, KEEP, KEEP + 1)
        for which in first:
            reads.start(which)
        reads.start(HIDDEN)
        reads.start(H1)
        for which in first:
            reads.wait(which)
        for c, (ref, b, at) in enumerate(steps):
            reads.start(W_DOWN, c, (at,))
            reads.start(SLOPE, c, (slice(None), at))
            reads.start(W_UP, c, (slice(None), at))
        for which in (NORMAL1, INV1, W_OUT):
            reads.start(which)
        got, buf = reads.buffers, writes.buffers
        g = jnp.concatenate([got[G][...], got[G + 1][...]], axis=0).astype(f32)
        place = jnp.where(half == 0, cls_side * (rows // 2), rows)
        here = lax.broadcasted_iota(jnp.int32, g.shape, 0) == place
        g = g + jnp.where(here, got[G_CLS][0:1, :], 0.0)
        normal = got[NORMAL2][...].astype(f32)
        g_h2 = norm_back(g, normal, got[INV2][:, 0:1], got[GAINS][1:2, :])
        keep = jnp.concatenate([got[KEEP][...], got[KEEP + 1][...]], axis=0)
        g_ff = (g_h2 * (keep.astype(f32) * inv_keep)).astype(bf16)
        g_h2_ref[...] = g_h2
        g_ff_ref[...] = g_ff
        second = [jnp.sum(v, axis=0, keepdims=True) for v in (g * normal, g, g_ff.astype(f32))]
        turned[...] = g_ff.T.reshape(turned.shape)
        reads.wait(HIDDEN)
        reads.wait(H1)
        for who, ref in ((1 - half, D_SEND), (half, D_KEEP)):
            lhs = jnp.concatenate([turned[who], turned[who + 2]], axis=0)
            for c, at in enumerate(cuts):
                out = dot(lhs, got[HIDDEN][:, at]).astype(bf16)
                for i in (0, 1):
                    for s in (0, 1):
                        lines = out[2 * s * deep : 2 * (s + 1) * deep, i * wide : (i + 1) * wide]
                        buf[ref][2 * c + i, s] = jnp.concatenate([lines[:deep], lines[deep:]], axis=1)
            writes.start(ref)
        turned_h1[...] = got[H1][...].T
        for c in range(4):
            for which in (W_DOWN, SLOPE, W_UP):
                reads.wait(which, c)
        g = g_h2_ref[...]
        for c, (ref, b, at) in enumerate(steps):
            g_up = (dot_t(g_ff_ref[...], got[W_DOWN][at, :]) * got[SLOPE][:, at].astype(f32)).astype(bf16)
            buf[UP_SUM][:, at] = jnp.sum(g_up.astype(f32), axis=0, keepdims=True)
            buf[ref][b] = dot(turned_h1[...], g_up).astype(bf16)
            writes.start(ref, b, (b,))
            g = g + dot_t(g_up, got[W_UP][:, at])
        writes.start(UP_SUM)
        for which in (NORMAL1, INV1, W_OUT):
            reads.wait(which)
        normal = got[NORMAL1][...].astype(f32)
        g_attn = norm_back(g, normal, got[INV1][:, 0:1], got[GAINS][0:1, :]).astype(bf16)
        for who, ref in ((1 - half, PAIR_), (half, OWN)):
            w = jnp.concatenate([got[W_OUT][who], got[W_OUT][who + 2]], axis=0)
            buf[ref][...] = dot_t(g_attn, w).astype(bf16)
            writes.start(ref)
        buf[G_ATTN][...] = g_attn
        writes.start(G_ATTN)
        first = [jnp.sum(v, axis=0, keepdims=True) for v in (g * normal, g, g_attn.astype(f32))]
        zero = jnp.zeros((2, width), f32)
        buf[SUMS][...] = jnp.concatenate(
            [first[0], second[0], zero, first[1], second[2], second[1], first[2]], axis=0
        )
        writes.start(SUMS)

    return streamed(
        body,
        [half, side],
        [
            *g_parts, g_cls, normal2, inv2, *keeps, gains, hidden, w_down, w_up, slope, h1_low, normal1, inv1, w_out,
        ],
        [
            down,
            down,
            up,
            up,
            struct((1, hid), f32),
            struct(full, bf16),
            narrow,
            narrow,
            struct((8, width), f32),
        ],
        [
            pltpu.VMEM((4, width // 4, rows), bf16),
            pltpu.VMEM((width, rows), bf16),
            pltpu.VMEM(full, f32),
            pltpu.VMEM(full, bf16),
        ],
        (25, 11),
        "feed_backward",
        20,
    )


def out_backward(half, own, pair, g_attn):
    rows, width = g_attn.shape
    size = width // 4
    padded = -(-size // 128) * 128
    part = struct((2, width, padded), bf16)

    def body(scalars, reads, writes, ctx, cut):
        (half,) = scalars
        for which in range(3):
            reads.start(which)
        own_t, pair_t = reads.wait(0)[...].T, reads.wait(1)[...].T
        for b in (0, 1):
            lines = slice(b * size, (b + 1) * size)
            ctx[2 * b + half] = own_t[lines]
            ctx[2 * b + 1 - half] = pair_t[lines]
        g = reads.wait(2)
        for b in range(4):
            cut[b] = g[:, b * size : (b + 1) * size]
        lhs = ctx[...].reshape(4 * size, -1)
        for who, ref in ((1 - half, 0), (half, 1)):
            for b in (0, 1):
                writes.buffers[ref][b, :, :size] = dot(lhs, cut[2 * b + who]).astype(bf16)
                writes.buffers[ref][b, :, size:] = jnp.zeros((width, padded - size), bf16)
            writes.start(ref)

    return streamed(
        body,
        [half],
        [own, pair, g_attn],
        [part, part],
        [pltpu.VMEM((4, size, rows), bf16), pltpu.VMEM((4, rows, size), bf16)],
        (3, 2),
        "out_backward",
        4,
    )


def pick(values, index, axis):
    return lax.dynamic_index_in_dim(values, index, axis, keepdims=False)


def add_low(*parts):
    total = parts[0].astype(f32)
    for part in parts[1:]:
        total = total + part.astype(f32)
    return total.astype(bf16)


class Halving:
    def __init__(self, values, shape, names, order, place):
        self.values = [v.reshape(shape) for v in values]
        self.names, self.order, self.place = list(names), list(order), place

    def total(self):
        return self.values[0] if len(self.values) == 1 else add_low(*self.values)

    def cut(self):
        step = self.order.pop(0)
        axis = self.names.index(step)
        self.names.pop(axis)
        side, dp, bits = self.place
        if step == "side":
            bit, self.route = side, ("seq", CROSS)
        else:
            bit = (dp >> step) & 1
            self.route = ("dp", [(d, d ^ (1 << step)) for d in range(1 << bits)])
        halves = []
        for which in (1 - bit, bit):
            parts = [pick(v, which, axis) for v in self.values]
            halves.append(parts[0] if len(parts) == 1 else add_low(*parts))
        return halves

    def join(self, arrived, kept):
        self.values = [kept, arrived]


class Summing:
    def __init__(self, values, bits):
        self.values = values
        self.order = [("seq", PAIR), ("seq", CROSS)]
        self.order += [("dp", [(d, d ^ (1 << k)) for d in range(1 << bits)]) for k in range(bits)]

    def cut(self):
        self.route = self.order.pop(0)
        return self.values, None

    def join(self, arrived, kept):
        self.values = self.values + arrived


class Rows:
    def __init__(self, own, send, length):
        self.values, self.send, self.length, self.order = own, send, length, [PAIR, CROSS]

    def cut(self):
        self.route = ("seq", self.order.pop(0))
        if self.order:
            return self.send, self.values
        return self.values[self.length :].astype(bf16), self.values[: self.length]

    def join(self, arrived, kept):
        self.values = kept.astype(f32) + arrived.astype(f32) if self.order else (kept, arrived)


def advance(streams, *others):
    streams = [stream for stream in streams if stream.order]
    cuts = [stream.cut() for stream in streams]
    cuts, others = lax.optimization_barrier((cuts, others))
    for stream, (send, kept) in zip(streams, cuts):
        stream.join(lax.ppermute(send, *stream.route), kept)
    return others


class Tiled:
    def __init__(self, values, names, lines, order):
        self.values, self.names, self.lines, self.order = values, list(names), lines, list(order)

    def total(self):
        parts = [lax.slice_in_dim(v, at, at + self.lines, axis=0) for v, at, _ in self.values]
        return parts[0] if len(parts) == 1 else add_low(*parts)


class Shared:
    def __init__(self, values, lines, order):
        self.values, self.lines, self.order = values, lines, list(order)

    total = Tiled.total


def combine(bits_of, streams):
    streams = [stream for stream in streams if stream.order]
    arrays, cuts, links = [], [], {}
    for stream in streams:
        step = stream.order.pop(0)
        if isinstance(stream, Shared):
            pre, half = 0, stream.lines
        elif step == "z":
            pre, half = -1, stream.lines
            for offset in (1, 2, 3):
                at = links.setdefault(f"z{offset}", 0)
                links[f"z{offset}"] += half
        else:
            axis = stream.names.index(step)
            stream.names.pop(axis)
            pre, half = 1 << axis, stream.lines << len(stream.names)
        if step != "z":
            at = links.setdefault(step, 0)
            links[step] += half
        loads = []
        for array, first, stride in stream.values:
            known = [i for i, a in enumerate(arrays) if a is array]
            loads.append((known[0] if known else len(arrays), first, stride))
            if not known:
                arrays.append(array)
        cuts.append((step, at, pre, stream.lines, half, loads))
    steps = list(links)
    width = arrays[0].shape[1]

    def piece(load, pre, lines, half):
        which, first, stride = load
        if pre <= 0:
            return which, first, lines if pre == 0 else 4 * lines
        return (which, first, 2 * half) if stride == lines else (which, 0, 2 * half // lines * stride)

    fetched = list({piece(load, *c[2:5]) for c in cuts for load in c[5]})
    fetched.sort()

    def body(scalars, reads, writes):
        (place,) = scalars
        for key in fetched:
            reads.start(key[0], key, (pl.ds(key[1], key[2]),))
        for i, (step, at, pre, lines, half, loads) in enumerate(cuts):
            for load in loads:
                reads.wait(load[0], piece(load, pre, lines, half))
            if pre == -1:
                own = 2 * place[3] + place[2]
                for offset in range(4):
                    rows = []
                    for w, first, _ in loads:
                        start = pl.multiple_of(first + (own ^ offset) * lines, 16)
                        rows.append(reads.buffers[w][pl.ds(start, lines), :])
                    if offset:
                        out = steps.index(f"z{offset}")
                        writes.buffers[out][at : at + lines, :] = add_low(*rows)
                        writes.start(out, i, (pl.ds(at, lines),))
                    else:
                        writes.buffers[len(steps) + i][...] = add_low(*rows)
                        writes.start(len(steps) + i)
                continue
            bit = place[0 if step == "side" else step + 1]
            if pre == 0:
                total = add_low(*[reads.buffers[w][first : first + lines, :] for w, first, _ in loads])
                writes.buffers[steps.index(step)][at : at + lines, :] = total
                writes.buffers[len(steps) + i][...] = total
            post = half // lines // max(pre, 1)
            for p in range(pre):
                for out, base, which in ((steps.index(step), at, 1 - bit), (len(steps) + i, 0, bit)):
                    block = (2 * p + which) * post

                    def one(t, block=block, out=out, base=base + p * post * lines, loads=loads, lines=lines):
                        rows = []
                        for w, first, stride in loads:
                            start = pl.multiple_of(first + (block + t) * stride, 16)
                            rows.append(reads.buffers[w][pl.ds(start, lines), :])
                        total = rows[0] if len(rows) == 1 else add_low(*rows)
                        writes.buffers[out][pl.ds(pl.multiple_of(base + t * lines, 16), lines), :] = total

                    if post == 1:
                        one(0)
                    else:
                        pl.loop(0, post)(one)
            writes.start(steps.index(step), i, (pl.ds(at, half),))
            writes.start(len(steps) + i)

    outs = streamed(
        body,
        [bits_of],
        arrays,
        [struct((links[step], width), bf16) for step in steps] + [struct((c[4], width), bf16) for c in cuts],
        [],
        (len(fetched), sum(4 if c[2] == -1 else 2 for c in cuts)),
        "combine",
        4,
        far=False,
    )
    sends = dict(zip(steps, outs))
    for stream, (step, at, _, _, _, _), kept in zip(streams, cuts, outs[len(steps) :]):
        came = ["z1", "z2", "z3"] if step == "z" else [step]
        stream.values = [(kept, 0, stream.lines)] + [(link, at, stream.lines) for link in came]
    return sends


def exchange(streams, sends, bits):
    arrived = {}
    for step, send in sends.items():
        if step == "side":
            arrived[step] = lax.ppermute(send, "seq", CROSS)
        else:
            apart = 2 * int(step[1]) if isinstance(step, str) else 1 << step
            arrived[step] = lax.ppermute(send, "dp", [(d, d ^ apart) for d in range(1 << bits)])
    for stream in streams:
        stream.values = [(arrived.get(v, v) if isinstance(v, (str, int)) else v, *at) for v, *at in stream.values]


def hold(small, streams):
    arrays = arrays_of(streams)
    replace(streams, arrays, advance(small, *arrays))


def arrays_of(streams):
    return list({id(v): v for stream in streams for v, _, _ in stream.values}.values())


def replace(streams, arrays, held):
    where = {id(v): h for v, h in zip(arrays, held)}
    for stream in streams:
        stream.values = [(where[id(v)], *at) for v, *at in stream.values]


def tie(streams, *others):
    arrays = arrays_of(streams)
    replace(streams, arrays, lax.optimization_barrier((*arrays, *others)))


def gather_step(values, at, bits):
    count = 4 << bits

    def partner(device, offset):
        for k in (0, 1):
            if offset >> k & 1 and at + k <= bits:
                device ^= 2 if at + k == 0 else 4 << (at + k - 1)
        return device

    offsets = range(1, 4 if at + 1 <= bits else 2)
    parts = [
        lax.ppermute(values, ("dp", "seq"), [(d, partner(d, offset)) for d in range(count)])
        for offset in offsets
    ]
    return jnp.concatenate([values] + parts, axis=0)


def own_heads(values, half, axis):
    size = values.shape[axis] // 4
    shape = values.shape[:axis] + (2, 2, size) + values.shape[axis + 1 :]
    out = pick(values.reshape(shape), half, axis + 1)
    return out.reshape(values.shape[:axis] + (2 * size,) + values.shape[axis + 1 :])


def after(value, *others):
    return lax.optimization_barrier((value,) + others)[0]


def body(
    embeds,
    lengths,
    drop_in,
    drop_ff,
    positive,
    w_qkv,
    w_out,
    w_up,
    w_down,
    pool_w,
    gains,
    biases,
    up_bias,
    out_grad,
):
    _, _, length, width = drop_in.shape
    n_dp = lax.axis_size("dp")
    bits = n_dp.bit_length() - 1
    seq = lax.axis_index("seq")
    dp = lax.axis_index("dp")
    side, half = seq // 2, seq % 2
    half1 = half.astype(jnp.int32).reshape(1)
    side1 = side.astype(jnp.int32).reshape(1)
    first_side = side == 0
    place_keys = jnp.stack([seq.astype(jnp.int32), lengths[0]])

    token = embeds[0]
    masks_in = (pick(drop_in, side, 0)[0], pick(drop_in, 1 - side, 0)[0])
    kept_send = token * masks_in[1].astype(bf16)
    kept_cross = lax.ppermute(kept_send, "seq", CROSS)
    kept_local = token * masks_in[0].astype(bf16)
    kept_local_pair = lax.ppermute(kept_local, "seq", PAIR)

    w_own, b_own, qkv_local = project_local(half1, kept_local, kept_local_pair, w_qkv, biases)
    rest = jnp.stack([pick(drop_ff, 1 - side, 0)[0].astype(bf16), pick(out_grad, 1 - side, 0)[0]])
    kept_cross, w_own, rest, place_keys = lax.optimization_barrier((kept_cross, w_own, rest, place_keys))
    kept_cross_pair = lax.ppermute(kept_cross, "seq", PAIR)
    qkv_cross = project_cross(kept_cross, kept_cross_pair, w_own, b_own)
    kept = (kept_local, kept_local_pair, kept_cross, kept_cross_pair)
    rest = lax.ppermute(after(rest, kept_cross), "seq", CROSS)
    keeps = (pick(drop_ff, side, 0)[0].astype(bf16), rest[0])
    g_parts = (pick(out_grad, side, 0)[0], rest[1])
    w_out4 = w_out.reshape(4, width // 4, width)
    up_bias2 = up_bias[None]

    own, send, lse = attend_forward(place_keys, qkv_local, qkv_cross)
    pair = lax.ppermute(send, "seq", PAIR)
    hidden, slope, h1_low, normal1, inv1, normal2, inv2, mixed_local, mixed_cross = layer_forward(
        half1, own, pair, (kept_local, kept_cross), keeps, w_out4, w_up, w_down, gains, biases, up_bias2
    )

    first = jnp.where(first_side, mixed_local[:1], mixed_cross[:1])
    rel = first
    for at in range(0, bits + 1, 2):
        rel = gather_step(rel, at, bits)
    shift = jnp.stack([side, dp]).astype(jnp.int32)
    positive_col = jnp.broadcast_to(positive[:, None], (n_dp, 128))
    _, _, _, g_cls = loss_parts(shift, rel, pool_w, positive_col)
    mixed_back = lax.ppermute(after(mixed_cross, g_cls), "seq", CROSS)

    down_send, down_keep, up_send, up_keep, up_sum, g_attn, g_own, g_send, sums = feed_backward(
        half1,
        side1,
        g_parts,
        g_cls,
        normal2,
        inv2,
        keeps,
        gains,
        hidden,
        w_down,
        w_up,
        slope,
        h1_low,
        normal1,
        inv1,
        w_out4,
    )
    g_attn, g_send, down_send, up_send, mixed_back = lax.optimization_barrier(
        (g_attn, g_send, down_send, up_send, mixed_back)
    )
    g_pair = lax.ppermute(g_send, "seq", PAIR)

    dims = (2,) * bits
    place = (side, dp, bits)
    dp_names = list(range(bits - 1, -1, -1))
    names = ["side"] + dp_names
    low = list(range(1, bits))
    sub = n_dp // GROUPS
    deep = width // n_dp
    cut = width // 4

    tiled = deep % 16 == 0
    down_pair = lax.ppermute(down_send, "seq", PAIR)
    up_pair = lax.ppermute(up_send, "seq", PAIR)
    side_first, dp_first = ["side", 0] + low, [0, "side"] + low
    low_first = low[:1] + ["side", 0] + low[1:]
    if tiled:

        def flat(values):
            return values.reshape(-1, width)

        bits_of = jnp.stack([side] + [(dp >> k) & 1 for k in range(bits)]).astype(jnp.int32)
        most = deep * 2 // 3

        def split(keep, pair, axes, order, rest):
            values = [(flat(keep), 0, deep), (flat(pair), 0, deep)]
            later = [(v, most, stride) for v, _, stride in values]
            return [Tiled(values, axes, most, order), Tiled(later, axes, deep - most, rest)]

        ups = split(up_keep, up_pair, names, side_first, low + ["side", 0])
        downs = split(down_keep, down_pair, dp_names + ["side"], dp_first, low + [0, "side"])
        early = [ups[0], downs[0], ups[1], downs[1]]
        out_send, out_keep = out_backward(half1, own, pair, g_attn)
        outs = (out_keep, lax.ppermute(out_send, "seq", PAIR))
        sends = combine(bits_of, early)
        rel_pair = lax.ppermute(rel, "seq", [(0, 1), (2, 3)])
        g_own, g_pair, rel_pair, *held = lax.optimization_barrier((g_own, g_pair, rel_pair, *sends.values()))
        exchange(early, dict(zip(sends, held)), bits)
        *grads, swapped = attend_backward(place_keys, qkv_local, qkv_cross, own, send, g_own, g_pair, lse)
        swapped = lax.ppermute(swapped, "seq", PAIR)
        tie(early, *grads)
        sends = combine(bits_of, early)
        grads = lax.optimization_barrier((*grads, *sends.values()))[:3]
        exchange(early, sends, bits)
        splits = ((0, deep // 2), (1, deep // 2))
        orders = (["side", 0, "z"], [0, "side", "z"])
        g_x, g_x_send, sums, *parts = project_backward(
            half1, bits_of, grads, swapped, kept, outs, w_own, g_attn, sums, up_sum, splits, deep
        )
        qkv = []
        for (_, take), order, send_part, keep_part in zip(splits, orders, parts[::2], parts[1::2]):
            left = [name for name in names if name != order[0]]
            stream = Tiled([(keep_part, 0, take), (order[0], 0, take)], left, take, order[1:])
            exchange([stream], {order[0]: send_part}, bits)
            qkv.append(stream)
        small = [Rows(g_x, g_x_send, length)]
        advance(small)
        sums = sums.astype(bf16)
        shared = Shared(
            [(sums, 0, 16), (lax.ppermute(sums, "seq", PAIR), 0, 16)], 16, low[:1] + ["side", 0]
        )
        tie(early, *parts)
        sends = combine(bits_of, early[:2] + [shared])
        exchange(early[:2] + [shared], sends, bits)
        streams = qkv + early + [shared]
        sends = combine(bits_of, streams)
        exchange(streams, sends, bits)
        rel = after(jnp.where(half == 0, rel, rel_pair), *sends.values())
        found = loss_parts(shift, rel, pool_w, positive_col)
        tie(streams, found[0])
    else:
        sub = n_dp // GROUPS

        def turned(values):
            values = values.reshape(GROUPS, 2, width // 8, 2, sub, -1)
            return values.transpose(0, 4, 1, 3, 2, 5)

        down = Halving(
            [turned(down_keep), turned(down_pair)], dims + (2, cut, -1), dp_names + ["side"], dp_first, place
        )
        up = Halving([up_keep, up_pair], (2,) + dims + (deep, -1), names, side_first, place)
        out_send, out_keep = out_backward(half1, own, pair, g_attn)
        outs = (out_keep, lax.ppermute(out_send, "seq", PAIR))
        g_own, g_pair = advance([up, down], g_own, g_pair)
        *grads, swapped = attend_backward(place_keys, qkv_local, qkv_cross, own, send, g_own, g_pair, lse)
        swapped = lax.ppermute(swapped, "seq", PAIR)
        g_x, g_x_send, sums, part = project_backward(
            half1, place_keys, grads, swapped, kept, outs, w_own, g_attn, sums, up_sum, (), 0
        )
        qkv = [Halving([part], (2,) + dims + (deep, width), names, side_first, place)]
        streams = qkv + [up, down]
        small = [Summing(sums, bits), Rows(g_x, g_x_send, length)]
    while any(stream.order for stream in streams + small):
        if tiled:
            hold(small, streams)
            if any(stream.order for stream in streams):
                sends = combine(bits_of, streams)
                exchange(streams, sends, bits)
        else:
            advance(streams + small)
    if not tiled:
        rel = jnp.where(half == 0, rel, lax.ppermute(rel, "seq", [(0, 1), (2, 3)]))
        found = loss_parts(shift, rel, pool_w, positive_col)
    if tiled:
        sums = shared.total()
        shared.values = [(sums, 0, 16), (lax.ppermute(sums, "dp", [(d, d ^ 4) for d in range(n_dp)]), 0, 16)]
        tie(qkv, shared.total())
    values, cls_all, g_pre, _ = found
    pool_rows, pool_cols = width // n_dp, width // 4
    grad_pool = t_dot(
        lax.dynamic_slice_in_dim(cls_all, dp * pool_rows, pool_rows, 1),
        lax.dynamic_slice_in_dim(g_pre, seq * pool_cols, pool_cols, 1),
    )
    mixed_out = jnp.stack(
        [jnp.where(first_side, mixed_local, mixed_back), jnp.where(first_side, mixed_back, mixed_local)]
    )[:, None]
    total = shared.total().astype(f32) if tiled else small[0].values
    g_x, g_x_cross = small[-1].values
    if tiled:
        grad_up = jnp.concatenate([stream.total() for stream in ups], axis=0).astype(f32)
        grad_down = jnp.concatenate([stream.total() for stream in downs], axis=0)
    else:
        grad_up = up.total().astype(f32)
        grad_down = down.total()
    if tiled:
        grad_down = grad_down.reshape(deep, 2, -1).swapaxes(0, 1).reshape(cut, -1)
    grad_down = grad_down.astype(f32).T
    sum_qkv = jnp.concatenate([stream.total() for stream in qkv], axis=0)
    grad_out = sum_qkv[:, 3 * cut :].astype(f32)
    grad_qkv = sum_qkv[:, : 3 * cut].astype(f32)
    embeds_grad = (g_x * masks_in[0].astype(f32) + g_x_cross.astype(f32) * masks_in[1].astype(f32)) * inv_keep
    return (
        mixed_out,
        embeds_grad[None],
        grad_qkv,
        grad_out,
        grad_up,
        grad_down,
        grad_pool,
        total[0:2],
        total[2:7],
        total[7],
        total[8 : 8 + up_bias.shape[0] // width].reshape(-1),
        values[0, 0],
        values[1, 0],
        values[2, 0],
    )


def solution(mesh):
    tokens = P(None, "dp", "seq", None)
    placed = (P("dp", "seq", None), P("dp"), tokens, tokens) + (P(),) * 9 + (tokens,)
    weight = P("dp", "seq")
    return jax.shard_map(
        body,
        mesh=mesh,
        in_specs=placed,
        out_specs=(tokens, P("dp", "seq", None)) + (weight,) * 5 + (P(),) * 7,
        check_vma=False,
    )
```

```python
import functools
import math

import jax
import jax.numpy as jnp
from jax import lax
from jax.experimental import pallas as pl
from jax.experimental.pallas import tpu as pltpu
from jax.sharding import PartitionSpec as P

HEAD = 64
keep_rate = 0.9
inv_keep = 1.0 / keep_rate
highest = lax.Precision.HIGHEST
f32 = jnp.float32
bf16 = jnp.bfloat16

CROSS = [(i, i ^ 2) for i in range(4)]
PAIR = [(i, i ^ 1) for i in range(4)]
GROUPS = 8
NEAR = 2048


def cost(time):
    return pl.CostEstimate(flops=time * 2_000_000_000, bytes_accessed=1 << 20, transcendentals=0)

CHUNK = 768


def dot(a, b):
    return jnp.dot(a, b, preferred_element_type=f32)


def dot_t(a, b):
    return lax.dot_general(a, b, (((1,), (1,)), ((), ())), preferred_element_type=f32)


def t_dot(a, b):
    return lax.dot_general(a, b, (((0,), (0,)), ((), ())), preferred_element_type=f32)


def whole(shape):
    return pl.BlockSpec(shape, lambda *_: (0,) * len(shape))


def struct(shape, dtype):
    return jax.ShapeDtypeStruct(shape, dtype)


def hbm(x):
    return pltpu.with_memory_space_constraint(x, pltpu.HBM)


def params(limit):
    return pltpu.CompilerParams(vmem_limit_bytes=limit << 20)


ALL = (slice(None),)


class Stream:
    def __init__(self, refs, buffers, sems, out):
        self.refs, self.buffers, self.sems, self.out = refs, buffers, sems, out
        self.count, self.copies = 0, {}

    def start(self, which, key=0, at=ALL):
        if self.refs[which] is self.buffers[which]:
            return
        ref, buffer = self.refs[which].at[at], self.buffers[which].at[at]
        source, target = (buffer, ref) if self.out else (ref, buffer)
        copy = pltpu.make_async_copy(source, target, self.sems.at[self.count])
        copy.start()
        self.count += 1
        self.copies[which, key] = copy

    def wait(self, which, key=0):
        copy = self.copies.pop((which, key), None)
        if copy is not None:
            copy.wait()
        return self.buffers[which]

    def drain(self):
        for which, key in list(self.copies):
            self.wait(which, key)


def streamed(body, scalars, ins, outs, scratch, copies, name, time, limit=56, near=(), stay=()):
    n_s, n_i, n_o = len(scalars), len(ins), len(outs)
    far = [i for i in range(n_i) if i not in near]
    leave = [i for i in range(n_o) if i not in stay]

    def kernel(*refs):
        cuts = [n_s, n_i, n_o, len(far), len(leave), len(scratch), 1, 1]
        parts, at = [], 0
        for cut in cuts:
            parts.append(refs[at : at + cut])
            at += cut
        buffers = list(parts[1])
        for i, buffer in zip(far, parts[3]):
            buffers[i] = buffer
        reads = Stream(parts[1], buffers, parts[6][0], False)
        results = list(parts[2])
        for i, buffer in zip(leave, parts[4]):
            results[i] = buffer
        writes = Stream(parts[2], results, parts[7][0], True)
        body([r[0] if r.shape[0] == 1 else r for r in parts[0]], reads, writes, *parts[5])
        reads.drain()
        writes.drain()

    smem, home = pl.BlockSpec(memory_space=pltpu.SMEM), pl.BlockSpec(memory_space=pltpu.HBM)
    close = pl.BlockSpec(memory_space=pltpu.VMEM)
    return pl.pallas_call(
        kernel,
        in_specs=[smem] * n_s + [close if i in near else home for i in range(n_i)],
        out_specs=[close if i in stay else home for i in range(n_o)],
        out_shape=[o if i in stay else pltpu.HBM(o.shape, o.dtype) for i, o in enumerate(outs)],
        scratch_shapes=[pltpu.VMEM(x.shape, x.dtype) for x in [ins[i] for i in far] + [outs[i] for i in leave]]
        + list(scratch)
        + [pltpu.SemaphoreType.DMA((max(copies[0], 1),)), pltpu.SemaphoreType.DMA((copies[1],))],
        compiler_params=params(limit),
        cost_estimate=cost(time),
        name=name,
    )(*scalars, *[x if i in near else hbm(x) for i, x in enumerate(ins)])


def one_head(block, head, extra):
    lane = lax.broadcasted_iota(jnp.int32, block.shape, 1)
    mine = (lane >= HEAD) if head else (lane < HEAD)
    out = jnp.where(mine, block, jnp.zeros_like(block))
    if extra is not None:
        out = jnp.where(lane == (0 if head else HEAD), extra, out)
    return out


def key_mask(place_ref, rows):
    quarter = rows // 4
    parts = []
    for b in range(4):
        at = lax.broadcasted_iota(jnp.int32, (quarter, 128), 0) + (place_ref[0] ^ b) * quarter
        parts.append(jnp.where(at < place_ref[1], 0.0, -1e30).astype(bf16))
    return jnp.concatenate(parts, axis=0)


def forward_kernel(place_ref, ql_ref, qc_ref, kl_ref, kc_ref, vl_ref, vc_ref, own_ref, send_ref, lse_ref):
    key = jnp.concatenate([kl_ref[...], kc_ref[...]], axis=0)
    mask = key_mask(place_ref, key.shape[0])
    keys = [one_head(key, h, mask) for h in (0, 1)]
    value_t = jnp.concatenate([vl_ref[...], vc_ref[...]], axis=0).T
    one = jnp.ones((), bf16)
    rows = ql_ref.shape[0]
    cut = rows // 2
    units = [(part, c, h) for part in (0, 1) for c in (0, 1) for h in (0, 1)]
    scores, weights = [], []
    for part, c, h in units:
        q = (ql_ref, qc_ref)[part][c * cut : (c + 1) * cut, :] * jnp.asarray(1.0 / math.sqrt(HEAD), bf16)
        scores.append(dot_t(keys[h], one_head(q, h, one)))
    for (part, c, h), s in zip(units, scores):
        top = jnp.max(s, axis=0, keepdims=True)
        p = jnp.exp(s - top)
        total = jnp.sum(p, axis=0, keepdims=True)
        start = part * rows + c * cut
        lse_ref[0, h : h + 1, start : start + cut] = top + jnp.log(total)
        weights.append((p.astype(bf16), total))
    outs = [
        dot(value_t[HEAD * h : HEAD * (h + 1), :], p) * (1.0 / total)
        for (part, c, h), (p, total) in zip(units, weights)
    ]
    for i in range(0, len(units), 2):
        part, c, _ = units[i]
        out = jnp.concatenate(outs[i : i + 2], axis=0).T.astype(bf16)
        (own_ref, send_ref)[c][part * cut : (part + 1) * cut, :] = out


def attend_forward(place, qkv_local, qkv_cross):
    rows, pairs = qkv_local.shape[0], qkv_local.shape[1] // 384

    def block(offset):
        return [pl.BlockSpec((rows, 128), lambda i: (0, i + offset))] * 2

    return pl.pallas_call(
        forward_kernel,
        grid=(pairs,),
        in_specs=[pl.BlockSpec(memory_space=pltpu.SMEM)] + block(0) + block(pairs) + block(2 * pairs),
        out_specs=block(0) + [pl.BlockSpec((1, 2, 2 * rows), lambda i: (i, 0, 0))],
        out_shape=[
            pltpu.HBM((rows, pairs * 128), bf16),
            pltpu.HBM((rows, pairs * 128), bf16),
            pltpu.HBM((pairs, 2, 2 * rows), f32),
        ],
        compiler_params=params(56),
        cost_estimate=cost(13),
        name="attend_forward",
    )(place, *(hbm(qkv_local), hbm(qkv_cross)) * 3)


def backward_kernel(
    place_ref,
    ql_ref,
    qc_ref,
    kl_ref,
    kc_ref,
    vl_ref,
    vc_ref,
    o0,
    o1,
    g0,
    g1,
    lse_ref,
    dq_ref,
    dk_ref,
    dv_ref,
    swap_ref,
    dk_acc,
    dv_acc,
):
    chunk = ql_ref.shape[0]
    scale = 1.0 / math.sqrt(HEAD)
    key = jnp.concatenate([kl_ref[...], kc_ref[...]], axis=0)
    mask = key_mask(place_ref, key.shape[0])
    keys = [one_head(key, h, mask) for h in (0, 1)]
    key_t = key.T
    value = jnp.concatenate([vl_ref[...], vc_ref[...]], axis=0)
    one = jnp.ones((), bf16)
    for c, q_ref in enumerate((ql_ref, qc_ref)):
        at = slice(c * chunk, (c + 1) * chunk)
        half = slice(c * chunk // 2, (c + 1) * chunk // 2)
        out = jnp.concatenate([o0[half, :], o1[half, :]], axis=0)
        do = jnp.concatenate([g0[half, :], g1[half, :]], axis=0)
        q = q_ref[...] * jnp.asarray(scale, bf16)
        prod_t = (do.astype(f32) * out.astype(f32)).T
        ps, dss, dos, qs, dq_t = [], [], [], [], []
        for h in (0, 1):
            rows = slice(HEAD * h, HEAD * (h + 1))
            s = dot_t(keys[h], one_head(q, h, one))
            p = jnp.exp(s - lse_ref[0, h : h + 1, at])
            do_h = one_head(do, h, None)
            dp = dot_t(value, do_h)
            delta = jnp.sum(prod_t[rows, :], axis=0, keepdims=True)
            ds = (p * (dp - delta)).astype(bf16)
            ps.append(p.astype(bf16))
            dss.append(ds)
            dos.append(do_h)
            qs.append(one_head(q, h, None))
            dq_t.append(dot(key_t[rows, :], ds))
        dv_c = dot(jnp.concatenate(ps, 1), jnp.concatenate(dos, 0))
        dk_c = dot(jnp.concatenate(dss, 1), jnp.concatenate(qs, 0))
        if c == 0:
            dv_acc[...] = dv_c
            dk_acc[...] = dk_c
        else:
            dv_ref[...] = (dv_acc[...] + dv_c).astype(bf16)
            dk_ref[...] = (dk_acc[...] + dk_c).astype(bf16)
        dq_ref[at, :] = (jnp.concatenate(dq_t, 0).T * scale).astype(bf16)

    step = pl.program_id(0)
    even = place_ref[0] % 2 == 0
    lane = lax.broadcasted_iota(jnp.int32, dq_ref.shape, 1) + 128 * step
    early = jnp.where(even, dk_ref[...], dq_ref[...])
    late = jnp.where(even, dv_ref[...], dk_ref[...])
    swap_ref[...] = jnp.where(lane < 64 * pl.num_programs(0), early, late)


def attend_backward(place, qkv_local, qkv_cross, own, send, g_own, g_pair, lse):
    rows, pairs = qkv_local.shape[0], qkv_local.shape[1] // 384

    def block(offset):
        return [pl.BlockSpec((rows, 128), lambda i: (0, i + offset))] * 2

    return pl.pallas_call(
        backward_kernel,
        grid=(pairs,),
        in_specs=[pl.BlockSpec(memory_space=pltpu.SMEM)]
        + block(0)
        + block(pairs)
        + block(2 * pairs)
        + block(0) * 2
        + [pl.BlockSpec((1, 2, 2 * rows), lambda i: (i, 0, 0))],
        out_specs=[pl.BlockSpec((2 * rows, 128), lambda i: (0, i))] * 4,
        out_shape=[struct((2 * rows, pairs * 128), bf16)] * 4,
        scratch_shapes=[pltpu.VMEM((2 * rows, 128), f32)] * 2,
        compiler_params=params(32),
        cost_estimate=cost(20),
        name="attend_backward",
    )(place, *[hbm(x) for x in (qkv_local, qkv_cross) * 3 + (own, send, g_own, g_pair, lse)])


def project_backward(half, bits_of, grads, swapped, kept, outs, w_own, g_attn, sums, up_sum, splits, lines):
    rows, width = g_attn.shape
    n, narrow = grads[0].shape
    quarter = n // 4
    cut = width // 4
    many = up_sum.shape[1] // width
    GRADS, KEPT, OUTS, W_OWN, G_ATTN, SUMS_IN, UP_SUM, SWAPPED = 0, 3, 7, 9, 10, 11, 12, 13
    OWN, SEND, SUMS, FIRST = range(4)
    if lines:
        weights = [(width // lines * take, width) for _, take in splits]
        results = [struct(shape, bf16) for shape in weights for _ in (0, 1)]
    else:
        results = [struct((2, width, width), bf16)]

    def body(scalars, reads, writes):
        half, bits_ref = scalars
        for which in (KEPT, KEPT + 1, KEPT + 2, KEPT + 3, 0, 1, 2, SWAPPED, OUTS, OUTS + 1, W_OWN, G_ATTN, SUMS_IN, UP_SUM):
            reads.start(which)
        buf = writes.buffers
        x = jnp.concatenate([reads.wait(KEPT + i)[...] for i in range(4)], axis=0)
        x_t = (x.astype(f32) * inv_keep).astype(bf16).T
        for which in (0, 1, 2, SWAPPED, OUTS, OUTS + 1):
            reads.wait(which)
        q, k, v = (reads.buffers[GRADS + i] for i in range(3))
        came = jnp.concatenate(
            [reads.buffers[SWAPPED][b * quarter : (b + 1) * quarter, :] for b in (1, 0, 3, 2)], axis=0
        )
        even = half == 0
        columns = (
            jnp.concatenate(
                [
                    jnp.where(even, q[:, :cut], q[:, cut:]),
                    came[:, :cut],
                    jnp.where(even, q[:, cut:], k[:, :cut]),
                ],
                axis=1,
            ),
            jnp.concatenate(
                [
                    jnp.where(even, k[:, cut:], v[:, :cut]),
                    came[:, cut:],
                    jnp.where(even, v[:, :cut], v[:, cut:]),
                ],
                axis=1,
            ),
        )
        for side in (0, 1):
            out = add_low(reads.buffers[OUTS][side, :, :cut], reads.buffers[OUTS + 1][side, :, :cut])
            part = jnp.concatenate([dot(x_t, columns[side]).astype(bf16), out], axis=1)
            if not lines:
                buf[FIRST][side] = part
                continue
            blocks = width // lines
            done = 0
            for i, (bit, take) in enumerate(splits):
                block = part.reshape(blocks, lines, width)[:, done : done + take]
                done += take
                target, kept = buf[FIRST + 2 * i], buf[FIRST + 2 * i + 1]
                if bit == 0:
                    block = block.reshape(blocks * take, width)

                    @pl.when(bits_ref[0] == side)
                    def _(block=block, kept=kept):
                        kept[...] = block

                    @pl.when(bits_ref[0] != side)
                    def _(block=block, target=target):
                        target[...] = block

                    continue
                post = 1 << bit - 1
                block = block.reshape(blocks // (2 * post), 2, post * take, width)
                size = blocks * take // 2
                spot = slice(side * size, (side + 1) * size)
                for value in (0, 1):
                    piece = block[:, value].reshape(size, width)

                    @pl.when(bits_ref[bit] == value)
                    def _(piece=piece, kept=kept, spot=spot):
                        kept[spot, :] = piece

                    @pl.when(bits_ref[bit] != value)
                    def _(piece=piece, target=target, spot=spot):
                        target[spot, :] = piece

        for i in range(len(results)):
            writes.start(FIRST + i)
        for which in (W_OWN, G_ATTN, SUMS_IN, UP_SUM):
            reads.wait(which)
        w = reads.buffers[W_OWN]
        for which, ref in ((1, SEND), (0, OWN)):
            total = None
            for i in range(3):
                g = reads.buffers[GRADS + i]
                g = jnp.concatenate(
                    [g[(which + b) * quarter : (which + b + 1) * quarter, :] for b in (0, 2)], axis=0
                )
                part = dot_t(g, w[:, i * narrow : (i + 1) * narrow])
                total = part if total is None else total + part
            if which == 0:
                total = total + reads.buffers[G_ATTN][...].astype(f32)
            buf[ref][...] = total.astype(bf16)
            writes.start(ref)
        buf[SUMS][0:8, :] = reads.buffers[SUMS_IN][...]
        tail = [reads.buffers[UP_SUM][:, i * width : (i + 1) * width] for i in range(many)]
        buf[SUMS][8:, :] = jnp.concatenate(tail + [jnp.zeros((8 - many, width), f32)], axis=0)
        for line, which in ((2, 0), (3, 2)):
            total = jnp.sum(reads.buffers[which][...].astype(f32), axis=0, keepdims=True)
            for b in (0, 1):
                block = total[:, b * cut : (b + 1) * cut]
                for who in (0, 1):
                    at = (2 * b + who) * cut
                    buf[SUMS][line : line + 1, at : at + cut] = jnp.where(half == who, block, jnp.zeros_like(block))
        writes.start(SUMS)

    return streamed(
        body,
        [half, bits_of],
        [*grads, *kept, *outs, w_own, g_attn, sums, up_sum, swapped],
        [struct((rows, width), bf16), struct((rows, width), bf16), struct((16, width), f32)] + results,
        [],
        (14, 3 + len(results)),
        "project_backward",
        10,
        limit=36,
        near=(0, 1, 2, 8, 13),
        stay=range(3 + len(results)) if lines else (),
    )


def project_local(half, own, pair, w_qkv, biases):
    rows, width = own.shape
    cut = width // 4

    def body(scalars, reads, writes, bias):
        (half,) = scalars
        for which in (2, 3, 0, 1):
            reads.start(which)
        w, b = reads.wait(2), reads.wait(3)
        w_own, b_own = writes.buffers[0], writes.buffers[1]
        for who in (0, 1):

            @pl.when(half == who)
            def _(who=who):
                for kind in range(3):
                    base = kind * width
                    lines = [slice(base + (who + 2 * i) * cut, base + (who + 2 * i + 1) * cut) for i in (0, 1)]
                    target = slice(kind * 2 * cut, (kind + 1) * 2 * cut)
                    w_own[:, target] = jnp.concatenate([w[:, line] for line in lines], axis=1)
                    if kind == 1:
                        b_own[:, target] = jnp.zeros((8, 2 * cut), f32)
                    else:
                        row = b[kind // 2 : kind // 2 + 1, :]
                        row = jnp.concatenate([row[:, line.start - base : line.stop - base] for line in lines], axis=1)
                        b_own[:, target] = jnp.broadcast_to(row, (8, 2 * cut))

        writes.start(0)
        writes.start(1)
        x = jnp.concatenate([reads.wait(0)[...], reads.wait(1)[...]], axis=0)
        x = (x.astype(f32) * inv_keep).astype(bf16)
        writes.buffers[2][...] = (dot(x, w_own[...]) + b_own[0:1, :]).astype(bf16)
        writes.start(2)

    return streamed(
        body,
        [half],
        [own, pair, w_qkv, biases],
        [struct((width, 6 * cut), bf16), struct((8, 6 * cut), f32), struct((2 * rows, 6 * cut), bf16)],
        [pltpu.VMEM((8, 128), f32)],
        (4, 3),
        "project_local",
        5,
    )


def project_cross(own, pair, w_own, b_own):
    rows = own.shape[0]

    def body(scalars, reads, writes):
        for which in range(4):
            reads.start(which)
        x = jnp.concatenate([reads.wait(0)[...], reads.wait(1)[...]], axis=0)
        x = (x.astype(f32) * inv_keep).astype(bf16)
        w, b = reads.wait(2), reads.wait(3)
        writes.buffers[0][...] = (dot(x, w[...]) + b[0:1, :]).astype(bf16)
        writes.start(0)

    return streamed(
        body,
        [],
        [own, pair, w_own, b_own],
        [struct((2 * rows, w_own.shape[1]), bf16)],
        [],
        (4, 1),
        "project_cross",
        4,
        limit=20,
        near=(0, 1),
    )[0]


def norm_parts(values):
    mean = jnp.mean(values, axis=-1, keepdims=True)
    centred = values - mean
    inv = lax.rsqrt(jnp.mean(centred * centred, axis=-1, keepdims=True) + 1e-06)
    return centred * inv, inv


def norm_back(g, normal, inv, gain):
    a = g * gain
    return (
        a - jnp.mean(a, axis=-1, keepdims=True) - normal * jnp.mean(a * normal, axis=-1, keepdims=True)
    ) * inv


def gelu_parts(u):
    e = jnp.exp(-0.5 * u * u)
    t = 1.0 / (1.0 + (0.3275911 / math.sqrt(2.0)) * jnp.abs(u))
    poly = 0.5 * 1.061405429
    for a in (-1.453152027, 1.421413741, -0.284496736, 0.254829592):
        poly = poly * t + 0.5 * a
    tail = poly * t * e
    phi = jnp.where(u < 0, tail, 1.0 - tail)
    return u * phi, phi + u * e * (1.0 / math.sqrt(2.0 * math.pi))


def layer_forward(half, own, pair, kept, keep, w_out, w_up, w_down, gains, biases, up_bias):
    rows, width = kept[0].shape
    hid = w_up.shape[1]
    parts = hid // width
    tile = (rows, width)
    full = (2 * rows, width)
    cuts = [slice(c * width, (c + 1) * width) for c in range(parts)]
    OWN, PAIR_, KEPT, KEEP, W_OUT, W_UP, W_DOWN, GAINS, BIASES, UP_BIAS = 0, 1, 2, 4, 6, 7, 8, 9, 10, 11
    HIDDEN, SLOPE, H1_LOW, NORMAL1, INV1, NORMAL2, INV2, MIXED = range(8)

    def body(scalars, reads, writes, h1):
        (half,) = scalars
        for which in (OWN, PAIR_, W_OUT, BIASES, KEPT, KEPT + 1, GAINS, UP_BIAS):
            reads.start(which)
        def fetch(c):
            reads.start(W_UP, c, (slice(None), cuts[c]))
            reads.start(W_DOWN, c, (cuts[c],))

        fetch(0)
        own, pair, w_out = (reads.wait(w)[...] for w in (OWN, PAIR_, W_OUT))
        for c in range(1, parts):
            fetch(c)
        reads.start(KEEP)
        reads.start(KEEP + 1, 0, (0,))
        biases = reads.wait(BIASES)
        half = jnp.int32(half)

        def mine(who):
            w = reads.buffers[W_OUT]
            return jnp.concatenate([w[who], w[who + 2]], axis=0)

        attn = dot(own, mine(half)) + dot(pair, mine(1 - half)) + biases[2:3, :]
        xin = jnp.concatenate([reads.wait(KEPT)[...], reads.wait(KEPT + 1)[...]], axis=0)
        normal, inv = norm_parts(xin.astype(f32) * inv_keep + attn)
        gains = reads.wait(GAINS)
        buf = writes.buffers
        buf[NORMAL1][...] = normal.astype(bf16)
        buf[INV1][...] = jnp.broadcast_to(inv, buf[INV1].shape)
        h1[...] = normal * gains[0:1, :] + biases[3:4, :]
        h1_low = h1[...].astype(bf16)
        buf[H1_LOW][...] = h1_low
        for which in (NORMAL1, INV1, H1_LOW):
            writes.start(which)
        up_bias = reads.wait(UP_BIAS)
        reads.wait(W_UP, 0)
        reads.wait(W_DOWN, 0)
        ff = biases[4:5, :]
        for c, at in enumerate(cuts):
            if c == 1:
                for k in range(1, parts):
                    reads.wait(W_UP, k)
                    reads.wait(W_DOWN, k)
            up = dot(h1_low, reads.buffers[W_UP][:, at]) + up_bias[:, at]
            hidden, slope = gelu_parts(up)
            hidden = hidden.astype(bf16)
            buf[HIDDEN][:, at] = hidden
            buf[SLOPE][:, at] = slope.astype(bf16)
            writes.start(HIDDEN, c, (slice(None), at))
            writes.start(SLOPE, c, (slice(None), at))
            ff = ff + dot(hidden, reads.buffers[W_DOWN][at, :])
        keep = jnp.concatenate([reads.wait(KEEP)[...], reads.wait(KEEP + 1)[0]], axis=0)
        normal, inv = norm_parts(h1[...] + ff * (keep.astype(f32) * inv_keep))
        mixed = (normal * gains[1:2, :] + biases[5:6, :]).astype(bf16)
        buf[MIXED][...] = mixed[:rows]
        buf[MIXED + 1][...] = mixed[rows:]
        writes.start(MIXED)
        writes.start(MIXED + 1)
        buf[NORMAL2][...] = normal.astype(bf16)
        buf[INV2][...] = jnp.broadcast_to(inv, buf[INV2].shape)
        writes.start(NORMAL2)
        writes.start(INV2)

    return streamed(
        body,
        [half],
        [own, pair, *kept, *keep, w_out, w_up, w_down, gains, biases, up_bias],
        [
            struct((2 * rows, hid), bf16),
            struct((2 * rows, hid), bf16),
            struct(full, bf16),
            struct(full, bf16),
            struct((2 * rows, 128), f32),
            struct(full, bf16),
            struct((2 * rows, 128), f32),
            struct(tile, bf16),
            struct(tile, bf16),
        ],
        [pltpu.VMEM(full, f32)],
        (10 + 2 * parts, 7 + 2 * parts),
        "layer_forward",
        16,
        limit=42,
        near=(1,),
    )


def loss_kernel(shift_ref, cls_ref, pool_ref, positive_ref, values_ref, order_ref, g_pre_ref, g_cls_ref):
    rows = cls_ref.shape[0]
    n = rows // 2
    row = lax.broadcasted_iota(jnp.int32, (rows, rows), 0)
    column = lax.broadcasted_iota(jnp.int32, (rows, rows), 1)
    view, sentence = (column % 2) ^ shift_ref[0], (column // 2) ^ shift_ref[1]
    cls = dot((row == view * n + sentence).astype(bf16), cls_ref[...]).astype(bf16)
    order_ref[...] = cls
    pooled = jnp.tanh(dot(cls, pool_ref[...]))
    inv = lax.rsqrt(jnp.sum(pooled * pooled, axis=-1, keepdims=True) + 1e-06)
    unit = pooled * inv
    anchors, candidates = unit[:n], unit[n:]

    def exact(a, b, dims):
        return lax.dot_general(a, b, (dims, ((), ())), precision=highest, preferred_element_type=f32)

    logits = exact(anchors, candidates, ((1,), (1,))) / 0.05
    mine = lax.broadcasted_iota(jnp.int32, (n, n), 0)
    other = lax.broadcasted_iota(jnp.int32, (n, n), 1)
    picked = (other == positive_ref[:, 0:1]).astype(f32)
    top = jnp.max(logits, axis=1, keepdims=True)
    expo = jnp.exp(logits - top)
    total = jnp.sum(expo, axis=1, keepdims=True)
    target = jnp.sum(logits * picked, axis=1, keepdims=True)
    loss = jnp.mean(jnp.log(total) + top - target, axis=0, keepdims=True)
    matched = exact(picked, candidates, ((1,), (0,)))
    offset = anchors - matched
    alignment = jnp.mean(jnp.sum(offset * offset, axis=-1, keepdims=True), axis=0, keepdims=True)
    inner = exact(anchors, anchors, ((1,), (1,)))
    norms = jnp.sum(anchors * anchors, axis=-1, keepdims=True)
    norms_row = jnp.sum(jnp.where(mine == other, norms, 0.0), axis=0, keepdims=True)
    dist = norms + norms_row - 2.0 * inner
    near = jnp.where(mine != other, jnp.exp(-2.0 * dist), 0.0)
    near = jnp.sum(jnp.sum(near, axis=1, keepdims=True), axis=0, keepdims=True)
    uniformity = jnp.log(near / (n * (n - 1)))
    line = lax.broadcasted_iota(jnp.int32, values_ref.shape, 0)
    values_ref[...] = jnp.where(line == 0, loss, jnp.where(line == 1, alignment, uniformity))
    g_logits = (expo / total - picked) * (1.0 / (0.05 * n))
    g_unit = jnp.concatenate(
        [exact(g_logits, candidates, ((1,), (0,))), exact(g_logits, anchors, ((0,), (0,)))], axis=0
    )
    g_pooled = inv * (g_unit - unit * jnp.sum(g_unit * unit, axis=-1, keepdims=True))
    g_pre = (g_pooled * (1.0 - pooled * pooled)).astype(bf16)
    g_pre_ref[...] = g_pre
    line = lax.broadcasted_iota(jnp.int32, g_pre.shape, 0)
    mine = jnp.where(line == shift_ref[0] * n + shift_ref[1], g_pre.astype(f32), 0.0)
    mine = jnp.broadcast_to(jnp.sum(mine, axis=0, keepdims=True), (8, mine.shape[1])).astype(bf16)
    g_cls_ref[...] = dot_t(mine, pool_ref[...])


def loss_parts(shift, cls, pool_w, positive):
    rows, width = cls.shape
    return pl.pallas_call(
        loss_kernel,
        in_specs=[pl.BlockSpec(memory_space=pltpu.SMEM)] + [pl.BlockSpec(memory_space=pltpu.VMEM)] * 3,
        out_shape=[
            struct((8, 128), f32),
            struct((rows, width), bf16),
            struct((rows, width), bf16),
            struct((8, width), f32),
        ],
        compiler_params=params(16),
        cost_estimate=cost(2),
        name="contrast",
    )(shift, cls, pool_w, positive)


def feed_backward(
    half, side, g_parts, g_cls, normal2, inv2, keeps, gains, hidden, w_down, w_up, slope, h1_low, normal1, inv1, w_out
):
    rows, width = h1_low.shape
    hid = hidden.shape[1]
    wide = hid // GROUPS
    chunk = hid // 4
    deep = width // 8
    full = (rows, width)
    down = struct((GROUPS, 2, deep, 2 * wide), bf16)
    up = struct((2, width, chunk), bf16)
    narrow = struct((rows, width // 2), bf16)
    G, G_CLS, NORMAL2, INV2, KEEP, GAINS, HIDDEN, W_DOWN, W_UP, SLOPE, H1, NORMAL1, INV1, W_OUT = (
        0, 1, 2, 3, 4, 6, 7, 8, 9, 10, 11, 12, 13, 14,
    )
    D_SEND, D_KEEP, U_SEND, U_KEEP, UP_SUM, G_ATTN, OWN, PAIR_, SUMS = range(9)
    cuts = [slice(i * wide, (i + 2) * wide) for i in range(0, GROUPS, 2)]

    def body(scalars, reads, writes, turned, turned_h1, g_h2_ref, g_ff_ref):
        half, cls_side = scalars
        steps = []
        for who, ref in ((1 - half, U_SEND), (half, U_KEEP)):
            for b in (0, 1):
                steps.append((ref, b, pl.ds(pl.multiple_of((2 * b + who) * chunk, chunk), chunk)))
        first = (G, G_CLS, NORMAL2, INV2, GAINS, KEEP, KEEP + 1)
        for which in first:
            reads.start(which)
        reads.start(HIDDEN)
        reads.start(H1)
        for which in first:
            reads.wait(which)
        for c, (ref, b, at) in enumerate(steps):
            reads.start(W_DOWN, c, (at,))
            reads.start(SLOPE, c, (slice(None), at))
            reads.start(W_UP, c, (slice(None), at))
        for which in (NORMAL1, INV1, W_OUT):
            reads.start(which)
        got, buf = reads.buffers, writes.buffers
        g = jnp.concatenate([got[G][...], got[KEEP + 1][1]], axis=0).astype(f32)
        place = jnp.where(half == 0, cls_side * (rows // 2), rows)
        here = lax.broadcasted_iota(jnp.int32, g.shape, 0) == place
        g = g + jnp.where(here, got[G_CLS][0:1, :], 0.0)
        normal = got[NORMAL2][...].astype(f32)
        g_h2 = norm_back(g, normal, got[INV2][:, 0:1], got[GAINS][1:2, :])
        keep = jnp.concatenate([got[KEEP][...], got[KEEP + 1][0]], axis=0)
        g_ff = (g_h2 * (keep.astype(f32) * inv_keep)).astype(bf16)
        g_h2_ref[...] = g_h2
        g_ff_ref[...] = g_ff
        second = [jnp.sum(v, axis=0, keepdims=True) for v in (g * normal, g, g_ff.astype(f32))]
        turned[...] = g_ff.T.reshape(turned.shape)
        reads.wait(HIDDEN)
        reads.wait(H1)
        for who, ref in ((1 - half, D_SEND), (half, D_KEEP)):
            lhs = jnp.concatenate([turned[who], turned[who + 2]], axis=0)
            for c, at in enumerate(cuts):
                out = dot(lhs, got[HIDDEN][:, at]).astype(bf16)
                for i in (0, 1):
                    for s in (0, 1):
                        lines = out[2 * s * deep : 2 * (s + 1) * deep, i * wide : (i + 1) * wide]
                        buf[ref][2 * c + i, s] = jnp.concatenate([lines[:deep], lines[deep:]], axis=1)
            writes.start(ref)
        turned_h1[...] = got[H1][...].T
        for c in range(4):
            for which in (W_DOWN, SLOPE, W_UP):
                reads.wait(which, c)
        g = g_h2_ref[...]
        for c, (ref, b, at) in enumerate(steps):
            g_up = (dot_t(g_ff_ref[...], got[W_DOWN][at, :]) * got[SLOPE][:, at].astype(f32)).astype(bf16)
            buf[UP_SUM][:, at] = jnp.sum(g_up.astype(f32), axis=0, keepdims=True)
            buf[ref][b] = dot(turned_h1[...], g_up).astype(bf16)
            writes.start(ref, b, (b,))
            g = g + dot_t(g_up, got[W_UP][:, at])
        writes.start(UP_SUM)
        for which in (NORMAL1, INV1, W_OUT):
            reads.wait(which)
        normal = got[NORMAL1][...].astype(f32)
        g_attn = norm_back(g, normal, got[INV1][:, 0:1], got[GAINS][0:1, :]).astype(bf16)
        for who, ref in ((1 - half, PAIR_), (half, OWN)):
            w = jnp.concatenate([got[W_OUT][who], got[W_OUT][who + 2]], axis=0)
            buf[ref][...] = dot_t(g_attn, w).astype(bf16)
            writes.start(ref)
        buf[G_ATTN][...] = g_attn
        writes.start(G_ATTN)
        first = [jnp.sum(v, axis=0, keepdims=True) for v in (g * normal, g, g_attn.astype(f32))]
        zero = jnp.zeros((2, width), f32)
        buf[SUMS][...] = jnp.concatenate(
            [first[0], second[0], zero, first[1], second[2], second[1], first[2]], axis=0
        )
        writes.start(SUMS)

    return streamed(
        body,
        [half, side],
        [
            g_parts[0], g_cls, normal2, inv2, *keeps, gains, hidden, w_down, w_up, slope, h1_low, normal1, inv1, w_out,
        ],
        [
            down,
            down,
            up,
            up,
            struct((1, hid), f32),
            struct(full, bf16),
            narrow,
            narrow,
            struct((8, width), f32),
        ],
        [
            pltpu.VMEM((4, width // 4, rows), bf16),
            pltpu.VMEM((width, rows), bf16),
            pltpu.VMEM(full, f32),
            pltpu.VMEM(full, bf16),
        ],
        (25, 11),
        "feed_backward",
        20,
        limit=50,
        near=(1,),
    )


def out_backward(half, own, pair, g_attn):
    rows, width = g_attn.shape
    size = width // 4
    padded = -(-size // 128) * 128
    part = struct((2, width, padded), bf16)

    def body(scalars, reads, writes, ctx, cut):
        (half,) = scalars
        for which in range(3):
            reads.start(which)
        own_t, pair_t = reads.wait(0)[...].T, reads.wait(1)[...].T
        for b in (0, 1):
            lines = slice(b * size, (b + 1) * size)
            ctx[2 * b + half] = own_t[lines]
            ctx[2 * b + 1 - half] = pair_t[lines]
        g = reads.wait(2)
        for b in range(4):
            cut[b] = g[:, b * size : (b + 1) * size]
        lhs = ctx[...].reshape(4 * size, -1)
        for who, ref in ((1 - half, 0), (half, 1)):
            for b in (0, 1):
                writes.buffers[ref][b, :, :size] = dot(lhs, cut[2 * b + who]).astype(bf16)
                writes.buffers[ref][b, :, size:] = jnp.zeros((width, padded - size), bf16)
            writes.start(ref)

    return streamed(
        body,
        [half],
        [own, pair, g_attn],
        [part, part],
        [pltpu.VMEM((4, size, rows), bf16), pltpu.VMEM((4, rows, size), bf16)],
        (3, 2),
        "out_backward",
        4,
        limit=16,
        near=(2,),
        stay=(0, 1),
    )


def pick(values, index, axis):
    return lax.dynamic_index_in_dim(values, index, axis, keepdims=False)


def add_low(*parts):
    total = parts[0].astype(f32)
    for part in parts[1:]:
        total = total + part.astype(f32)
    return total.astype(bf16)


class Halving:
    def __init__(self, values, shape, names, order, place):
        self.values = [v.reshape(shape) for v in values]
        self.names, self.order, self.place = list(names), list(order), place

    def total(self):
        return self.values[0] if len(self.values) == 1 else add_low(*self.values)

    def cut(self):
        step = self.order.pop(0)
        axis = self.names.index(step)
        self.names.pop(axis)
        side, dp, bits = self.place
        if step == "side":
            bit, self.route = side, ("seq", CROSS)
        else:
            bit = (dp >> step) & 1
            self.route = ("dp", [(d, d ^ (1 << step)) for d in range(1 << bits)])
        halves = []
        for which in (1 - bit, bit):
            parts = [pick(v, which, axis) for v in self.values]
            halves.append(parts[0] if len(parts) == 1 else add_low(*parts))
        return halves

    def join(self, arrived, kept):
        self.values = [kept, arrived]


class Summing:
    def __init__(self, values, bits):
        self.values = values
        self.order = [("seq", PAIR), ("seq", CROSS)]
        self.order += [("dp", [(d, d ^ (1 << k)) for d in range(1 << bits)]) for k in range(bits)]

    def cut(self):
        self.route = self.order.pop(0)
        return self.values, None

    def join(self, arrived, kept):
        self.values = self.values + arrived


class Rows:
    def __init__(self, own, send, length):
        self.values, self.send, self.length, self.order = own, send, length, [PAIR, CROSS]

    def cut(self):
        self.route = ("seq", self.order.pop(0))
        if self.order:
            return self.send, self.values
        return self.values[self.length :].astype(bf16), self.values[: self.length]

    def join(self, arrived, kept):
        self.values = kept.astype(f32) + arrived.astype(f32) if self.order else (kept, arrived)


def advance(streams, *others):
    streams = [stream for stream in streams if stream.order]
    cuts = [stream.cut() for stream in streams]
    cuts, others = lax.optimization_barrier((cuts, others))
    for stream, (send, kept) in zip(streams, cuts):
        stream.join(lax.ppermute(send, *stream.route), kept)
    return others


class Tiled:
    def __init__(self, values, names, lines, order):
        self.values, self.names, self.lines, self.order = values, list(names), lines, list(order)

    def total(self):
        parts = [lax.slice_in_dim(v, at, at + self.lines, axis=0) for v, at, _ in self.values]
        return parts[0] if len(parts) == 1 else add_low(*parts)


class Shared:
    def __init__(self, values, lines, order):
        self.values, self.lines, self.order = values, lines, list(order)

    total = Tiled.total


def combine(bits_of, streams):
    streams = [stream for stream in streams if stream.order]
    arrays, cuts, links, close = [], [], {}, set()
    for stream in streams:
        step = stream.order.pop(0)
        if isinstance(stream, Shared):
            pre, half = 0, stream.lines
        elif step == "z":
            pre, half = -1, stream.lines
            for offset in (1, 2, 3):
                at = links.setdefault(f"z{offset}", 0)
                links[f"z{offset}"] += half
        else:
            axis = stream.names.index(step)
            stream.names.pop(axis)
            pre, half = 1 << axis, stream.lines << len(stream.names)
        if step != "z":
            at = links.setdefault(step, 0)
            links[step] += half
        loads = []
        for array, first, stride in stream.values:
            known = [i for i, a in enumerate(arrays) if a is array]
            loads.append((known[0] if known else len(arrays), first, stride))
            if not known:
                arrays.append(array)
            if array.shape[0] <= NEAR:
                close.add(loads[-1][0])
        cuts.append((step, at, pre, stream.lines, half, loads))
    steps = list(links)
    width = arrays[0].shape[1]

    def piece(load, pre, lines, half):
        which, first, stride = load
        if pre <= 0:
            return which, first, lines if pre == 0 else 4 * lines
        return (which, first, 2 * half) if stride == lines else (which, 0, 2 * half // lines * stride)

    fetched = list({piece(load, *c[2:5]) for c in cuts for load in c[5]})
    fetched.sort()

    def body(scalars, reads, writes):
        (place,) = scalars
        for key in fetched:
            reads.start(key[0], key, (pl.ds(key[1], key[2]),))
        for i, (step, at, pre, lines, half, loads) in enumerate(cuts):
            for load in loads:
                reads.wait(load[0], piece(load, pre, lines, half))
            if pre == -1:
                own = 2 * place[3] + place[2]
                for offset in range(4):
                    rows = []
                    for w, first, _ in loads:
                        start = pl.multiple_of(first + (own ^ offset) * lines, 16)
                        rows.append(reads.buffers[w][pl.ds(start, lines), :])
                    if offset:
                        out = steps.index(f"z{offset}")
                        writes.buffers[out][at : at + lines, :] = add_low(*rows)
                        writes.start(out, i, (pl.ds(at, lines),))
                    else:
                        writes.buffers[len(steps) + i][...] = add_low(*rows)
                        writes.start(len(steps) + i)
                continue
            bit = place[0 if step == "side" else step + 1]
            if pre == 0:
                total = add_low(*[reads.buffers[w][first : first + lines, :] for w, first, _ in loads])
                writes.buffers[steps.index(step)][at : at + lines, :] = total
                writes.buffers[len(steps) + i][...] = total
            post = half // lines // max(pre, 1)
            for p in range(pre):
                for out, base, which in ((steps.index(step), at, 1 - bit), (len(steps) + i, 0, bit)):
                    block = (2 * p + which) * post

                    def one(t, block=block, out=out, base=base + p * post * lines, loads=loads, lines=lines):
                        rows = []
                        for w, first, stride in loads:
                            start = pl.multiple_of(first + (block + t) * stride, 16)
                            rows.append(reads.buffers[w][pl.ds(start, lines), :])
                        total = rows[0] if len(rows) == 1 else add_low(*rows)
                        writes.buffers[out][pl.ds(pl.multiple_of(base + t * lines, 16), lines), :] = total

                    if post == 1:
                        one(0)
                    else:
                        pl.loop(0, post)(one)
            writes.start(steps.index(step), i, (pl.ds(at, half),))
            writes.start(len(steps) + i)

    small = sum(links.values()) <= 1024
    stay = set(range(len(steps) + len(cuts))) if small else ()
    outs = streamed(
        body,
        [bits_of],
        arrays,
        [struct((links[step], width), bf16) for step in steps] + [struct((c[4], width), bf16) for c in cuts],
        [],
        (len(fetched), sum(4 if c[2] == -1 else 2 for c in cuts)),
        "combine",
        4,
        limit=24,
        near=close,
        stay=stay,
    )
    sends = dict(zip(steps, outs))
    for stream, (step, at, _, _, _, _), kept in zip(streams, cuts, outs[len(steps) :]):
        came = ["z1", "z2", "z3"] if step == "z" else [step]
        stream.values = [(kept, 0, stream.lines)] + [(link, at, stream.lines) for link in came]
    return sends


def exchange(streams, sends, bits):
    arrived = {}
    for step, send in sends.items():
        if step == "side":
            arrived[step] = lax.ppermute(send, "seq", CROSS)
        else:
            apart = 2 * int(step[1]) if isinstance(step, str) else 1 << step
            arrived[step] = lax.ppermute(send, "dp", [(d, d ^ apart) for d in range(1 << bits)])
    for stream in streams:
        stream.values = [(arrived.get(v, v) if isinstance(v, (str, int)) else v, *at) for v, *at in stream.values]


def hold(small, streams):
    arrays = arrays_of(streams)
    replace(streams, arrays, advance(small, *arrays))


def arrays_of(streams):
    return list({id(v): v for stream in streams for v, _, _ in stream.values}.values())


def replace(streams, arrays, held):
    where = {id(v): h for v, h in zip(arrays, held)}
    for stream in streams:
        stream.values = [(where[id(v)], *at) for v, *at in stream.values]


def tie(streams, *others):
    arrays = arrays_of(streams)
    replace(streams, arrays, lax.optimization_barrier((*arrays, *others)))


def gather_step(values, at, bits):
    count = 4 << bits

    def partner(device, offset):
        for k in (0, 1):
            if offset >> k & 1 and at + k <= bits:
                device ^= 2 if at + k == 0 else 4 << (at + k - 1)
        return device

    offsets = range(1, 4 if at + 1 <= bits else 2)
    parts = [
        lax.ppermute(values, ("dp", "seq"), [(d, partner(d, offset)) for d in range(count)])
        for offset in offsets
    ]
    return jnp.concatenate([values] + parts, axis=0)


def own_heads(values, half, axis):
    size = values.shape[axis] // 4
    shape = values.shape[:axis] + (2, 2, size) + values.shape[axis + 1 :]
    out = pick(values.reshape(shape), half, axis + 1)
    return out.reshape(values.shape[:axis] + (2 * size,) + values.shape[axis + 1 :])


def after(value, *others):
    return lax.optimization_barrier((value,) + others)[0]


def body(
    embeds,
    lengths,
    drop_in,
    drop_ff,
    positive,
    w_qkv,
    w_out,
    w_up,
    w_down,
    pool_w,
    gains,
    biases,
    up_bias,
    out_grad,
):
    _, _, length, width = drop_in.shape
    n_dp = lax.axis_size("dp")
    bits = n_dp.bit_length() - 1
    seq = lax.axis_index("seq")
    dp = lax.axis_index("dp")
    side, half = seq // 2, seq % 2
    half1 = half.astype(jnp.int32).reshape(1)
    side1 = side.astype(jnp.int32).reshape(1)
    first_side = side == 0
    place_keys = jnp.stack([seq.astype(jnp.int32), lengths[0]])

    token = embeds[0]
    masks_in = (pick(drop_in, side, 0)[0], pick(drop_in, 1 - side, 0)[0])
    kept_send = token * masks_in[1].astype(bf16)
    kept_cross = lax.ppermute(kept_send, "seq", CROSS)
    kept_local = token * masks_in[0].astype(bf16)
    kept_local_pair = lax.ppermute(kept_local, "seq", PAIR)

    w_own, b_own, qkv_local = project_local(half1, kept_local, kept_local_pair, w_qkv, biases)
    rest = jnp.stack([pick(drop_ff, 1 - side, 0)[0].astype(bf16), pick(out_grad, 1 - side, 0)[0]])
    kept_cross, w_own, rest, place_keys = lax.optimization_barrier((kept_cross, w_own, rest, place_keys))
    kept_cross_pair = lax.ppermute(kept_cross, "seq", PAIR)
    qkv_cross = project_cross(kept_cross, kept_cross_pair, w_own, b_own)
    kept = (kept_local, kept_local_pair, kept_cross, kept_cross_pair)
    rest = lax.ppermute(after(rest, kept_cross), "seq", CROSS)
    keeps = (pick(drop_ff, side, 0)[0].astype(bf16), rest)
    g_parts = (pick(out_grad, side, 0)[0], rest)
    w_out4 = w_out.reshape(4, width // 4, width)
    up_bias2 = up_bias[None]

    own, send, lse = attend_forward(place_keys, qkv_local, qkv_cross)
    pair = lax.ppermute(send, "seq", PAIR)
    hidden, slope, h1_low, normal1, inv1, normal2, inv2, mixed_local, mixed_cross = layer_forward(
        half1, own, pair, (kept_local, kept_cross), keeps, w_out4, w_up, w_down, gains, biases, up_bias2
    )

    first = jnp.where(first_side, mixed_local[:1], mixed_cross[:1])
    rel = first
    for at in range(0, bits + 1, 2):
        rel = gather_step(rel, at, bits)
    shift = jnp.stack([side, dp]).astype(jnp.int32)
    positive_col = jnp.broadcast_to(positive[:, None], (n_dp, 128))
    _, _, _, g_cls = loss_parts(shift, rel, pool_w, positive_col)
    mixed_back = lax.ppermute(after(mixed_cross, g_cls), "seq", CROSS)

    down_send, down_keep, up_send, up_keep, up_sum, g_attn, g_own, g_send, sums = feed_backward(
        half1,
        side1,
        g_parts,
        g_cls,
        normal2,
        inv2,
        keeps,
        gains,
        hidden,
        w_down,
        w_up,
        slope,
        h1_low,
        normal1,
        inv1,
        w_out4,
    )
    g_attn, g_send, down_send, up_send, mixed_back = lax.optimization_barrier(
        (g_attn, g_send, down_send, up_send, mixed_back)
    )
    g_pair = lax.ppermute(g_send, "seq", PAIR)

    dims = (2,) * bits
    place = (side, dp, bits)
    dp_names = list(range(bits - 1, -1, -1))
    names = ["side"] + dp_names
    low = list(range(1, bits))
    sub = n_dp // GROUPS
    deep = width // n_dp
    cut = width // 4

    tiled = deep % 16 == 0
    down_pair = lax.ppermute(down_send, "seq", PAIR)
    up_pair = lax.ppermute(up_send, "seq", PAIR)
    side_first, dp_first = ["side", 0] + low, [0, "side"] + low
    low_first = low[:1] + ["side", 0] + low[1:]
    if tiled:

        def flat(values):
            return values.reshape(-1, width)

        bits_of = jnp.stack([side] + [(dp >> k) & 1 for k in range(bits)]).astype(jnp.int32)
        most = deep * 2 // 3

        def split(keep, pair, axes, order, rest):
            values = [(flat(keep), 0, deep), (flat(pair), 0, deep)]
            later = [(v, most, stride) for v, _, stride in values]
            return [Tiled(values, axes, most, order), Tiled(later, axes, deep - most, rest)]

        ups = split(up_keep, up_pair, names, side_first, low + ["side", 0])
        downs = split(down_keep, down_pair, dp_names + ["side"], dp_first, low + [0, "side"])
        early = [ups[0], downs[0], ups[1], downs[1]]
        out_send, out_keep = out_backward(half1, own, pair, g_attn)
        outs = (out_keep, lax.ppermute(out_send, "seq", PAIR))
        sends = combine(bits_of, early)
        rel_pair = lax.ppermute(rel, "seq", [(0, 1), (2, 3)])
        g_own, g_pair, rel_pair, *held = lax.optimization_barrier((g_own, g_pair, rel_pair, *sends.values()))
        exchange(early, dict(zip(sends, held)), bits)
        *grads, swapped = attend_backward(place_keys, qkv_local, qkv_cross, own, send, g_own, g_pair, lse)
        swapped = lax.ppermute(swapped, "seq", PAIR)
        tie(early, *grads)
        sends = combine(bits_of, early)
        grads = lax.optimization_barrier((*grads, *sends.values()))[:3]
        exchange(early, sends, bits)
        splits = ((0, deep // 2), (1, deep // 2))
        orders = (["side", 0, "z"], [0, "side", "z"])
        g_x, g_x_send, sums, *parts = project_backward(
            half1, bits_of, grads, swapped, kept, outs, w_own, g_attn, sums, up_sum, splits, deep
        )
        qkv = []
        for (_, take), order, send_part, keep_part in zip(splits, orders, parts[::2], parts[1::2]):
            left = [name for name in names if name != order[0]]
            stream = Tiled([(keep_part, 0, take), (order[0], 0, take)], left, take, order[1:])
            exchange([stream], {order[0]: send_part}, bits)
            qkv.append(stream)
        small = [Rows(g_x, g_x_send, length)]
        advance(small)
        sums = sums.astype(bf16)
        shared = Shared(
            [(sums, 0, 16), (lax.ppermute(sums, "seq", PAIR), 0, 16)], 16, low[:1] + ["side", 0]
        )
        tie(early, *parts)
        sends = combine(bits_of, early[:2] + [shared])
        exchange(early[:2] + [shared], sends, bits)
        streams = qkv + early + [shared]
        sends = combine(bits_of, streams)
        exchange(streams, sends, bits)
        rel = after(jnp.where(half == 0, rel, rel_pair), *sends.values())
        found = loss_parts(shift, rel, pool_w, positive_col)
        tie(streams, found[0])
    else:
        sub = n_dp // GROUPS

        def turned(values):
            values = values.reshape(GROUPS, 2, width // 8, 2, sub, -1)
            return values.transpose(0, 4, 1, 3, 2, 5)

        down = Halving(
            [turned(down_keep), turned(down_pair)], dims + (2, cut, -1), dp_names + ["side"], dp_first, place
        )
        up = Halving([up_keep, up_pair], (2,) + dims + (deep, -1), names, side_first, place)
        out_send, out_keep = out_backward(half1, own, pair, g_attn)
        outs = (out_keep, lax.ppermute(out_send, "seq", PAIR))
        g_own, g_pair = advance([up, down], g_own, g_pair)
        *grads, swapped = attend_backward(place_keys, qkv_local, qkv_cross, own, send, g_own, g_pair, lse)
        swapped = lax.ppermute(swapped, "seq", PAIR)
        g_x, g_x_send, sums, part = project_backward(
            half1, place_keys, grads, swapped, kept, outs, w_own, g_attn, sums, up_sum, (), 0
        )
        qkv = [Halving([part], (2,) + dims + (deep, width), names, side_first, place)]
        streams = qkv + [up, down]
        small = [Summing(sums, bits), Rows(g_x, g_x_send, length)]
    while any(stream.order for stream in streams + small):
        if tiled:
            hold(small, streams)
            if any(stream.order for stream in streams):
                sends = combine(bits_of, streams)
                exchange(streams, sends, bits)
        else:
            advance(streams + small)
    if not tiled:
        rel = jnp.where(half == 0, rel, lax.ppermute(rel, "seq", [(0, 1), (2, 3)]))
        found = loss_parts(shift, rel, pool_w, positive_col)
    if tiled:
        sums = shared.total()
        shared.values = [(sums, 0, 16), (lax.ppermute(sums, "dp", [(d, d ^ 4) for d in range(n_dp)]), 0, 16)]
        tie(qkv, shared.total())
    values, cls_all, g_pre, _ = found
    pool_rows, pool_cols = width // n_dp, width // 4
    grad_pool = t_dot(
        lax.dynamic_slice_in_dim(cls_all, dp * pool_rows, pool_rows, 1),
        lax.dynamic_slice_in_dim(g_pre, seq * pool_cols, pool_cols, 1),
    )
    mixed_out = jnp.stack(
        [jnp.where(first_side, mixed_local, mixed_back), jnp.where(first_side, mixed_back, mixed_local)]
    )[:, None]
    total = shared.total().astype(f32) if tiled else small[0].values
    g_x, g_x_cross = small[-1].values
    if tiled:
        grad_up = jnp.concatenate([stream.total() for stream in ups], axis=0).astype(f32)
        grad_down = jnp.concatenate([stream.total() for stream in downs], axis=0)
    else:
        grad_up = up.total().astype(f32)
        grad_down = down.total()
    if tiled:
        grad_down = grad_down.reshape(deep, 2, -1).swapaxes(0, 1).reshape(cut, -1)
    grad_down = grad_down.astype(f32).T
    sum_qkv = jnp.concatenate([stream.total() for stream in qkv], axis=0)
    grad_out = sum_qkv[:, 3 * cut :].astype(f32)
    grad_qkv = sum_qkv[:, : 3 * cut].astype(f32)
    embeds_grad = (g_x * masks_in[0].astype(f32) + g_x_cross.astype(f32) * masks_in[1].astype(f32)) * inv_keep
    return (
        mixed_out,
        embeds_grad[None],
        grad_qkv,
        grad_out,
        grad_up,
        grad_down,
        grad_pool,
        total[0:2],
        total[2:7],
        total[7],
        total[8 : 8 + up_bias.shape[0] // width].reshape(-1),
        values[0, 0],
        values[1, 0],
        values[2, 0],
    )


def solution(mesh):
    tokens = P(None, "dp", "seq", None)
    placed = (P("dp", "seq", None), P("dp"), tokens, tokens) + (P(),) * 9 + (tokens,)
    weight = P("dp", "seq")
    return jax.shard_map(
        body,
        mesh=mesh,
        in_specs=placed,
        out_specs=(tokens, P("dp", "seq", None)) + (weight,) * 5 + (P(),) * 7,
        check_vma=False,
    )
```

```python
import functools
import math

import jax
import jax.numpy as jnp
from jax import lax
from jax.experimental import pallas as pl
from jax.experimental.pallas import tpu as pltpu
from jax.sharding import PartitionSpec as P

HEAD = 64
keep_rate = 0.9
inv_keep = 1.0 / keep_rate
highest = lax.Precision.HIGHEST
f32 = jnp.float32
bf16 = jnp.bfloat16

CROSS = [(i, i ^ 2) for i in range(4)]
PAIR = [(i, i ^ 1) for i in range(4)]
GROUPS = 8
NEAR = 2048


def cost(time):
    return pl.CostEstimate(flops=time * 2_000_000_000, bytes_accessed=1 << 20, transcendentals=0)

CHUNK = 768


def dot(a, b):
    return jnp.dot(a, b, preferred_element_type=f32)


def dot_t(a, b):
    return lax.dot_general(a, b, (((1,), (1,)), ((), ())), preferred_element_type=f32)


def t_dot(a, b):
    return lax.dot_general(a, b, (((0,), (0,)), ((), ())), preferred_element_type=f32)


def whole(shape):
    return pl.BlockSpec(shape, lambda *_: (0,) * len(shape))


def struct(shape, dtype):
    return jax.ShapeDtypeStruct(shape, dtype)


def hbm(x):
    return pltpu.with_memory_space_constraint(x, pltpu.HBM)


def params(limit):
    return pltpu.CompilerParams(vmem_limit_bytes=limit << 20)


ALL = (slice(None),)


class Stream:
    def __init__(self, refs, buffers, sems, out):
        self.refs, self.buffers, self.sems, self.out = refs, buffers, sems, out
        self.count, self.copies = 0, {}

    def start(self, which, key=0, at=ALL):
        if self.refs[which] is self.buffers[which]:
            return
        ref, buffer = self.refs[which].at[at], self.buffers[which].at[at]
        source, target = (buffer, ref) if self.out else (ref, buffer)
        copy = pltpu.make_async_copy(source, target, self.sems.at[self.count])
        copy.start()
        self.count += 1
        self.copies[which, key] = copy

    def wait(self, which, key=0):
        copy = self.copies.pop((which, key), None)
        if copy is not None:
            copy.wait()
        return self.buffers[which]

    def drain(self):
        for which, key in list(self.copies):
            self.wait(which, key)


def streamed(body, scalars, ins, outs, scratch, copies, name, time, limit=56, near=(), stay=()):
    n_s, n_i, n_o = len(scalars), len(ins), len(outs)
    far = [i for i in range(n_i) if i not in near]
    leave = [i for i in range(n_o) if i not in stay]

    def kernel(*refs):
        cuts = [n_s, n_i, n_o, len(far), len(leave), len(scratch), 1, 1]
        parts, at = [], 0
        for cut in cuts:
            parts.append(refs[at : at + cut])
            at += cut
        buffers = list(parts[1])
        for i, buffer in zip(far, parts[3]):
            buffers[i] = buffer
        reads = Stream(parts[1], buffers, parts[6][0], False)
        results = list(parts[2])
        for i, buffer in zip(leave, parts[4]):
            results[i] = buffer
        writes = Stream(parts[2], results, parts[7][0], True)
        body([r[0] if r.shape[0] == 1 else r for r in parts[0]], reads, writes, *parts[5])
        reads.drain()
        writes.drain()

    smem, home = pl.BlockSpec(memory_space=pltpu.SMEM), pl.BlockSpec(memory_space=pltpu.HBM)
    close = pl.BlockSpec(memory_space=pltpu.VMEM)
    return pl.pallas_call(
        kernel,
        in_specs=[smem] * n_s + [close if i in near else home for i in range(n_i)],
        out_specs=[close if i in stay else home for i in range(n_o)],
        out_shape=[o if i in stay else pltpu.HBM(o.shape, o.dtype) for i, o in enumerate(outs)],
        scratch_shapes=[pltpu.VMEM(x.shape, x.dtype) for x in [ins[i] for i in far] + [outs[i] for i in leave]]
        + list(scratch)
        + [pltpu.SemaphoreType.DMA((max(copies[0], 1),)), pltpu.SemaphoreType.DMA((copies[1],))],
        compiler_params=params(limit),
        cost_estimate=cost(time),
        name=name,
    )(*scalars, *[x if i in near else hbm(x) for i, x in enumerate(ins)])


def one_head(block, head, extra):
    lane = lax.broadcasted_iota(jnp.int32, block.shape, 1)
    mine = (lane >= HEAD) if head else (lane < HEAD)
    out = jnp.where(mine, block, jnp.zeros_like(block))
    if extra is not None:
        out = jnp.where(lane == (0 if head else HEAD), extra, out)
    return out


def key_mask(place_ref, rows):
    quarter = rows // 4
    parts = []
    for b in range(4):
        at = lax.broadcasted_iota(jnp.int32, (quarter, 128), 0) + (place_ref[0] ^ b) * quarter
        parts.append(jnp.where(at < place_ref[1], 0.0, -1e30).astype(bf16))
    return jnp.concatenate(parts, axis=0)


def forward_kernel(place_ref, ql_ref, qc_ref, kl_ref, kc_ref, vl_ref, vc_ref, own_ref, send_ref, lse_ref):
    key = jnp.concatenate([kl_ref[...], kc_ref[...]], axis=0)
    mask = key_mask(place_ref, key.shape[0])
    keys = [one_head(key, h, mask) for h in (0, 1)]
    value_t = jnp.concatenate([vl_ref[...], vc_ref[...]], axis=0).T
    one = jnp.ones((), bf16)
    rows = ql_ref.shape[0]
    cut = rows // 2
    units = [(part, c, h) for part in (0, 1) for c in (0, 1) for h in (0, 1)]
    scores, weights = [], []
    for part, c, h in units:
        q = (ql_ref, qc_ref)[part][c * cut : (c + 1) * cut, :] * jnp.asarray(1.0 / math.sqrt(HEAD), bf16)
        scores.append(dot_t(keys[h], one_head(q, h, one)))
    for (part, c, h), s in zip(units, scores):
        top = jnp.max(s, axis=0, keepdims=True)
        p = jnp.exp(s - top)
        total = jnp.sum(p, axis=0, keepdims=True)
        start = part * rows + c * cut
        lse_ref[0, h : h + 1, start : start + cut] = top + jnp.log(total)
        weights.append((p.astype(bf16), total))
    outs = [
        dot(value_t[HEAD * h : HEAD * (h + 1), :], p) * (1.0 / total)
        for (part, c, h), (p, total) in zip(units, weights)
    ]
    for i in range(0, len(units), 2):
        part, c, _ = units[i]
        out = jnp.concatenate(outs[i : i + 2], axis=0).T.astype(bf16)
        (own_ref, send_ref)[c][part * cut : (part + 1) * cut, :] = out


def attend_forward(place, qkv_local, qkv_cross):
    rows, pairs = qkv_local.shape[0], qkv_local.shape[1] // 384

    def block(offset):
        return [pl.BlockSpec((rows, 128), lambda i: (0, i + offset))] * 2

    return pl.pallas_call(
        forward_kernel,
        grid=(pairs,),
        in_specs=[pl.BlockSpec(memory_space=pltpu.SMEM)] + block(0) + block(pairs) + block(2 * pairs),
        out_specs=block(0) + [pl.BlockSpec((1, 2, 2 * rows), lambda i: (i, 0, 0))],
        out_shape=[
            pltpu.HBM((rows, pairs * 128), bf16),
            pltpu.HBM((rows, pairs * 128), bf16),
            pltpu.HBM((pairs, 2, 2 * rows), f32),
        ],
        compiler_params=params(56),
        cost_estimate=cost(13),
        name="attend_forward",
    )(place, *(hbm(qkv_local), hbm(qkv_cross)) * 3)


def backward_kernel(
    place_ref,
    ql_ref,
    qc_ref,
    kl_ref,
    kc_ref,
    vl_ref,
    vc_ref,
    o0,
    o1,
    g0,
    g1,
    lse_ref,
    dq_ref,
    dk_ref,
    dv_ref,
    swap_ref,
    dk_acc,
    dv_acc,
):
    chunk = ql_ref.shape[0]
    scale = 1.0 / math.sqrt(HEAD)
    key = jnp.concatenate([kl_ref[...], kc_ref[...]], axis=0)
    mask = key_mask(place_ref, key.shape[0])
    keys = [one_head(key, h, mask) for h in (0, 1)]
    key_t = key.T
    value = jnp.concatenate([vl_ref[...], vc_ref[...]], axis=0)
    one = jnp.ones((), bf16)
    for c, q_ref in enumerate((ql_ref, qc_ref)):
        at = slice(c * chunk, (c + 1) * chunk)
        half = slice(c * chunk // 2, (c + 1) * chunk // 2)
        out = jnp.concatenate([o0[half, :], o1[half, :]], axis=0)
        do = jnp.concatenate([g0[half, :], g1[half, :]], axis=0)
        q = q_ref[...] * jnp.asarray(scale, bf16)
        prod_t = (do.astype(f32) * out.astype(f32)).T
        ps, dss, dos, qs, dq_t = [], [], [], [], []
        for h in (0, 1):
            rows = slice(HEAD * h, HEAD * (h + 1))
            s = dot_t(keys[h], one_head(q, h, one))
            p = jnp.exp(s - lse_ref[0, h : h + 1, at])
            do_h = one_head(do, h, None)
            dp = dot_t(value, do_h)
            delta = jnp.sum(prod_t[rows, :], axis=0, keepdims=True)
            ds = (p * (dp - delta)).astype(bf16)
            ps.append(p.astype(bf16))
            dss.append(ds)
            dos.append(do_h)
            qs.append(one_head(q, h, None))
            dq_t.append(dot(key_t[rows, :], ds))
        dv_c = dot(jnp.concatenate(ps, 1), jnp.concatenate(dos, 0))
        dk_c = dot(jnp.concatenate(dss, 1), jnp.concatenate(qs, 0))
        if c == 0:
            dv_acc[...] = dv_c
            dk_acc[...] = dk_c
        else:
            dv_ref[...] = (dv_acc[...] + dv_c).astype(bf16)
            dk_ref[...] = (dk_acc[...] + dk_c).astype(bf16)
        dq_ref[at, :] = (jnp.concatenate(dq_t, 0).T * scale).astype(bf16)

    step = pl.program_id(0)
    even = place_ref[0] % 2 == 0
    lane = lax.broadcasted_iota(jnp.int32, dq_ref.shape, 1) + 128 * step
    early = jnp.where(even, dk_ref[...], dq_ref[...])
    late = jnp.where(even, dv_ref[...], dk_ref[...])
    swap_ref[...] = jnp.where(lane < 64 * pl.num_programs(0), early, late)


def attend_backward(place, qkv_local, qkv_cross, own, send, g_own, g_pair, lse):
    rows, pairs = qkv_local.shape[0], qkv_local.shape[1] // 384

    def block(offset):
        return [pl.BlockSpec((rows, 128), lambda i: (0, i + offset))] * 2

    return pl.pallas_call(
        backward_kernel,
        grid=(pairs,),
        in_specs=[pl.BlockSpec(memory_space=pltpu.SMEM)]
        + block(0)
        + block(pairs)
        + block(2 * pairs)
        + block(0) * 2
        + [pl.BlockSpec((1, 2, 2 * rows), lambda i: (i, 0, 0))],
        out_specs=[pl.BlockSpec((2 * rows, 128), lambda i: (0, i))] * 4,
        out_shape=[struct((2 * rows, pairs * 128), bf16)] * 4,
        scratch_shapes=[pltpu.VMEM((2 * rows, 128), f32)] * 2,
        compiler_params=params(32),
        cost_estimate=cost(20),
        name="attend_backward",
    )(place, *[hbm(x) for x in (qkv_local, qkv_cross) * 3 + (own, send, g_own, g_pair, lse)])


def project_backward(half, bits_of, grads, swapped, kept, outs, w_own, g_attn, sums, up_sum, splits, lines):
    rows, width = g_attn.shape
    n, narrow = grads[0].shape
    quarter = n // 4
    cut = width // 4
    many = up_sum.shape[1] // width
    GRADS, KEPT, OUTS, W_OWN, G_ATTN, SUMS_IN, UP_SUM, SWAPPED = 0, 3, 7, 9, 10, 11, 12, 13
    OWN, SEND, SUMS, FIRST = range(4)
    if lines:
        weights = [(width // lines * take, width) for _, take in splits]
        results = [struct(shape, bf16) for shape in weights for _ in (0, 1)]
    else:
        results = [struct((2, width, width), bf16)]

    def body(scalars, reads, writes):
        half, bits_ref = scalars
        for which in (KEPT, KEPT + 1, KEPT + 2, KEPT + 3, 0, 1, 2, SWAPPED, OUTS, OUTS + 1, W_OWN, G_ATTN, SUMS_IN, UP_SUM):
            reads.start(which)
        buf = writes.buffers
        x = jnp.concatenate([reads.wait(KEPT + i)[...] for i in range(4)], axis=0)
        x_t = (x.astype(f32) * inv_keep).astype(bf16).T
        for which in (0, 1, 2, SWAPPED, OUTS, OUTS + 1):
            reads.wait(which)
        q, k, v = (reads.buffers[GRADS + i] for i in range(3))
        came = jnp.concatenate(
            [reads.buffers[SWAPPED][b * quarter : (b + 1) * quarter, :] for b in (1, 0, 3, 2)], axis=0
        )
        even = half == 0
        columns = (
            jnp.concatenate(
                [
                    jnp.where(even, q[:, :cut], q[:, cut:]),
                    came[:, :cut],
                    jnp.where(even, q[:, cut:], k[:, :cut]),
                ],
                axis=1,
            ),
            jnp.concatenate(
                [
                    jnp.where(even, k[:, cut:], v[:, :cut]),
                    came[:, cut:],
                    jnp.where(even, v[:, :cut], v[:, cut:]),
                ],
                axis=1,
            ),
        )
        for side in (0, 1):
            out = add_low(reads.buffers[OUTS][side, :, :cut], reads.buffers[OUTS + 1][side, :, :cut])
            part = jnp.concatenate([dot(x_t, columns[side]).astype(bf16), out], axis=1)
            if not lines:
                buf[FIRST][side] = part
                continue
            blocks = width // lines
            done = 0
            for i, (bit, take) in enumerate(splits):
                block = part.reshape(blocks, lines, width)[:, done : done + take]
                done += take
                target, kept = buf[FIRST + 2 * i], buf[FIRST + 2 * i + 1]
                if bit == 0:
                    block = block.reshape(blocks * take, width)

                    @pl.when(bits_ref[0] == side)
                    def _(block=block, kept=kept):
                        kept[...] = block

                    @pl.when(bits_ref[0] != side)
                    def _(block=block, target=target):
                        target[...] = block

                    continue
                post = 1 << bit - 1
                block = block.reshape(blocks // (2 * post), 2, post * take, width)
                size = blocks * take // 2
                spot = slice(side * size, (side + 1) * size)
                for value in (0, 1):
                    piece = block[:, value].reshape(size, width)

                    @pl.when(bits_ref[bit] == value)
                    def _(piece=piece, kept=kept, spot=spot):
                        kept[spot, :] = piece

                    @pl.when(bits_ref[bit] != value)
                    def _(piece=piece, target=target, spot=spot):
                        target[spot, :] = piece

        for i in range(len(results)):
            writes.start(FIRST + i)
        for which in (W_OWN, G_ATTN, SUMS_IN, UP_SUM):
            reads.wait(which)
        w = reads.buffers[W_OWN]
        for which, ref in ((1, SEND), (0, OWN)):
            total = None
            for i in range(3):
                g = reads.buffers[GRADS + i]
                g = jnp.concatenate(
                    [g[(which + b) * quarter : (which + b + 1) * quarter, :] for b in (0, 2)], axis=0
                )
                part = dot_t(g, w[:, i * narrow : (i + 1) * narrow])
                total = part if total is None else total + part
            if which == 0:
                total = total + reads.buffers[G_ATTN][...].astype(f32)
            buf[ref][...] = total.astype(bf16)
            writes.start(ref)
        buf[SUMS][0:8, :] = reads.buffers[SUMS_IN][...]
        tail = [reads.buffers[UP_SUM][:, i * width : (i + 1) * width] for i in range(many)]
        buf[SUMS][8:, :] = jnp.concatenate(tail + [jnp.zeros((8 - many, width), f32)], axis=0)
        for line, which in ((2, 0), (3, 2)):
            total = jnp.sum(reads.buffers[which][...].astype(f32), axis=0, keepdims=True)
            for b in (0, 1):
                block = total[:, b * cut : (b + 1) * cut]
                for who in (0, 1):
                    at = (2 * b + who) * cut
                    buf[SUMS][line : line + 1, at : at + cut] = jnp.where(half == who, block, jnp.zeros_like(block))
        writes.start(SUMS)

    return streamed(
        body,
        [half, bits_of],
        [*grads, *kept, *outs, w_own, g_attn, sums, up_sum, swapped],
        [struct((rows, width), bf16), struct((rows, width), bf16), struct((16, width), f32)] + results,
        [],
        (14, 3 + len(results)),
        "project_backward",
        10,
        limit=36,
        near=(0, 1, 2, 7, 8, 13),
        stay=range(3 + len(results)) if lines else (),
    )


def project_local(half, own, pair, w_qkv, biases):
    rows, width = own.shape
    cut = width // 4

    def body(scalars, reads, writes, bias):
        (half,) = scalars
        for which in (2, 3, 0, 1):
            reads.start(which)
        w, b = reads.wait(2), reads.wait(3)
        w_own, b_own = writes.buffers[0], writes.buffers[1]
        for who in (0, 1):

            @pl.when(half == who)
            def _(who=who):
                for kind in range(3):
                    base = kind * width
                    lines = [slice(base + (who + 2 * i) * cut, base + (who + 2 * i + 1) * cut) for i in (0, 1)]
                    target = slice(kind * 2 * cut, (kind + 1) * 2 * cut)
                    w_own[:, target] = jnp.concatenate([w[:, line] for line in lines], axis=1)
                    if kind == 1:
                        b_own[:, target] = jnp.zeros((8, 2 * cut), f32)
                    else:
                        row = b[kind // 2 : kind // 2 + 1, :]
                        row = jnp.concatenate([row[:, line.start - base : line.stop - base] for line in lines], axis=1)
                        b_own[:, target] = jnp.broadcast_to(row, (8, 2 * cut))

        writes.start(0)
        writes.start(1)
        x = jnp.concatenate([reads.wait(0)[...], reads.wait(1)[...]], axis=0)
        x = (x.astype(f32) * inv_keep).astype(bf16)
        writes.buffers[2][...] = (dot(x, w_own[...]) + b_own[0:1, :]).astype(bf16)
        writes.start(2)

    return streamed(
        body,
        [half],
        [own, pair, w_qkv, biases],
        [struct((width, 6 * cut), bf16), struct((8, 6 * cut), f32), struct((2 * rows, 6 * cut), bf16)],
        [pltpu.VMEM((8, 128), f32)],
        (4, 3),
        "project_local",
        5,
        limit=24,
        near=(0, 1),
        stay=(0, 1),
    )


def project_cross(own, pair, w_own, b_own):
    rows = own.shape[0]

    def body(scalars, reads, writes):
        for which in range(4):
            reads.start(which)
        x = jnp.concatenate([reads.wait(0)[...], reads.wait(1)[...]], axis=0)
        x = (x.astype(f32) * inv_keep).astype(bf16)
        w, b = reads.wait(2), reads.wait(3)
        writes.buffers[0][...] = (dot(x, w[...]) + b[0:1, :]).astype(bf16)
        writes.start(0)

    return streamed(
        body,
        [],
        [own, pair, w_own, b_own],
        [struct((2 * rows, w_own.shape[1]), bf16)],
        [],
        (4, 1),
        "project_cross",
        4,
        limit=20,
        near=(0, 1, 2, 3),
    )[0]


def norm_parts(values):
    mean = jnp.mean(values, axis=-1, keepdims=True)
    centred = values - mean
    inv = lax.rsqrt(jnp.mean(centred * centred, axis=-1, keepdims=True) + 1e-06)
    return centred * inv, inv


def norm_back(g, normal, inv, gain):
    a = g * gain
    return (
        a - jnp.mean(a, axis=-1, keepdims=True) - normal * jnp.mean(a * normal, axis=-1, keepdims=True)
    ) * inv


def gelu_parts(u):
    e = jnp.exp(-0.5 * u * u)
    t = 1.0 / (1.0 + (0.3275911 / math.sqrt(2.0)) * jnp.abs(u))
    poly = 0.5 * 1.061405429
    for a in (-1.453152027, 1.421413741, -0.284496736, 0.254829592):
        poly = poly * t + 0.5 * a
    tail = poly * t * e
    phi = jnp.where(u < 0, tail, 1.0 - tail)
    return u * phi, phi + u * e * (1.0 / math.sqrt(2.0 * math.pi))


def layer_forward(half, own, pair, kept, keep, w_out, w_up, w_down, gains, biases, up_bias):
    rows, width = kept[0].shape
    hid = w_up.shape[1]
    parts = hid // width
    tile = (rows, width)
    full = (2 * rows, width)
    cuts = [slice(c * width, (c + 1) * width) for c in range(parts)]
    OWN, PAIR_, KEPT, KEEP, W_OUT, W_UP, W_DOWN, GAINS, BIASES, UP_BIAS = 0, 1, 2, 4, 6, 7, 8, 9, 10, 11
    HIDDEN, SLOPE, H1_LOW, NORMAL1, INV1, NORMAL2, INV2, MIXED = range(8)

    def body(scalars, reads, writes, h1):
        (half,) = scalars
        for which in (OWN, PAIR_, W_OUT, BIASES, KEPT, KEPT + 1, GAINS, UP_BIAS):
            reads.start(which)
        def fetch(c):
            reads.start(W_UP, c, (slice(None), cuts[c]))
            reads.start(W_DOWN, c, (cuts[c],))

        fetch(0)
        own, pair, w_out = (reads.wait(w)[...] for w in (OWN, PAIR_, W_OUT))
        for c in range(1, parts):
            fetch(c)
        reads.start(KEEP)
        reads.start(KEEP + 1, 0, (0,))
        biases = reads.wait(BIASES)
        half = jnp.int32(half)

        def mine(who):
            w = reads.buffers[W_OUT]
            return jnp.concatenate([w[who], w[who + 2]], axis=0)

        attn = dot(own, mine(half)) + dot(pair, mine(1 - half)) + biases[2:3, :]
        xin = jnp.concatenate([reads.wait(KEPT)[...], reads.wait(KEPT + 1)[...]], axis=0)
        normal, inv = norm_parts(xin.astype(f32) * inv_keep + attn)
        gains = reads.wait(GAINS)
        buf = writes.buffers
        buf[NORMAL1][...] = normal.astype(bf16)
        buf[INV1][...] = jnp.broadcast_to(inv, buf[INV1].shape)
        h1[...] = normal * gains[0:1, :] + biases[3:4, :]
        h1_low = h1[...].astype(bf16)
        buf[H1_LOW][...] = h1_low
        for which in (NORMAL1, INV1, H1_LOW):
            writes.start(which)
        up_bias = reads.wait(UP_BIAS)
        reads.wait(W_UP, 0)
        reads.wait(W_DOWN, 0)
        ff = biases[4:5, :]
        for c, at in enumerate(cuts):
            if c == 1:
                for k in range(1, parts):
                    reads.wait(W_UP, k)
                    reads.wait(W_DOWN, k)
            up = dot(h1_low, reads.buffers[W_UP][:, at]) + up_bias[:, at]
            hidden, slope = gelu_parts(up)
            hidden = hidden.astype(bf16)
            buf[HIDDEN][:, at] = hidden
            buf[SLOPE][:, at] = slope.astype(bf16)
            writes.start(HIDDEN, c, (slice(None), at))
            writes.start(SLOPE, c, (slice(None), at))
            ff = ff + dot(hidden, reads.buffers[W_DOWN][at, :])
        keep = jnp.concatenate([reads.wait(KEEP)[...], reads.wait(KEEP + 1)[0]], axis=0)
        normal, inv = norm_parts(h1[...] + ff * (keep.astype(f32) * inv_keep))
        mixed = (normal * gains[1:2, :] + biases[5:6, :]).astype(bf16)
        buf[MIXED][...] = mixed[:rows]
        buf[MIXED + 1][...] = mixed[rows:]
        writes.start(MIXED)
        writes.start(MIXED + 1)
        buf[NORMAL2][...] = normal.astype(bf16)
        buf[INV2][...] = jnp.broadcast_to(inv, buf[INV2].shape)
        writes.start(NORMAL2)
        writes.start(INV2)

    return streamed(
        body,
        [half],
        [own, pair, *kept, *keep, w_out, w_up, w_down, gains, biases, up_bias],
        [
            struct((2 * rows, hid), bf16),
            struct((2 * rows, hid), bf16),
            struct(full, bf16),
            struct(full, bf16),
            struct((2 * rows, 128), f32),
            struct(full, bf16),
            struct((2 * rows, 128), f32),
            struct(tile, bf16),
            struct(tile, bf16),
        ],
        [pltpu.VMEM(full, f32)],
        (10 + 2 * parts, 7 + 2 * parts),
        "layer_forward",
        16,
        limit=42,
        near=(1,),
    )


def loss_kernel(shift_ref, cls_ref, pool_ref, positive_ref, values_ref, order_ref, g_pre_ref, g_cls_ref):
    rows = cls_ref.shape[0]
    n = rows // 2
    row = lax.broadcasted_iota(jnp.int32, (rows, rows), 0)
    column = lax.broadcasted_iota(jnp.int32, (rows, rows), 1)
    view, sentence = (column % 2) ^ shift_ref[0], (column // 2) ^ shift_ref[1]
    cls = dot((row == view * n + sentence).astype(bf16), cls_ref[...]).astype(bf16)
    order_ref[...] = cls
    pooled = jnp.tanh(dot(cls, pool_ref[...]))
    inv = lax.rsqrt(jnp.sum(pooled * pooled, axis=-1, keepdims=True) + 1e-06)
    unit = pooled * inv
    anchors, candidates = unit[:n], unit[n:]

    def exact(a, b, dims):
        return lax.dot_general(a, b, (dims, ((), ())), precision=highest, preferred_element_type=f32)

    logits = exact(anchors, candidates, ((1,), (1,))) / 0.05
    mine = lax.broadcasted_iota(jnp.int32, (n, n), 0)
    other = lax.broadcasted_iota(jnp.int32, (n, n), 1)
    picked = (other == positive_ref[:, 0:1]).astype(f32)
    top = jnp.max(logits, axis=1, keepdims=True)
    expo = jnp.exp(logits - top)
    total = jnp.sum(expo, axis=1, keepdims=True)
    target = jnp.sum(logits * picked, axis=1, keepdims=True)
    loss = jnp.mean(jnp.log(total) + top - target, axis=0, keepdims=True)
    matched = exact(picked, candidates, ((1,), (0,)))
    offset = anchors - matched
    alignment = jnp.mean(jnp.sum(offset * offset, axis=-1, keepdims=True), axis=0, keepdims=True)
    inner = exact(anchors, anchors, ((1,), (1,)))
    norms = jnp.sum(anchors * anchors, axis=-1, keepdims=True)
    norms_row = jnp.sum(jnp.where(mine == other, norms, 0.0), axis=0, keepdims=True)
    dist = norms + norms_row - 2.0 * inner
    near = jnp.where(mine != other, jnp.exp(-2.0 * dist), 0.0)
    near = jnp.sum(jnp.sum(near, axis=1, keepdims=True), axis=0, keepdims=True)
    uniformity = jnp.log(near / (n * (n - 1)))
    line = lax.broadcasted_iota(jnp.int32, values_ref.shape, 0)
    values_ref[...] = jnp.where(line == 0, loss, jnp.where(line == 1, alignment, uniformity))
    g_logits = (expo / total - picked) * (1.0 / (0.05 * n))
    g_unit = jnp.concatenate(
        [exact(g_logits, candidates, ((1,), (0,))), exact(g_logits, anchors, ((0,), (0,)))], axis=0
    )
    g_pooled = inv * (g_unit - unit * jnp.sum(g_unit * unit, axis=-1, keepdims=True))
    g_pre = (g_pooled * (1.0 - pooled * pooled)).astype(bf16)
    g_pre_ref[...] = g_pre
    line = lax.broadcasted_iota(jnp.int32, g_pre.shape, 0)
    mine = jnp.where(line == shift_ref[0] * n + shift_ref[1], g_pre.astype(f32), 0.0)
    mine = jnp.broadcast_to(jnp.sum(mine, axis=0, keepdims=True), (8, mine.shape[1])).astype(bf16)
    g_cls_ref[...] = dot_t(mine, pool_ref[...])


def loss_parts(shift, cls, pool_w, positive):
    rows, width = cls.shape
    return pl.pallas_call(
        loss_kernel,
        in_specs=[pl.BlockSpec(memory_space=pltpu.SMEM)] + [pl.BlockSpec(memory_space=pltpu.VMEM)] * 3,
        out_shape=[
            struct((8, 128), f32),
            struct((rows, width), bf16),
            struct((rows, width), bf16),
            struct((8, width), f32),
        ],
        compiler_params=params(16),
        cost_estimate=cost(2),
        name="contrast",
    )(shift, cls, pool_w, positive)


def feed_backward(
    half, side, g_parts, g_cls, normal2, inv2, keeps, gains, hidden, w_down, w_up, slope, h1_low, normal1, inv1, w_out
):
    rows, width = h1_low.shape
    hid = hidden.shape[1]
    wide = hid // GROUPS
    chunk = hid // 4
    deep = width // 8
    full = (rows, width)
    down = struct((GROUPS, 2, deep, 2 * wide), bf16)
    up = struct((2, width, chunk), bf16)
    narrow = struct((rows, width // 2), bf16)
    G, G_CLS, NORMAL2, INV2, KEEP, GAINS, HIDDEN, W_DOWN, W_UP, SLOPE, H1, NORMAL1, INV1, W_OUT = (
        0, 1, 2, 3, 4, 6, 7, 8, 9, 10, 11, 12, 13, 14,
    )
    D_SEND, D_KEEP, U_SEND, U_KEEP, UP_SUM, G_ATTN, OWN, PAIR_, SUMS = range(9)
    cuts = [slice(i * wide, (i + 2) * wide) for i in range(0, GROUPS, 2)]

    def body(scalars, reads, writes, turned, turned_h1, g_h2_ref, g_ff_ref):
        half, cls_side = scalars
        steps = []
        for who, ref in ((1 - half, U_SEND), (half, U_KEEP)):
            for b in (0, 1):
                steps.append((ref, b, pl.ds(pl.multiple_of((2 * b + who) * chunk, chunk), chunk)))
        first = (G, G_CLS, NORMAL2, INV2, GAINS, KEEP, KEEP + 1)
        for which in first:
            reads.start(which)
        reads.start(HIDDEN)
        reads.start(H1)
        for which in first:
            reads.wait(which)
        for c, (ref, b, at) in enumerate(steps):
            reads.start(W_DOWN, c, (at,))
            reads.start(SLOPE, c, (slice(None), at))
            reads.start(W_UP, c, (slice(None), at))
        for which in (NORMAL1, INV1, W_OUT):
            reads.start(which)
        got, buf = reads.buffers, writes.buffers
        g = jnp.concatenate([got[G][...], got[KEEP + 1][1]], axis=0).astype(f32)
        place = jnp.where(half == 0, cls_side * (rows // 2), rows)
        here = lax.broadcasted_iota(jnp.int32, g.shape, 0) == place
        g = g + jnp.where(here, got[G_CLS][0:1, :], 0.0)
        normal = got[NORMAL2][...].astype(f32)
        g_h2 = norm_back(g, normal, got[INV2][:, 0:1], got[GAINS][1:2, :])
        keep = jnp.concatenate([got[KEEP][...], got[KEEP + 1][0]], axis=0)
        g_ff = (g_h2 * (keep.astype(f32) * inv_keep)).astype(bf16)
        g_h2_ref[...] = g_h2
        g_ff_ref[...] = g_ff
        second = [jnp.sum(v, axis=0, keepdims=True) for v in (g * normal, g, g_ff.astype(f32))]
        turned[...] = g_ff.T.reshape(turned.shape)
        reads.wait(HIDDEN)
        reads.wait(H1)
        for who, ref in ((1 - half, D_SEND), (half, D_KEEP)):
            lhs = jnp.concatenate([turned[who], turned[who + 2]], axis=0)
            for c, at in enumerate(cuts):
                out = dot(lhs, got[HIDDEN][:, at]).astype(bf16)
                for i in (0, 1):
                    for s in (0, 1):
                        lines = out[2 * s * deep : 2 * (s + 1) * deep, i * wide : (i + 1) * wide]
                        buf[ref][2 * c + i, s] = jnp.concatenate([lines[:deep], lines[deep:]], axis=1)
            writes.start(ref)
        turned_h1[...] = got[H1][...].T
        for c in range(4):
            for which in (W_DOWN, SLOPE, W_UP):
                reads.wait(which, c)
        g = g_h2_ref[...]
        for c, (ref, b, at) in enumerate(steps):
            g_up = (dot_t(g_ff_ref[...], got[W_DOWN][at, :]) * got[SLOPE][:, at].astype(f32)).astype(bf16)
            buf[UP_SUM][:, at] = jnp.sum(g_up.astype(f32), axis=0, keepdims=True)
            buf[ref][b] = dot(turned_h1[...], g_up).astype(bf16)
            writes.start(ref, b, (b,))
            g = g + dot_t(g_up, got[W_UP][:, at])
        writes.start(UP_SUM)
        for which in (NORMAL1, INV1, W_OUT):
            reads.wait(which)
        normal = got[NORMAL1][...].astype(f32)
        g_attn = norm_back(g, normal, got[INV1][:, 0:1], got[GAINS][0:1, :]).astype(bf16)
        for who, ref in ((1 - half, PAIR_), (half, OWN)):
            w = jnp.concatenate([got[W_OUT][who], got[W_OUT][who + 2]], axis=0)
            buf[ref][...] = dot_t(g_attn, w).astype(bf16)
            writes.start(ref)
        buf[G_ATTN][...] = g_attn
        writes.start(G_ATTN)
        first = [jnp.sum(v, axis=0, keepdims=True) for v in (g * normal, g, g_attn.astype(f32))]
        zero = jnp.zeros((2, width), f32)
        buf[SUMS][...] = jnp.concatenate(
            [first[0], second[0], zero, first[1], second[2], second[1], first[2]], axis=0
        )
        writes.start(SUMS)

    return streamed(
        body,
        [half, side],
        [
            g_parts[0], g_cls, normal2, inv2, *keeps, gains, hidden, w_down, w_up, slope, h1_low, normal1, inv1, w_out,
        ],
        [
            down,
            down,
            up,
            up,
            struct((1, hid), f32),
            struct(full, bf16),
            narrow,
            narrow,
            struct((8, width), f32),
        ],
        [
            pltpu.VMEM((4, width // 4, rows), bf16),
            pltpu.VMEM((width, rows), bf16),
            pltpu.VMEM(full, f32),
            pltpu.VMEM(full, bf16),
        ],
        (25, 11),
        "feed_backward",
        20,
        limit=50,
        near=(1,),
    )


def out_backward(half, own, pair, g_attn):
    rows, width = g_attn.shape
    size = width // 4
    padded = -(-size // 128) * 128
    part = struct((2, width, padded), bf16)

    def body(scalars, reads, writes, ctx, cut):
        (half,) = scalars
        for which in range(3):
            reads.start(which)
        own_t, pair_t = reads.wait(0)[...].T, reads.wait(1)[...].T
        for b in (0, 1):
            lines = slice(b * size, (b + 1) * size)
            ctx[2 * b + half] = own_t[lines]
            ctx[2 * b + 1 - half] = pair_t[lines]
        g = reads.wait(2)
        for b in range(4):
            cut[b] = g[:, b * size : (b + 1) * size]
        lhs = ctx[...].reshape(4 * size, -1)
        for who, ref in ((1 - half, 0), (half, 1)):
            for b in (0, 1):
                writes.buffers[ref][b, :, :size] = dot(lhs, cut[2 * b + who]).astype(bf16)
                writes.buffers[ref][b, :, size:] = jnp.zeros((width, padded - size), bf16)
            writes.start(ref)

    return streamed(
        body,
        [half],
        [own, pair, g_attn],
        [part, part],
        [pltpu.VMEM((4, size, rows), bf16), pltpu.VMEM((4, rows, size), bf16)],
        (3, 2),
        "out_backward",
        4,
        limit=16,
        near=(2,),
        stay=(0, 1),
    )


def pick(values, index, axis):
    return lax.dynamic_index_in_dim(values, index, axis, keepdims=False)


def add_low(*parts):
    total = parts[0].astype(f32)
    for part in parts[1:]:
        total = total + part.astype(f32)
    return total.astype(bf16)


class Halving:
    def __init__(self, values, shape, names, order, place):
        self.values = [v.reshape(shape) for v in values]
        self.names, self.order, self.place = list(names), list(order), place

    def total(self):
        return self.values[0] if len(self.values) == 1 else add_low(*self.values)

    def cut(self):
        step = self.order.pop(0)
        axis = self.names.index(step)
        self.names.pop(axis)
        side, dp, bits = self.place
        if step == "side":
            bit, self.route = side, ("seq", CROSS)
        else:
            bit = (dp >> step) & 1
            self.route = ("dp", [(d, d ^ (1 << step)) for d in range(1 << bits)])
        halves = []
        for which in (1 - bit, bit):
            parts = [pick(v, which, axis) for v in self.values]
            halves.append(parts[0] if len(parts) == 1 else add_low(*parts))
        return halves

    def join(self, arrived, kept):
        self.values = [kept, arrived]


class Summing:
    def __init__(self, values, bits):
        self.values = values
        self.order = [("seq", PAIR), ("seq", CROSS)]
        self.order += [("dp", [(d, d ^ (1 << k)) for d in range(1 << bits)]) for k in range(bits)]

    def cut(self):
        self.route = self.order.pop(0)
        return self.values, None

    def join(self, arrived, kept):
        self.values = self.values + arrived


class Rows:
    def __init__(self, own, send, length):
        self.values, self.send, self.length, self.order = own, send, length, [PAIR, CROSS]

    def cut(self):
        self.route = ("seq", self.order.pop(0))
        if self.order:
            return self.send, self.values
        return self.values[self.length :].astype(bf16), self.values[: self.length]

    def join(self, arrived, kept):
        self.values = kept.astype(f32) + arrived.astype(f32) if self.order else (kept, arrived)


def advance(streams, *others):
    streams = [stream for stream in streams if stream.order]
    cuts = [stream.cut() for stream in streams]
    cuts, others = lax.optimization_barrier((cuts, others))
    for stream, (send, kept) in zip(streams, cuts):
        stream.join(lax.ppermute(send, *stream.route), kept)
    return others


class Tiled:
    def __init__(self, values, names, lines, order):
        self.values, self.names, self.lines, self.order = values, list(names), lines, list(order)

    def total(self):
        parts = [lax.slice_in_dim(v, at, at + self.lines, axis=0) for v, at, _ in self.values]
        return parts[0] if len(parts) == 1 else add_low(*parts)


class Shared:
    def __init__(self, values, lines, order):
        self.values, self.lines, self.order = values, lines, list(order)

    total = Tiled.total


def combine(bits_of, streams):
    streams = [stream for stream in streams if stream.order]
    arrays, cuts, links, close = [], [], {}, set()
    for stream in streams:
        step = stream.order.pop(0)
        if isinstance(stream, Shared):
            pre, half = 0, stream.lines
        elif step == "z":
            pre, half = -1, stream.lines
            for offset in (1, 2, 3):
                at = links.setdefault(f"z{offset}", 0)
                links[f"z{offset}"] += half
        else:
            axis = stream.names.index(step)
            stream.names.pop(axis)
            pre, half = 1 << axis, stream.lines << len(stream.names)
        if step != "z":
            at = links.setdefault(step, 0)
            links[step] += half
        loads = []
        for array, first, stride in stream.values:
            known = [i for i, a in enumerate(arrays) if a is array]
            loads.append((known[0] if known else len(arrays), first, stride))
            if not known:
                arrays.append(array)
            if array.shape[0] <= NEAR:
                close.add(loads[-1][0])
        cuts.append((step, at, pre, stream.lines, half, loads))
    steps = list(links)
    width = arrays[0].shape[1]

    def piece(load, pre, lines, half):
        which, first, stride = load
        if pre <= 0:
            return which, first, lines if pre == 0 else 4 * lines
        return (which, first, 2 * half) if stride == lines else (which, 0, 2 * half // lines * stride)

    fetched = list({piece(load, *c[2:5]) for c in cuts for load in c[5]})
    fetched.sort()

    def body(scalars, reads, writes):
        (place,) = scalars
        for key in fetched:
            reads.start(key[0], key, (pl.ds(key[1], key[2]),))
        for i, (step, at, pre, lines, half, loads) in enumerate(cuts):
            for load in loads:
                reads.wait(load[0], piece(load, pre, lines, half))
            if pre == -1:
                own = 2 * place[3] + place[2]
                for offset in range(4):
                    rows = []
                    for w, first, _ in loads:
                        start = pl.multiple_of(first + (own ^ offset) * lines, 16)
                        rows.append(reads.buffers[w][pl.ds(start, lines), :])
                    if offset:
                        out = steps.index(f"z{offset}")
                        writes.buffers[out][at : at + lines, :] = add_low(*rows)
                        writes.start(out, i, (pl.ds(at, lines),))
                    else:
                        writes.buffers[len(steps) + i][...] = add_low(*rows)
                        writes.start(len(steps) + i)
                continue
            bit = place[0 if step == "side" else step + 1]
            if pre == 0:
                total = add_low(*[reads.buffers[w][first : first + lines, :] for w, first, _ in loads])
                writes.buffers[steps.index(step)][at : at + lines, :] = total
                writes.buffers[len(steps) + i][...] = total
            post = half // lines // max(pre, 1)
            for p in range(pre):
                for out, base, which in ((steps.index(step), at, 1 - bit), (len(steps) + i, 0, bit)):
                    block = (2 * p + which) * post

                    def one(t, block=block, out=out, base=base + p * post * lines, loads=loads, lines=lines):
                        rows = []
                        for w, first, stride in loads:
                            start = pl.multiple_of(first + (block + t) * stride, 16)
                            rows.append(reads.buffers[w][pl.ds(start, lines), :])
                        total = rows[0] if len(rows) == 1 else add_low(*rows)
                        writes.buffers[out][pl.ds(pl.multiple_of(base + t * lines, 16), lines), :] = total

                    if post == 1:
                        one(0)
                    else:
                        pl.loop(0, post)(one)
            writes.start(steps.index(step), i, (pl.ds(at, half),))
            writes.start(len(steps) + i)

    small = sum(links.values()) <= 1024
    stay = set(range(len(steps) + len(cuts))) if small else ()
    outs = streamed(
        body,
        [bits_of],
        arrays,
        [struct((links[step], width), bf16) for step in steps] + [struct((c[4], width), bf16) for c in cuts],
        [],
        (len(fetched), sum(4 if c[2] == -1 else 2 for c in cuts)),
        "combine",
        4,
        limit=24,
        near=close,
        stay=stay,
    )
    sends = dict(zip(steps, outs))
    for stream, (step, at, _, _, _, _), kept in zip(streams, cuts, outs[len(steps) :]):
        came = ["z1", "z2", "z3"] if step == "z" else [step]
        stream.values = [(kept, 0, stream.lines)] + [(link, at, stream.lines) for link in came]
    return sends


def exchange(streams, sends, bits):
    arrived = {}
    for step, send in sends.items():
        if step == "side":
            arrived[step] = lax.ppermute(send, "seq", CROSS)
        else:
            apart = 2 * int(step[1]) if isinstance(step, str) else 1 << step
            arrived[step] = lax.ppermute(send, "dp", [(d, d ^ apart) for d in range(1 << bits)])
    for stream in streams:
        stream.values = [(arrived.get(v, v) if isinstance(v, (str, int)) else v, *at) for v, *at in stream.values]


def hold(small, streams):
    arrays = arrays_of(streams)
    replace(streams, arrays, advance(small, *arrays))


def arrays_of(streams):
    return list({id(v): v for stream in streams for v, _, _ in stream.values}.values())


def replace(streams, arrays, held):
    where = {id(v): h for v, h in zip(arrays, held)}
    for stream in streams:
        stream.values = [(where[id(v)], *at) for v, *at in stream.values]


def tie(streams, *others):
    arrays = arrays_of(streams)
    replace(streams, arrays, lax.optimization_barrier((*arrays, *others)))


def gather_step(values, at, bits):
    count = 4 << bits

    def partner(device, offset):
        for k in (0, 1):
            if offset >> k & 1 and at + k <= bits:
                device ^= 2 if at + k == 0 else 4 << (at + k - 1)
        return device

    offsets = range(1, 4 if at + 1 <= bits else 2)
    parts = [
        lax.ppermute(values, ("dp", "seq"), [(d, partner(d, offset)) for d in range(count)])
        for offset in offsets
    ]
    return jnp.concatenate([values] + parts, axis=0)


def own_heads(values, half, axis):
    size = values.shape[axis] // 4
    shape = values.shape[:axis] + (2, 2, size) + values.shape[axis + 1 :]
    out = pick(values.reshape(shape), half, axis + 1)
    return out.reshape(values.shape[:axis] + (2 * size,) + values.shape[axis + 1 :])


def after(value, *others):
    return lax.optimization_barrier((value,) + others)[0]


def body(
    embeds,
    lengths,
    drop_in,
    drop_ff,
    positive,
    w_qkv,
    w_out,
    w_up,
    w_down,
    pool_w,
    gains,
    biases,
    up_bias,
    out_grad,
):
    _, _, length, width = drop_in.shape
    n_dp = lax.axis_size("dp")
    bits = n_dp.bit_length() - 1
    seq = lax.axis_index("seq")
    dp = lax.axis_index("dp")
    side, half = seq // 2, seq % 2
    half1 = half.astype(jnp.int32).reshape(1)
    side1 = side.astype(jnp.int32).reshape(1)
    first_side = side == 0
    place_keys = jnp.stack([seq.astype(jnp.int32), lengths[0]])

    token = embeds[0]
    masks_in = (pick(drop_in, side, 0)[0], pick(drop_in, 1 - side, 0)[0])
    kept_send = token * masks_in[1].astype(bf16)
    kept_cross = lax.ppermute(kept_send, "seq", CROSS)
    kept_local = token * masks_in[0].astype(bf16)
    kept_local_pair = lax.ppermute(kept_local, "seq", PAIR)

    w_own, b_own, qkv_local = project_local(half1, kept_local, kept_local_pair, w_qkv, biases)
    rest = jnp.stack([pick(drop_ff, 1 - side, 0)[0].astype(bf16), pick(out_grad, 1 - side, 0)[0]])
    kept_cross, w_own, rest, place_keys = lax.optimization_barrier((kept_cross, w_own, rest, place_keys))
    kept_cross_pair = lax.ppermute(kept_cross, "seq", PAIR)
    qkv_cross = project_cross(kept_cross, kept_cross_pair, w_own, b_own)
    kept = (kept_local, kept_local_pair, kept_cross, kept_cross_pair)
    rest = lax.ppermute(after(rest, kept_cross), "seq", CROSS)
    keeps = (pick(drop_ff, side, 0)[0].astype(bf16), rest)
    g_parts = (pick(out_grad, side, 0)[0], rest)
    w_out4 = w_out.reshape(4, width // 4, width)
    up_bias2 = up_bias[None]

    own, send, lse = attend_forward(place_keys, qkv_local, qkv_cross)
    pair = lax.ppermute(send, "seq", PAIR)
    hidden, slope, h1_low, normal1, inv1, normal2, inv2, mixed_local, mixed_cross = layer_forward(
        half1, own, pair, (kept_local, kept_cross), keeps, w_out4, w_up, w_down, gains, biases, up_bias2
    )

    first = jnp.where(first_side, mixed_local[:1], mixed_cross[:1])
    rel = first
    for at in range(0, bits + 1, 2):
        rel = gather_step(rel, at, bits)
    shift = jnp.stack([side, dp]).astype(jnp.int32)
    positive_col = jnp.broadcast_to(positive[:, None], (n_dp, 128))
    _, _, _, g_cls = loss_parts(shift, rel, pool_w, positive_col)
    mixed_back = lax.ppermute(after(mixed_cross, g_cls), "seq", CROSS)

    down_send, down_keep, up_send, up_keep, up_sum, g_attn, g_own, g_send, sums = feed_backward(
        half1,
        side1,
        g_parts,
        g_cls,
        normal2,
        inv2,
        keeps,
        gains,
        hidden,
        w_down,
        w_up,
        slope,
        h1_low,
        normal1,
        inv1,
        w_out4,
    )
    g_attn, g_send, down_send, up_send, mixed_back = lax.optimization_barrier(
        (g_attn, g_send, down_send, up_send, mixed_back)
    )
    g_pair = lax.ppermute(g_send, "seq", PAIR)

    dims = (2,) * bits
    place = (side, dp, bits)
    dp_names = list(range(bits - 1, -1, -1))
    names = ["side"] + dp_names
    low = list(range(1, bits))
    sub = n_dp // GROUPS
    deep = width // n_dp
    cut = width // 4

    tiled = deep % 16 == 0
    down_pair = lax.ppermute(down_send, "seq", PAIR)
    up_pair = lax.ppermute(up_send, "seq", PAIR)
    side_first, dp_first = ["side", 0] + low, [0, "side"] + low
    low_first = low[:1] + ["side", 0] + low[1:]
    if tiled:

        def flat(values):
            return values.reshape(-1, width)

        bits_of = jnp.stack([side] + [(dp >> k) & 1 for k in range(bits)]).astype(jnp.int32)
        most = deep * 2 // 3

        def split(keep, pair, axes, order, rest):
            values = [(flat(keep), 0, deep), (flat(pair), 0, deep)]
            later = [(v, most, stride) for v, _, stride in values]
            return [Tiled(values, axes, most, order), Tiled(later, axes, deep - most, rest)]

        ups = split(up_keep, up_pair, names, side_first, low + ["side", 0])
        downs = split(down_keep, down_pair, dp_names + ["side"], dp_first, low + [0, "side"])
        early = [ups[0], downs[0], ups[1], downs[1]]
        out_send, out_keep = out_backward(half1, own, pair, g_attn)
        outs = (out_keep, lax.ppermute(out_send, "seq", PAIR))
        sends = combine(bits_of, early)
        rel_pair = lax.ppermute(rel, "seq", [(0, 1), (2, 3)])
        g_own, g_pair, rel_pair, *held = lax.optimization_barrier((g_own, g_pair, rel_pair, *sends.values()))
        exchange(early, dict(zip(sends, held)), bits)
        *grads, swapped = attend_backward(place_keys, qkv_local, qkv_cross, own, send, g_own, g_pair, lse)
        swapped = lax.ppermute(swapped, "seq", PAIR)
        tie(early, *grads)
        sends = combine(bits_of, early)
        grads = lax.optimization_barrier((*grads, *sends.values()))[:3]
        exchange(early, sends, bits)
        splits = ((0, deep // 2), (1, deep // 2))
        orders = (["side", 0, "z"], [0, "side", "z"])
        g_x, g_x_send, sums, *parts = project_backward(
            half1, bits_of, grads, swapped, kept, outs, w_own, g_attn, sums, up_sum, splits, deep
        )
        qkv = []
        for (_, take), order, send_part, keep_part in zip(splits, orders, parts[::2], parts[1::2]):
            left = [name for name in names if name != order[0]]
            stream = Tiled([(keep_part, 0, take), (order[0], 0, take)], left, take, order[1:])
            exchange([stream], {order[0]: send_part}, bits)
            qkv.append(stream)
        small = [Rows(g_x, g_x_send, length)]
        advance(small)
        sums = sums.astype(bf16)
        shared = Shared(
            [(sums, 0, 16), (lax.ppermute(sums, "seq", PAIR), 0, 16)], 16, low[:1] + ["side", 0]
        )
        tie(early, *parts)
        sends = combine(bits_of, early[:2] + [shared])
        exchange(early[:2] + [shared], sends, bits)
        streams = qkv + early + [shared]
        sends = combine(bits_of, streams)
        exchange(streams, sends, bits)
        rel = after(jnp.where(half == 0, rel, rel_pair), *sends.values())
        found = loss_parts(shift, rel, pool_w, positive_col)
        tie(streams, found[0])
    else:
        sub = n_dp // GROUPS

        def turned(values):
            values = values.reshape(GROUPS, 2, width // 8, 2, sub, -1)
            return values.transpose(0, 4, 1, 3, 2, 5)

        down = Halving(
            [turned(down_keep), turned(down_pair)], dims + (2, cut, -1), dp_names + ["side"], dp_first, place
        )
        up = Halving([up_keep, up_pair], (2,) + dims + (deep, -1), names, side_first, place)
        out_send, out_keep = out_backward(half1, own, pair, g_attn)
        outs = (out_keep, lax.ppermute(out_send, "seq", PAIR))
        g_own, g_pair = advance([up, down], g_own, g_pair)
        *grads, swapped = attend_backward(place_keys, qkv_local, qkv_cross, own, send, g_own, g_pair, lse)
        swapped = lax.ppermute(swapped, "seq", PAIR)
        g_x, g_x_send, sums, part = project_backward(
            half1, place_keys, grads, swapped, kept, outs, w_own, g_attn, sums, up_sum, (), 0
        )
        qkv = [Halving([part], (2,) + dims + (deep, width), names, side_first, place)]
        streams = qkv + [up, down]
        small = [Summing(sums, bits), Rows(g_x, g_x_send, length)]
    while any(stream.order for stream in streams + small):
        if tiled:
            hold(small, streams)
            if any(stream.order for stream in streams):
                sends = combine(bits_of, streams)
                exchange(streams, sends, bits)
        else:
            advance(streams + small)
    if not tiled:
        rel = jnp.where(half == 0, rel, lax.ppermute(rel, "seq", [(0, 1), (2, 3)]))
        found = loss_parts(shift, rel, pool_w, positive_col)
    if tiled:
        sums = shared.total()
        shared.values = [(sums, 0, 16), (lax.ppermute(sums, "dp", [(d, d ^ 4) for d in range(n_dp)]), 0, 16)]
        tie(qkv, shared.total())
    values, cls_all, g_pre, _ = found
    pool_rows, pool_cols = width // n_dp, width // 4
    grad_pool = t_dot(
        lax.dynamic_slice_in_dim(cls_all, dp * pool_rows, pool_rows, 1),
        lax.dynamic_slice_in_dim(g_pre, seq * pool_cols, pool_cols, 1),
    )
    mixed_out = jnp.stack(
        [jnp.where(first_side, mixed_local, mixed_back), jnp.where(first_side, mixed_back, mixed_local)]
    )[:, None]
    total = shared.total().astype(f32) if tiled else small[0].values
    g_x, g_x_cross = small[-1].values
    if tiled:
        grad_up = jnp.concatenate([stream.total() for stream in ups], axis=0).astype(f32)
        grad_down = jnp.concatenate([stream.total() for stream in downs], axis=0)
    else:
        grad_up = up.total().astype(f32)
        grad_down = down.total()
    if tiled:
        grad_down = grad_down.reshape(deep, 2, -1).swapaxes(0, 1).reshape(cut, -1)
    grad_down = grad_down.astype(f32).T
    sum_qkv = jnp.concatenate([stream.total() for stream in qkv], axis=0)
    grad_out = sum_qkv[:, 3 * cut :].astype(f32)
    grad_qkv = sum_qkv[:, : 3 * cut].astype(f32)
    embeds_grad = (g_x * masks_in[0].astype(f32) + g_x_cross.astype(f32) * masks_in[1].astype(f32)) * inv_keep
    return (
        mixed_out,
        embeds_grad[None],
        grad_qkv,
        grad_out,
        grad_up,
        grad_down,
        grad_pool,
        total[0:2],
        total[2:7],
        total[7],
        total[8 : 8 + up_bias.shape[0] // width].reshape(-1),
        values[0, 0],
        values[1, 0],
        values[2, 0],
    )


def solution(mesh):
    tokens = P(None, "dp", "seq", None)
    placed = (P("dp", "seq", None), P("dp"), tokens, tokens) + (P(),) * 9 + (tokens,)
    weight = P("dp", "seq")
    return jax.shard_map(
        body,
        mesh=mesh,
        in_specs=placed,
        out_specs=(tokens, P("dp", "seq", None)) + (weight,) * 5 + (P(),) * 7,
        check_vma=False,
    )
```
